32 devices in a mesh: grp: 2 (over y), pb: 16 (over z, x, core).
Axes of the slice: x: 2, y: 2, z: 4, core: 2. Of those that a mesh axis runs over, the one named last changes fastest.
Arguments:
- queries: bfloat16 [4096, 2048], P('pb', 'grp'), parts along dimension 1, may hold values from -150 to 150
- keys: bfloat16 [4096, 256], P('pb', 'grp'), parts along dimension 1, may hold values from -6 to 6
- values: bfloat16 [4096, 256], P('pb', 'grp'), parts along dimension 1, may hold values from -6 to 6
- basis: bfloat16 [256, 128], P('grp'), parts along dimension 0, may hold values from -0.5 to 0.5
- picks: int32 [64, 16], P('grp'), parts along dimension 0, may hold values from -1 to 7, as said below
Outputs:
- attended: bfloat16 [4096, 2048], P('pb', 'grp'), parts along dimension 1
The draws below stay inside these ranges and needn't reach their ends.
There are 2 independent parts, one for each index of `grp`. The reference program is written for one: setup_inputs(seed, part) draws one part's arguments, and reference() takes and returns one part's arrays. A program takes and returns all parts, laid end to end along the dimension named above; each array names one. Nothing has to cross between parts.
Inputs may be any that keep to these rules, and one draw needn't show every extreme that they name: picks[b, s] is -1 when neither block of device s (blocks s and 31 - s) ends before block b - 1 begins; else it names a sub-block of one of those blocks that lies wholly before block b - 1.
All inputs are finite; a program needn't handle non-finite values.
Results may differ from the reference program's by a relative error of at most 0.011.
Values may be sent and summed in bfloat16 or wider, within the bound.
No kernel may reach another device: no remote copies, remote signals or barrier semaphores. Data moves between devices by JAX's collectives and lax.ppermute only.
A program may use at most 64 MiB of HBM per device.

```python
import jax
import jax.numpy as jnp
from jax import lax

HQ = 8
HD = 128
KB = 32
H = 128
NBLK = 32
SEQ = 4096


def draw_picks(key, part):
    sources = NBLK // 2
    per_block = H // KB
    block = jnp.arange(NBLK, dtype=jnp.int32)[:, None]
    source = jnp.arange(sources, dtype=jnp.int32)[None, :]
    early_ok = source < block - 1
    late_ok = NBLK - 1 - source < block - 1
    first, second = jax.random.split(jax.random.fold_in(key, 7))
    coin = jax.random.randint(first, (NBLK, sources), 0, 2)
    within = jax.random.randint(second, (NBLK, sources), 0, per_block)
    use_late = late_ok & (jnp.logical_not(early_ok) | (coin == 1))
    use_early = early_ok & jnp.logical_not(use_late)
    return jnp.where(use_late, per_block + within, jnp.where(use_early, within, -1)).astype(jnp.int32)


def draw_queries(key, part):
    shape = (NBLK * H, HQ * HD)
    first = jax.random.fold_in(jax.random.fold_in(key, 11), 0)
    return jnp.clip(jax.random.normal(first, shape, jnp.float32) * 2.0, -12.0, 12.0).astype(jnp.bfloat16)


def shard_levels(stream_key, shape, shards, least, high):
    gain, own = 1.0, jax.random.fold_in(stream_key, 6)
    for position, parts in shards:
        draws = jnp.exp(jax.random.uniform(jax.random.fold_in(own, position), (parts,), jnp.float32, least / len(shards), high / len(shards)))
        gain = gain * jnp.repeat(draws, shape[position] // parts).reshape([-1 if axis == position else 1 for axis in range(len(shape))])
    return gain


def gaussian(key, shape, scale, limit, cuts=(), kind=jnp.bfloat16):
    factor_of = shard_levels(key, shape, cuts, -0.22, 0.18) if cuts else 1.0
    drawn = jax.random.normal(key, shape, jnp.float32) * scale * factor_of
    return jnp.minimum(jnp.maximum(drawn, -limit), limit).astype(kind)


def setup_inputs(seed: int = 0, part: int = 0) -> dict:
    streams_of = jax.random.split(jax.random.key(seed), 6)
    own_keys = jax.random.split(jax.random.fold_in(streams_of[5], part), 6)
    return {
        "queries": draw_queries(jax.random.fold_in(jax.random.fold_in(streams_of[5], part), 71), part),
        "keys": gaussian(own_keys[1], (SEQ, HD), 1.0, 6.0, ((0, 16),)),
        "values": gaussian(own_keys[2], (SEQ, HD), 1.0, 6.0, ((0, 16),)),
        "basis": gaussian(own_keys[3], (HD, HD), HD ** -0.5, 0.5),
        "picks": draw_picks(jax.random.fold_in(jax.random.fold_in(streams_of[5], part), 71), part),
    }


def block_start(block, half):
    count = NBLK // 2
    early = block < count
    device = jnp.where(early, block, NBLK - 1 - block)
    return (device * 2 * half + jnp.where(early, 0, half)).astype(jnp.int32)


def attend(q_rot, chosen, chosen_ok, own):
    nq = q_rot.shape[0]
    dim = q_rot.shape[2]
    keys_all = jnp.concatenate([chosen[:, :dim], own[:, :dim]], axis=0)
    vals_all = jnp.concatenate([chosen[:, dim:], own[:, dim:]], axis=0)
    causal = jnp.arange(nq)[:, None] >= jnp.arange(nq)[None, :]
    usable = jnp.concatenate([jnp.broadcast_to(chosen_ok[None, :], (nq, chosen.shape[0])), causal], axis=1)
    scores = jnp.einsum('qhd,kd->hqk', q_rot.astype(jnp.float32), keys_all.astype(jnp.float32)) * (dim ** -0.5)
    scores = jnp.where(usable[None], scores, jnp.float32(-1e30))
    top = jnp.max(scores, axis=-1, keepdims=True)
    weight = jnp.exp(scores - top)
    total = jnp.sum(weight, axis=-1)
    weight_b = weight.astype(jnp.bfloat16)
    summed = jnp.einsum('hqk,kd->qhd', weight_b.astype(jnp.float32), vals_all.astype(jnp.float32))
    result = summed / jnp.transpose(total)[:, :, None]
    return result.astype(jnp.bfloat16).reshape(nq, -1)


def reference(queries, keys, values, basis, picks):
    seq = NBLK * H
    sources = NBLK // 2
    q_rot = jnp.einsum('shd,de->she', queries.reshape(seq, HQ, HD).astype(jnp.float32), basis.astype(jnp.float32)).astype(jnp.bfloat16)
    kv_rows = jnp.concatenate([keys, values], axis=1)
    offsets = jnp.arange(KB, dtype=jnp.int32)

    def one_block(block):
        start = block_start(block, H)
        prev_start = block_start(jnp.maximum(block - 1, 0), H)
        chosen_ids = picks[block]
        index = jnp.arange(sources, dtype=jnp.int32)[:, None] * (2 * H) + jnp.maximum(chosen_ids, 0)[:, None] * KB + offsets[None, :]
        picked = jnp.take(kv_rows, index.reshape(-1).astype(jnp.int32), axis=0)
        ok_pick = jnp.repeat(chosen_ids >= 0, KB)
        before = lax.dynamic_slice_in_dim(kv_rows, prev_start, H, 0)
        ok_before = jnp.broadcast_to(block >= 1, (H,))
        chosen = jnp.concatenate([picked, before], axis=0)
        chosen_ok = jnp.concatenate([ok_pick, ok_before], axis=0)
        own = lax.dynamic_slice_in_dim(kv_rows, start, H, 0)
        q_block = lax.dynamic_slice_in_dim(q_rot, start, H, 0)
        return attend(q_block, chosen, chosen_ok, own)

    blocks = lax.map(one_block, jnp.arange(NBLK, dtype=jnp.int32))
    stored = jnp.stack([blocks[:sources], blocks[sources:][::-1]], axis=1)
    return stored.reshape(seq, HQ * HD)
```

```python
import functools
import math

import jax
import jax.numpy as jnp
from jax import lax
from jax.experimental import pallas as pl
from jax.experimental.pallas import tpu as pltpu
from jax.sharding import PartitionSpec as P

KB = 32
NEG = -1e30
VMEM_BYTES = 40 * 1024 * 1024


def passed_along(value, axis, steps):
    count = lax.axis_size(axis)
    leading, last = (max(0, -steps), min(count, count - steps))
    return lax.ppermute(value, axis, [(source, source + steps) for source in range(leading, last)])


def scores_of(k, q):
    return lax.dot_general(k, q, (((1,), (1,)), ((), ())), preferred_element_type=jnp.float32)


def pack_kernel(count, picks_ref, k_ref, v_ref, out_ref, first_ref, second_ref):
    me = lax.axis_index("pb")
    dim = k_ref.shape[1]
    half = k_ref.shape[0] // 2
    first_ref[:, :dim] = k_ref[:half]
    first_ref[:, dim:] = v_ref[:half]
    second_ref[:, :dim] = k_ref[half:]
    second_ref[:, dim:] = v_ref[half:]

    def one(dest, carry):
        for slot in range(2):
            block = dest if slot == 0 else 2 * count - 1 - dest
            pick = jnp.maximum(picks_ref[block, me], 0)
            rows = pl.ds(pl.multiple_of(pick * KB, KB), KB)
            out_ref[dest, slot, :, :dim] = k_ref[rows, :]
            out_ref[dest, slot, :, dim:] = v_ref[rows, :]
        return carry

    lax.fori_loop(0, count, one, 0, unroll=min(count, 16))


def near_kernel(count, scale, q_ref, basis_ref, k_ref, v_ref, earlier_ref, later_ref, rot_ref, m_ref, l_ref, acc_ref):
    me = lax.axis_index("pb")
    dim = basis_ref.shape[0]
    half = q_ref.shape[0] // 2
    heads = q_ref.shape[1] // dim
    basis = basis_ref[...]
    step = 2 * half
    key_row = lax.broadcasted_iota(jnp.int32, (half, step), 0)
    query = lax.broadcasted_iota(jnp.int32, (half, step), 1) % half
    causal = key_row <= query
    for block in range(2):
        rows = slice(block * half, (block + 1) * half)
        k_own, v_own = k_ref[rows], v_ref[rows]
        if block == 0:
            k_prev, v_prev = earlier_ref[:, :dim], earlier_ref[:, dim:]
            usable = me >= 1
        else:
            last = me == count - 1
            k_prev = jnp.where(last, k_ref[:half], later_ref[:, :dim])
            v_prev = jnp.where(last, v_ref[:half], later_ref[:, dim:])
        k_all = jnp.concatenate([k_prev, k_own], axis=0)
        v_t = jnp.concatenate([v_prev, v_own], axis=0).T
        for pair in range(heads // 2):
            q = [
                jnp.dot(
                    q_ref[rows, (2 * pair + h) * dim : (2 * pair + h + 1) * dim], basis, preferred_element_type=jnp.float32
                ).astype(jnp.bfloat16)
                for h in range(2)
            ]
            q = jnp.concatenate(q, axis=0)
            cols = slice(pair * step, (pair + 1) * step)
            rot_ref[block, cols, :] = q
            s = scores_of(k_all, q) * scale
            s_prev, s_own = s[:half], jnp.where(causal, s[half:], NEG)
            if block == 0:
                s_prev = jnp.where(usable, s_prev, NEG)
            s = jnp.concatenate([s_prev, s_own], axis=0)
            m = jnp.max(s, axis=0, keepdims=True)
            w = jnp.exp2(s - m)
            m_ref[block, :, cols] = m
            l_ref[block, :, cols] = jnp.sum(w, axis=0, keepdims=True)
            acc_ref[block, :, cols] = jnp.dot(v_t, w.astype(jnp.bfloat16), preferred_element_type=jnp.float32)


def far_kernel(count, chunk, scale, kv_ref, rot_ref, m_ref, l_ref, acc_ref, out_ref):
    me = lax.axis_index("pb")
    dim = rot_ref.shape[2]
    half = out_ref.shape[0] // 2
    heads = out_ref.shape[1] // dim
    step = 2 * half
    nk = chunk * KB

    def finish(block, pair, l, acc):
        done = acc / l
        for h in range(2):
            head = 2 * pair + h
            out_ref[block * half : (block + 1) * half, head * dim : (head + 1) * dim] = (
                done[:, h * half : (h + 1) * half].T.astype(out_ref.dtype)
            )

    def run(block):
        def part(c, m_all, l_all, acc_all):
            source = c * chunk + lax.broadcasted_iota(jnp.int32, (nk, step), 0) // KB
            if block == 0:
                usable = source < me - 1
            else:
                usable = (source < 2 * count - 2 - me) | (source > me + 1)
            k = kv_ref[pl.ds(c * chunk, chunk), block, :, :dim].reshape(nk, dim)
            v_t = kv_ref[pl.ds(c * chunk, chunk), block, :, dim:].reshape(nk, dim).T
            ms, ls, accs = [], [], []
            for pair in range(heads // 2):
                cols = slice(pair * step, (pair + 1) * step)
                s = scores_of(k, rot_ref[block, cols, :]) * scale
                s = jnp.where(usable, s, NEG)
                m_old = m_all[pair]
                m = jnp.maximum(m_old, jnp.max(s, axis=0, keepdims=True))
                w = jnp.exp2(s - m)
                old = jnp.exp2(m_old - m)
                ms.append(m)
                ls.append(l_all[pair] * old + jnp.sum(w, axis=0, keepdims=True))
                accs.append(acc_all[pair] * old + jnp.dot(v_t, w.astype(jnp.bfloat16), preferred_element_type=jnp.float32))
            return ms, ls, accs

        pairs = range(heads // 2)
        state = tuple(
            [ref[block, :, pair * step : (pair + 1) * step] for pair in pairs] for ref in (m_ref, l_ref, acc_ref)
        )
        if count == chunk:
            state = part(0, *state)
        else:
            state = lax.fori_loop(0, count // chunk, lambda c, carry: part(c, *carry), state)
        for pair in pairs:
            finish(block, pair, state[1][pair], state[2][pair])

    run(1)

    @pl.when(me >= 2)
    def _():
        run(0)

    @pl.when(me < 2)
    def _():
        for pair in range(heads // 2):
            cols = slice(pair * step, (pair + 1) * step)
            finish(0, pair, l_ref[0, :, cols], acc_ref[0, :, cols])


def per_device(queries, keys, values, basis, picks):
    rows_dev, dim = keys.shape
    half = rows_dev // 2
    count = lax.axis_size("pb")
    wide = queries.shape[1] // dim * half
    scale = dim**-0.5 * math.log2(math.e)
    vmem = pl.BlockSpec(memory_space=pltpu.VMEM)
    smem = pl.BlockSpec(memory_space=pltpu.SMEM)
    params = pltpu.CompilerParams(vmem_limit_bytes=VMEM_BYTES)
    bf16, f32 = jnp.bfloat16, jnp.float32

    outgoing, first, second = pl.pallas_call(
        functools.partial(pack_kernel, count),
        out_shape=[
            jax.ShapeDtypeStruct((count, 2, KB, 2 * dim), bf16),
            jax.ShapeDtypeStruct((half, 2 * dim), bf16),
            jax.ShapeDtypeStruct((half, 2 * dim), bf16),
        ],
        in_specs=[smem, vmem, vmem],
        out_specs=[vmem] * 3,
        compiler_params=params,
        name="pack",
    )(picks, keys, values)
    incoming = lax.all_to_all(outgoing, "pb", split_axis=0, concat_axis=0, tiled=True)
    earlier = passed_along(first, "pb", 1)
    later = passed_along(second, "pb", -1)
    near = pl.pallas_call(
        functools.partial(near_kernel, count, scale),
        out_shape=[
            jax.ShapeDtypeStruct((2, wide, dim), bf16),
            jax.ShapeDtypeStruct((2, 1, wide), f32),
            jax.ShapeDtypeStruct((2, 1, wide), f32),
            jax.ShapeDtypeStruct((2, dim, wide), f32),
        ],
        in_specs=[vmem] * 6,
        out_specs=[vmem] * 4,
        compiler_params=params,
        cost_estimate=pl.CostEstimate(flops=700_000_000, bytes_accessed=2_500_000, transcendentals=600_000),
        name="near",
    )(queries, basis, keys, values, earlier, later)
    return pl.pallas_call(
        functools.partial(far_kernel, count, min(count, 16), scale),
        out_shape=jax.ShapeDtypeStruct(queries.shape, bf16),
        in_specs=[vmem] * 5,
        out_specs=vmem,
        compiler_params=params,
        name="far",
    )(incoming, *near)


def solution(mesh):
    in_specs = (P("pb", "grp"), P("pb", "grp"), P("pb", "grp"), P("grp", None), P("grp", None))
    out_specs = P("pb", "grp")
    return jax.shard_map(
        per_device, mesh=mesh, in_specs=in_specs, out_specs=out_specs, check_vma=False
    )
```

```python
import functools
import math

import jax
import jax.numpy as jnp
from jax import lax
from jax.experimental import pallas as pl
from jax.experimental.pallas import tpu as pltpu
from jax.sharding import PartitionSpec as P

KB = 32
PLANE = 4
NEG = -1e30
VMEM_BYTES = 40 * 1024 * 1024


def place(count):
    me = lax.axis_index("pb")
    return me, me // PLANE, me % PLANE


def sub(index):
    return pl.ds(pl.multiple_of(index * KB, KB), KB)


def scores_of(k, q):
    return lax.dot_general(k, q, (((1,), (1,)), ((), ())), preferred_element_type=jnp.float32)


def pack_kernel(count, picks_ref, k_ref, v_ref, *refs):
    planes = count // PLANE
    kv_ref, cross_ref, own_refs, packet_refs, sems = refs[0], refs[1], refs[2:5], refs[5:-1], refs[-1]
    me, z, r = place(count)
    dim = k_ref.shape[1]
    half = k_ref.shape[0] // 2
    per_half = half // KB
    copies = [
        pltpu.make_async_copy(k_ref, kv_ref.at[:, :dim], sems.at[0]),
        pltpu.make_async_copy(v_ref, kv_ref.at[:, dim:], sems.at[1]),
    ]
    for copy in copies:
        copy.start()
    for copy in copies:
        copy.wait()

    def late_pick(dest):
        return jnp.maximum(picks_ref[me, 2 * count - 1 - dest], 0)

    for j, ref in enumerate(packet_refs, 1):
        up = z + j < planes
        to = jnp.where(up, 0, (z + j - planes) * PLANE)
        for t in range(PLANE):
            index = jnp.where(up, t, late_pick(to + t))
            ref[t * KB : (t + 1) * KB] = kv_ref[sub(index)]
    for m, ref in enumerate(own_refs, 1):
        peer = r ^ m
        late = kv_ref[sub(late_pick(z * PLANE + peer))]
        if m == 2:
            ref[:KB] = late
            ref[KB:] = kv_ref[sub(jnp.maximum(picks_ref[me, z * PLANE + peer], 0))]
        else:
            ref[:KB] = late
            start = jnp.where(r < peer, 0, per_half)
            for t in range(per_half):
                ref[(t + 1) * KB : (t + 2) * KB] = kv_ref[sub(start + t)]
    start = jnp.where(r == PLANE - 1, 0, per_half)
    for t in range(per_half):
        cross_ref[t * KB : (t + 1) * KB] = kv_ref[sub(start + t)]


def select_kernel(count, picks_ref, *refs):
    planes = count // PLANE
    packet_refs, late_refs, early_refs = refs[: planes - 1], refs[planes - 1 : planes + 2], refs[planes + 2 :]
    me, z, r = place(count)
    for j, ref in enumerate(packet_refs, 1):
        up = z >= j
        source = jnp.where(up, z - j, z - j + planes) * PLANE + r
        for m, (late_ref, early_ref) in enumerate(zip(late_refs, early_refs, strict=True), 1):
            peer = r ^ m
            dest = z * PLANE + peer
            late = jnp.where(up, jnp.maximum(picks_ref[source, 2 * count - 1 - dest], 0), peer)
            early = jnp.where(up, jnp.maximum(picks_ref[source, dest], 0), 0)
            late_ref[(j - 1) * KB : j * KB] = ref[sub(late)]
            early_ref[(j - 1) * KB : j * KB] = ref[sub(early)]


def near_kernel(count, scale, q_ref, basis_ref, kv_ref, cross_ref, own1_ref, own3_ref, rot_ref, m_ref, l_ref, acc_ref):
    me, z, r = place(count)
    dim = basis_ref.shape[0]
    half = q_ref.shape[0] // 2
    heads = q_ref.shape[1] // dim
    basis = basis_ref[...]
    step = 2 * half
    key_row = lax.broadcasted_iota(jnp.int32, (half, step), 0)
    query = lax.broadcasted_iota(jnp.int32, (half, step), 1) % half
    causal = key_row <= query
    cross, own1, own3 = cross_ref[...], own1_ref[KB:], own3_ref[KB:]
    for block in range(2):
        rows = slice(block * half, (block + 1) * half)
        if block == 0:
            prev = jnp.where(r == 0, cross, jnp.where(r == 2, own3, own1))
        else:
            prev = jnp.where(r == PLANE - 1, cross, jnp.where(r == 1, own3, own1))
            prev = jnp.where(me == count - 1, kv_ref[:half], prev)
        kv = jnp.concatenate([prev, kv_ref[rows]], axis=0)
        k_all, v_t = kv[:, :dim], kv[:, dim:].T
        for pair in range(heads // 2):
            q = [
                jnp.dot(
                    q_ref[rows, (2 * pair + h) * dim : (2 * pair + h + 1) * dim], basis, preferred_element_type=jnp.float32
                ).astype(jnp.bfloat16)
                for h in range(2)
            ]
            q = jnp.concatenate(q, axis=0)
            cols = slice(pair * step, (pair + 1) * step)
            rot_ref[block, cols, :] = q
            s = scores_of(k_all, q) * scale
            s_prev, s_own = s[:half], jnp.where(causal, s[half:], NEG)
            if block == 0:
                s_prev = jnp.where(me >= 1, s_prev, NEG)
            s = jnp.concatenate([s_prev, s_own], axis=0)
            m = jnp.max(s, axis=0, keepdims=True)
            w = jnp.exp2(s - m)
            m_ref[block, :, cols] = m
            l_ref[block, :, cols] = jnp.sum(w, axis=0, keepdims=True)
            acc_ref[block, :, cols] = jnp.dot(v_t, w.astype(jnp.bfloat16), preferred_element_type=jnp.float32)


def far_kernel(count, chunk, scale, picks_ref, *refs):
    planes = count // PLANE
    packet_refs, refs = refs[: planes - 1], refs[planes - 1 :]
    late_refs, early_refs, own_refs = refs[0:3], refs[3:6], refs[6:9]
    kv_ref, rot_ref, m_ref, l_ref, acc_ref, out_ref, keys_ref = refs[9:]
    me, z, r = place(count)
    dim = rot_ref.shape[2]
    half = out_ref.shape[0] // 2
    heads = out_ref.shape[1] // dim
    step = 2 * half
    nk = chunk * KB
    pairs = range(heads // 2)

    def put(m, j, value):
        keys_ref[(m * planes + j) * KB : (m * planes + j + 1) * KB] = value

    def gather(block):
        mine = me if block == 0 else 2 * count - 1 - me
        put(0, 0, kv_ref[sub(jnp.maximum(picks_ref[me, mine], 0))])
        for j, ref in enumerate(packet_refs, 1):
            up = z >= j
            source = jnp.where(up, z - j, z - j + planes) * PLANE + r
            put(0, j, ref[sub(jnp.where(up, jnp.maximum(picks_ref[source, mine], 0), r))])
        for m in range(1, PLANE):
            own = own_refs[m - 1]
            if block == 1:
                put(m, 0, own[:KB])
            elif m == 2:
                put(m, 0, own[KB:])
            else:
                put(m, 0, own[sub(jnp.maximum(picks_ref[z * PLANE + (r ^ m), mine], 0) % (half // KB) + 1)])
            moved = late_refs if block == 1 else early_refs
            keys_ref[(m * planes + 1) * KB : (m + 1) * planes * KB] = moved[m - 1][...]

    def finish(block, pair, l, acc):
        done = acc / l
        for h in range(2):
            head = 2 * pair + h
            out_ref[block * half : (block + 1) * half, head * dim : (head + 1) * dim] = (
                done[:, h * half : (h + 1) * half].T.astype(out_ref.dtype)
            )

    def usable(block, g):
        m, j = g // planes, g % planes
        home = z - j
        source = jnp.where(home < 0, home + planes, home) * PLANE + (r ^ m)
        if block == 0:
            return source < me - 1
        return (source < 2 * count - 2 - me) | (source > me + 1)

    def run(block):
        gather(block)

        def part(c, m_all, l_all, acc_all):
            rows = slice(None) if count == chunk else pl.ds(pl.multiple_of(c * nk, nk), nk)
            k = keys_ref[rows, :dim]
            v_t = keys_ref[rows, dim:].T
            ok = [usable(block, c * chunk + g) for g in range(chunk)]
            ms, ls, accs = [], [], []
            for pair in pairs:
                cols = slice(pair * step, (pair + 1) * step)
                s = scores_of(k, rot_ref[block, cols, :]) * scale
                s = jnp.concatenate([jnp.where(ok[g], s[g * KB : (g + 1) * KB], NEG) for g in range(chunk)], axis=0)
                m_old = m_all[pair]
                m = jnp.maximum(m_old, jnp.max(s, axis=0, keepdims=True))
                w = jnp.exp2(s - m)
                old = jnp.exp2(m_old - m)
                ms.append(m)
                ls.append(l_all[pair] * old + jnp.sum(w, axis=0, keepdims=True))
                accs.append(acc_all[pair] * old + jnp.dot(v_t, w.astype(jnp.bfloat16), preferred_element_type=jnp.float32))
            return ms, ls, accs

        state = tuple([ref[block, :, pair * step : (pair + 1) * step] for pair in pairs] for ref in (m_ref, l_ref, acc_ref))
        if count == chunk:
            state = part(0, *state)
        else:
            state = lax.fori_loop(0, count // chunk, lambda c, carry: part(c, *carry), state)
        for pair in pairs:
            finish(block, pair, state[1][pair], state[2][pair])

    run(1)

    @pl.when(me >= 2)
    def _():
        run(0)

    @pl.when(me < 2)
    def _():
        for pair in pairs:
            cols = slice(pair * step, (pair + 1) * step)
            finish(0, pair, l_ref[0, :, cols], acc_ref[0, :, cols])


def per_device(queries, keys, values, basis, picks):
    rows_dev, dim = keys.shape
    half = rows_dev // 2
    count = lax.axis_size("pb")
    planes = count // PLANE
    wide = queries.shape[1] // dim * half
    scale = dim**-0.5 * math.log2(math.e)
    vmem = pl.BlockSpec(memory_space=pltpu.VMEM)
    smem = pl.BlockSpec(memory_space=pltpu.SMEM)
    hbm = pl.BlockSpec(memory_space=pltpu.HBM)
    params = pltpu.CompilerParams(vmem_limit_bytes=VMEM_BYTES)
    bf16, f32 = jnp.bfloat16, jnp.float32
    by_source = picks.T

    def rows(n):
        return jax.ShapeDtypeStruct((n, 2 * dim), bf16)

    def permute(value, pairs):
        return lax.ppermute(value, "pb", pairs)

    kv, cross, *rest = pl.pallas_call(
        functools.partial(pack_kernel, count),
        out_shape=[rows(rows_dev), rows(half), rows(half + KB), rows(2 * KB), rows(half + KB)]
        + [rows(PLANE * KB)] * (planes - 1),
        in_specs=[smem, hbm, hbm],
        out_specs=[vmem] * (4 + planes),
        scratch_shapes=[pltpu.SemaphoreType.DMA((2,))],
        compiler_params=params,
        name="pack",
    )(by_source, keys, values)
    own, packets = rest[:3], rest[3:]

    packets = [
        permute(packet, [(s, (s + j * PLANE) % count) for s in range(count)]) for j, packet in enumerate(packets, 1)
    ]
    borders = range(PLANE - 1, count - 1, PLANE)
    cross = permute(cross, [(s, s + 1) for s in borders] + [(s + 1, s) for s in borders])
    own = [permute(value, [(s, s ^ m) for s in range(count)]) for m, value in enumerate(own, 1)]

    near = pl.pallas_call(
        functools.partial(near_kernel, count, scale),
        out_shape=[
            jax.ShapeDtypeStruct((2, wide, dim), bf16),
            jax.ShapeDtypeStruct((2, 1, wide), f32),
            jax.ShapeDtypeStruct((2, 1, wide), f32),
            jax.ShapeDtypeStruct((2, dim, wide), f32),
        ],
        in_specs=[vmem] * 6,
        out_specs=[vmem] * 4,
        compiler_params=params,
        cost_estimate=pl.CostEstimate(flops=700_000_000, bytes_accessed=2_500_000, transcendentals=600_000),
        name="near",
    )(queries, basis, kv, cross, own[0], own[2])

    moved = pl.pallas_call(
        functools.partial(select_kernel, count),
        out_shape=[rows((planes - 1) * KB)] * 6,
        in_specs=[smem] + [vmem] * (planes - 1),
        out_specs=[vmem] * 6,
        compiler_params=params,
        name="select",
    )(by_source, *packets)
    late = [permute(moved[m - 1], [(s, s ^ m) for s in range(count)]) for m in range(1, PLANE)]
    early = [permute(moved[m + 2], [(s, s ^ m) for s in range(PLANE, count)]) for m in range(1, PLANE)]

    return pl.pallas_call(
        functools.partial(far_kernel, count, min(count, 16), scale),
        out_shape=jax.ShapeDtypeStruct(queries.shape, bf16),
        in_specs=[smem] + [vmem] * (planes + 13),
        out_specs=vmem,
        scratch_shapes=[pltpu.VMEM((count * KB, 2 * dim), bf16)],
        compiler_params=params,
        name="far",
    )(by_source, *packets, *late, *early, *own, kv, *near)


def solution(mesh):
    in_specs = (P("pb", "grp"), P("pb", "grp"), P("pb", "grp"), P("grp", None), P("grp", None))
    out_specs = P("pb", "grp")
    return jax.shard_map(
        per_device, mesh=mesh, in_specs=in_specs, out_specs=out_specs, check_vma=False
    )
```

```python
import functools
import math

import jax
import jax.numpy as jnp
from jax import lax
from jax.experimental import pallas as pl
from jax.experimental.pallas import tpu as pltpu
from jax.sharding import PartitionSpec as P

KB = 32
PLANE = 4
NEG = -1e30
VMEM_BYTES = 40 * 1024 * 1024
CHUNK = 16


def place(count):
    me = lax.axis_index("pb")
    return me, me // PLANE, me % PLANE


def sub(index):
    return pl.ds(pl.multiple_of(index * KB, KB), KB)


def at(n):
    return slice(n * KB, (n + 1) * KB)


def scores_of(k, q):
    return lax.dot_general(k, q, (((1,), (1,)), ((), ())), preferred_element_type=jnp.float32)


def pack_kernel(count, picks_ref, k_ref, v_ref, *refs):
    planes = count // PLANE
    kv_ref, table_ref, mine_ref, cross_ref, own_refs, packet_refs = refs[0], refs[1], refs[2], refs[3], refs[4:7], refs[7:]
    me, z, r = place(count)
    dim = k_ref.shape[1]
    per_half = k_ref.shape[0] // 2 // KB
    kv_ref[:, :dim] = k_ref[...]
    kv_ref[:, dim:] = v_ref[...]

    def late_pick(source, dest):
        return jnp.maximum(picks_ref[source, 2 * count - 1 - dest], 0)

    for j, ref in enumerate(packet_refs, 1):
        up = z + j < planes
        to = jnp.where(up, 0, (z + j - planes) * PLANE)
        for t in range(PLANE):
            ref[at(t)] = kv_ref[sub(jnp.where(up, t, late_pick(me, to + t)))]
    mine_ref[...] = kv_ref[sub(late_pick(me, me))]
    for m, ref in enumerate(own_refs, 1):
        peer = r ^ m
        dest = z * PLANE + peer
        ref[at(0)] = kv_ref[sub(late_pick(me, dest))]
        ref[at(1)] = kv_ref[sub(jnp.maximum(picks_ref[me, dest], 0))]
        if m != 2:
            start = jnp.where(r < peer, 0, per_half)
            for t in range(per_half):
                ref[at(t + 2)] = kv_ref[sub(start + t)]
    start = jnp.where(r == PLANE - 1, 0, per_half)
    for t in range(per_half):
        cross_ref[at(t)] = kv_ref[sub(start + t)]
    for j in range(1, planes):
        up = z >= j
        source = jnp.where(up, z - j, z - j + planes) * PLANE + r
        for m in range(PLANE):
            peer = r ^ m
            dest = z * PLANE + peer
            row = ((j - 1) * PLANE + m) * 2
            late = jnp.where(up, late_pick(source, dest), peer)
            early = jnp.where(up, jnp.maximum(picks_ref[source, dest], 0), 0)
            table_ref[row : row + 1] = jnp.full((1, dim), late, jnp.int32)
            table_ref[row + 1 : row + 2] = jnp.full((1, dim), early, jnp.int32)


def select_kernel(count, table_ref, own2_ref, *refs):
    planes = count // PLANE
    packet_refs, moved_refs = refs[: planes - 1], refs[planes - 1 :]
    dim = table_ref.shape[1]
    moved_refs[2][at(2 * planes - 2)] = own2_ref[at(0)]
    moved_refs[2][at(2 * planes - 1)] = own2_ref[at(1)]
    for j, packet in enumerate(packet_refs):
        for part in (slice(0, dim), slice(dim, 2 * dim)):
            choices = [packet[at(t), part] for t in range(PLANE)]
            for m in range(PLANE):
                for kind in range(2):
                    row = (j * PLANE + m) * 2 + kind
                    index = jnp.broadcast_to(table_ref[row : row + 1], (KB, dim))
                    value = choices[0]
                    for t in range(1, PLANE):
                        value = jnp.where(index == t, choices[t], value)
                    moved_refs[m][at(j + kind * (planes - 1)), part] = value


def attend_all(n_cols, score, v_ts, state, save):
    ahead = score(0)
    for step in range(n_cols):
        s = ahead
        if step + 1 < n_cols:
            ahead = score(step + 1)
        m = jnp.max(s, axis=0, keepdims=True)
        if state is not None:
            m_old, l_old, acc_old = state(step)
            m = jnp.maximum(m, m_old)
        w = jnp.exp2(s - m)
        l = jnp.sum(w, axis=0, keepdims=True)
        acc = jnp.dot(v_ts, w.astype(jnp.bfloat16), preferred_element_type=jnp.float32)
        if state is not None:
            old = jnp.exp2(m_old - m)
            l = l + l_old * old
            acc = acc + acc_old * old
        save(step, m, l, acc)


def fold(kv, masks, scale, width, block, rot_ref, old_refs, save):
    dim = rot_ref.shape[2]
    total = len(masks)
    steps = rot_ref.shape[1] // width
    carried = [tuple(ref[block, :, step * width : (step + 1) * width] for ref in old_refs) for step in range(steps)]
    for first in range(0, total, CHUNK):
        last = min(first + CHUNK, total)
        k = kv[first * KB : last * KB, :dim]
        v_t = kv[first * KB : last * KB, dim:].T

        def score(step, k=k, first=first, last=last):
            s = scores_of(k, rot_ref[block, step * width : (step + 1) * width, :]) * scale
            if all(ok is None for ok in masks[first:last]):
                return s
            return jnp.concatenate(
                [s[at(g - first)] if masks[g] is None else jnp.where(masks[g], s[at(g - first)], NEG) for g in range(first, last)]
            )

        def keep(step, *values):
            carried[step] = values

        attend_all(steps, score, v_t, carried.__getitem__, save if last == total else keep)


def near_kernel(scale, width, q_ref, basis_ref, kv_ref, rot_ref, m_ref, l_ref, acc_ref):
    dim = basis_ref.shape[0]
    half = q_ref.shape[0] // 2
    heads = q_ref.shape[1] // dim
    basis = basis_ref[...]
    key_row = lax.broadcasted_iota(jnp.int32, (half, width), 0)
    query = lax.broadcasted_iota(jnp.int32, (half, width), 1) % half
    causal = key_row <= query
    for block in range(2):
        rows = slice(block * half, (block + 1) * half)
        for h in range(heads):
            q = jnp.dot(q_ref[rows, h * dim : (h + 1) * dim], basis, preferred_element_type=jnp.float32)
            rot_ref[block, h * half : (h + 1) * half, :] = q.astype(jnp.bfloat16)
    for block in range(2):
        rows = slice(block * half, (block + 1) * half)
        k, v_t = kv_ref[rows, :dim], kv_ref[rows, dim:].T

        def score(step, block=block, k=k):
            s = scores_of(k, rot_ref[block, step * width : (step + 1) * width, :]) * scale
            return jnp.where(causal, s, NEG)

        def save(step, m, l, acc, block=block):
            for ref, value in zip((m_ref, l_ref, acc_ref), (m, l, acc), strict=True):
                ref[block, :, step * width : (step + 1) * width] = value

        attend_all(heads * half // width, score, v_t, None, save)


def mid_kernel(count, scale, width, *refs):
    kv_ref, cross_ref, own1_ref, own3_ref, mine_ref, moved_ref = refs[:6]
    rot_ref, old, new = refs[6], refs[7:10], refs[10:13]
    me, z, r = place(count)
    planes = count // PLANE
    half = cross_ref.shape[0]
    cross, own1, own3 = cross_ref[...], own1_ref[2 * KB :], own3_ref[2 * KB :]
    for block in range(2):
        if block == 0:
            prev = jnp.where(r == 0, cross, jnp.where(r == 2, own3, own1))
            kv = [prev, own3_ref[at(1)], moved_ref[(planes - 1) * KB :]]
            masks = [me >= 1] * (half // KB) + [(r ^ 3) < r - 1] + [z >= j for j in range(1, planes)]
        else:
            prev = jnp.where(r == PLANE - 1, cross, jnp.where(r == 1, own3, own1))
            prev = jnp.where(me == count - 1, kv_ref[:half], prev)
            kv = [prev, own1_ref[at(0)], own3_ref[at(0)], mine_ref[...], moved_ref[: (planes - 1) * KB]]
            masks = [None] * (half // KB + 2) + [me < count - 1] + [None] * (planes - 1)

        def save(step, m, l, acc, block=block):
            for ref, value in zip(new, (m, l, acc), strict=True):
                ref[block, :, step * width : (step + 1) * width] = value

        fold(jnp.concatenate(kv, axis=0), masks, scale, width, block, rot_ref, old, save)


def far_kernel(count, scale, width, *refs):
    moved_refs, rot_ref, old, out_ref = refs[0:3], refs[3], refs[4:7], refs[7]
    me, z, r = place(count)
    planes = count // PLANE
    dim = rot_ref.shape[2]
    half = out_ref.shape[0] // 2

    def finish(block, step, l, acc):
        done = acc / l
        for h in range(width // half):
            head = step * (width // half) + h
            out_ref[block * half : (block + 1) * half, head * dim : (head + 1) * dim] = (
                done[:, h * half : (h + 1) * half].T.astype(out_ref.dtype)
            )

    def run(block):
        parts, masks = [], []
        for m, ref in enumerate(moved_refs, 1):
            first = (1 - block) * (planes - 1)
            parts.append(ref[first * KB : (first + planes - 1) * KB])
            masks += [None if block else (z >= j) & ((z - j) * PLANE + (r ^ m) < me - 1) for j in range(1, planes)]
        parts.append(moved_refs[1][at(2 * planes - 1 - block)])
        masks.append(None if block else (r ^ 2) < r - 1)
        kv = jnp.concatenate(parts, axis=0)
        fold(kv, masks, scale, width, block, rot_ref, old, lambda step, m, l, acc: finish(block, step, l, acc))

    run(1)

    @pl.when(me >= 2)
    def _():
        run(0)

    @pl.when(me < 2)
    def _():
        for step in range(rot_ref.shape[1] // width):
            cols = slice(step * width, (step + 1) * width)
            finish(0, step, old[1][0, :, cols], old[2][0, :, cols])


def per_device(queries, keys, values, basis, picks):
    rows_dev, dim = keys.shape
    half = rows_dev // 2
    count = lax.axis_size("pb")
    planes = count // PLANE
    wide = queries.shape[1] // dim * half
    width = 2 * half
    scale = dim**-0.5 * math.log2(math.e)
    vmem = pl.BlockSpec(memory_space=pltpu.VMEM)
    smem = pl.BlockSpec(memory_space=pltpu.SMEM)
    params = pltpu.CompilerParams(vmem_limit_bytes=VMEM_BYTES)
    bf16, f32 = jnp.bfloat16, jnp.float32
    state = [
        jax.ShapeDtypeStruct((2, 1, wide), f32),
        jax.ShapeDtypeStruct((2, 1, wide), f32),
        jax.ShapeDtypeStruct((2, dim, wide), f32),
    ]

    def rows(n):
        return jax.ShapeDtypeStruct((n * KB, 2 * dim), bf16)

    def permute(value, pairs):
        return lax.ppermute(value, "pb", pairs)

    def cost(keys_each):
        return pl.CostEstimate(
            flops=8 * wide * keys_each * dim, bytes_accessed=4_000_000, transcendentals=2 * wide * keys_each
        )

    by_source = picks.T
    per_half = half // KB
    table = jax.ShapeDtypeStruct(((planes - 1) * PLANE * 2, dim), jnp.int32)
    kv, table, mine, cross, *rest = pl.pallas_call(
        functools.partial(pack_kernel, count),
        out_shape=[rows(2 * per_half), table, rows(1), rows(per_half), rows(2 + per_half), rows(2), rows(2 + per_half)]
        + [rows(PLANE)] * (planes - 1),
        in_specs=[smem, vmem, vmem],
        out_specs=[vmem] * (6 + planes),
        compiler_params=pltpu.CompilerParams(vmem_limit_bytes=62 * 1024 * 1024),
        name="pack",
    )(by_source, keys, values)
    own, packets = rest[:3], rest[3:]

    packets = [
        permute(packet, [(s, (s + j * PLANE) % count) for s in range(count)]) for j, packet in enumerate(packets, 1)
    ]

    near = pl.pallas_call(
        functools.partial(near_kernel, scale, width),
        out_shape=[jax.ShapeDtypeStruct((2, wide, dim), bf16)] + state,
        in_specs=[vmem] * 3,
        out_specs=[vmem] * 4,
        compiler_params=params,
        cost_estimate=cost(half),
        name="near",
    )(queries, basis, kv)
    packets, near = lax.optimization_barrier((packets, near))
    direct = [permute(own[m - 1], [(s, s ^ m) for s in range(count)]) for m in (1, 3)]
    borders = range(PLANE - 1, count - 1, PLANE)
    cross = permute(cross, [(s, s + 1) for s in borders] + [(s + 1, s) for s in borders])

    moved = list(
        pl.pallas_call(
            functools.partial(select_kernel, count),
            out_shape=[rows(2 * planes - 2 + 2 * (m == 2)) for m in range(PLANE)],
            in_specs=[vmem] * (planes + 1),
            out_specs=[vmem] * PLANE,
            compiler_params=params,
            name="select",
        )(table, own[1], *packets)
    )
    for m in (2, 3):
        moved[m] = permute(moved[m], [(s, s ^ m) for s in range(count)])

    mid = pl.pallas_call(
        functools.partial(mid_kernel, count, scale, width),
        out_shape=state,
        in_specs=[vmem] * 10,
        out_specs=[vmem] * 3,
        compiler_params=params,
        cost_estimate=cost(2 * half),
        name="mid",
    )(kv, cross, *direct, mine, moved[0], *near)
    moved[1], mid = lax.optimization_barrier((moved[1], mid))
    moved[1] = permute(moved[1], [(s, s ^ 1) for s in range(count)])

    return pl.pallas_call(
        functools.partial(far_kernel, count, scale, width),
        out_shape=jax.ShapeDtypeStruct(queries.shape, bf16),
        in_specs=[vmem] * 7,
        out_specs=vmem,
        compiler_params=params,
        cost_estimate=cost(3 * half),
        name="far",
    )(*moved[1:], near[0], *mid)


def solution(mesh):
    in_specs = (P("pb", "grp"), P("pb", "grp"), P("pb", "grp"), P("grp", None), P("grp", None))
    out_specs = P("pb", "grp")
    return jax.shard_map(
        per_device, mesh=mesh, in_specs=in_specs, out_specs=out_specs, check_vma=False
    )
```

```python
import functools
import math

import jax
import jax.numpy as jnp
from jax import lax
from jax.experimental import pallas as pl
from jax.experimental.pallas import tpu as pltpu
from jax.sharding import PartitionSpec as P

KB = 32
PLANE = 4
NEG = -1e30
VMEM_BYTES = 40 * 1024 * 1024
CHUNK = 16


def place(count):
    me = lax.axis_index("pb")
    return me, me // PLANE, me % PLANE


def sub(index):
    return pl.ds(pl.multiple_of(index * KB, KB), KB)


def at(n):
    return slice(n * KB, (n + 1) * KB)


def scores_of(k, q):
    return lax.dot_general(k, q, (((1,), (1,)), ((), ())), preferred_element_type=jnp.float32)


def pack_kernel(count, picks_ref, k_ref, v_ref, *refs):
    planes = count // PLANE
    kv_ref, table_ref, own_ref, inner_ref, cross_ref, packet_refs = *refs[:5], refs[5:]
    me, z, r = place(count)
    dim = k_ref.shape[1]
    per_half = k_ref.shape[0] // 2 // KB
    kv_ref[:, :dim] = k_ref[...]
    kv_ref[:, dim:] = v_ref[...]

    def late_pick(source, dest):
        return jnp.maximum(picks_ref[source, 2 * count - 1 - dest], 0)

    def early_pick(source, dest):
        return jnp.maximum(picks_ref[source, dest], 0)

    for j, ref in enumerate(packet_refs, 1):
        up = z + j < planes
        to = jnp.where(up, 0, (z + j - planes) * PLANE)
        for t in range(PLANE):
            ref[at(t)] = kv_ref[sub(jnp.where(up, t, late_pick(me, to + t)))]
    for m in range(PLANE):
        dest = z * PLANE + (r ^ m)
        own_ref[at(2 * m)] = kv_ref[sub(late_pick(me, dest))]
        own_ref[at(2 * m + 1)] = kv_ref[sub(early_pick(me, dest))]
    for t in range(per_half):
        index = jnp.where(r == 1, t, per_half + t)
        if t == 0:
            index = jnp.where(r == 0, early_pick(me, me + PLANE - 1), index)
        inner_ref[at(t)] = kv_ref[sub(index)]
        cross_ref[at(t)] = kv_ref[sub(jnp.where(r == PLANE - 1, t, per_half + t))]
    for j in range(1, planes):
        up = z >= j
        source = jnp.where(up, z - j, z - j + planes) * PLANE + r
        for m in range(PLANE):
            peer = r ^ m
            dest = z * PLANE + peer
            row = ((j - 1) * PLANE + m) * 2
            late = jnp.where(up, late_pick(source, dest), peer)
            early = jnp.where(up, early_pick(source, dest), 0)
            table_ref[row : row + 1] = jnp.full((1, dim), late, jnp.int32)
            table_ref[row + 1 : row + 2] = jnp.full((1, dim), early, jnp.int32)


def select_kernel(count, table_ref, own_ref, kv_ref, *refs):
    planes = count // PLANE
    packet_refs, moved_refs = refs[: planes - 1], refs[planes - 1 :]
    dim = table_ref.shape[1]
    per_half = kv_ref.shape[0] // 2 // KB
    for t in range(per_half):
        moved_refs[1][at(2 * planes + t)] = kv_ref[sub(lax.axis_index("pb") % 2 * per_half + t)]
    for m, ref in enumerate(moved_refs):
        ref[at(0)] = own_ref[at(2 * m)]
        if m < PLANE - 1:
            ref[at(planes)] = own_ref[at(2 * m + 1)]
    for j, packet in enumerate(packet_refs, 1):
        for part in (slice(0, dim), slice(dim, 2 * dim)):
            choices = [packet[at(t), part] for t in range(PLANE)]
            for m, ref in enumerate(moved_refs):
                for kind in range(2):
                    row = ((j - 1) * PLANE + m) * 2 + kind
                    index = jnp.broadcast_to(table_ref[row : row + 1], (KB, dim))
                    value = choices[0]
                    for t in range(1, PLANE):
                        value = jnp.where(index == t, choices[t], value)
                    ref[at(kind * (planes - (m == PLANE - 1)) + j), part] = value


def usable(count, block, m):
    me, z, r = place(count)
    planes = count // PLANE
    if block == 1:
        return [me < count - 1 if m == 0 else None] + [None] * (planes - 1)
    return [(r ^ m) < r - 1] + [(z >= j) & ((z - j) * PLANE + (r ^ m) < me - 1) for j in range(1, planes)]


def attend_all(n_cols, score, v_ts, state, save):
    ahead = score(0)
    for step in range(n_cols):
        s = ahead
        if step + 1 < n_cols:
            ahead = score(step + 1)
        m = jnp.max(s, axis=0, keepdims=True)
        if state is not None:
            m_old, l_old, acc_old = state(step)
            m = jnp.maximum(m, m_old)
        w = jnp.exp2(s - m)
        l = jnp.sum(w, axis=0, keepdims=True)
        acc = jnp.dot(v_ts, w.astype(jnp.bfloat16), preferred_element_type=jnp.float32)
        if state is not None:
            old = jnp.exp2(m_old - m)
            l = l + l_old * old
            acc = acc + acc_old * old
        save(step, m, l, acc)


def fold(kv, masks, scale, width, block, rot_ref, old_refs, save):
    dim = rot_ref.shape[2]
    total = len(masks)
    steps = rot_ref.shape[1] // width
    carried = [tuple(ref[block, :, step * width : (step + 1) * width] for ref in old_refs) for step in range(steps)]
    for first in range(0, total, CHUNK):
        last = min(first + CHUNK, total)
        k = kv[first * KB : last * KB, :dim]
        v_t = kv[first * KB : last * KB, dim:].T

        def score(step, k=k, first=first, last=last):
            s = scores_of(k, rot_ref[block, step * width : (step + 1) * width, :]) * scale
            if all(ok is None for ok in masks[first:last]):
                return s
            return jnp.concatenate(
                [s[at(g - first)] if masks[g] is None else jnp.where(masks[g], s[at(g - first)], NEG) for g in range(first, last)]
            )

        def keep(step, *values):
            carried[step] = values

        attend_all(steps, score, v_t, carried.__getitem__, save if last == total else keep)


def near_kernel(scale, width, q_ref, basis_ref, kv_ref, rot_ref, m_ref, l_ref, acc_ref):
    dim = basis_ref.shape[0]
    half = q_ref.shape[0] // 2
    heads = q_ref.shape[1] // dim
    basis = basis_ref[...]
    key_row = lax.broadcasted_iota(jnp.int32, (half, width), 0)
    query = lax.broadcasted_iota(jnp.int32, (half, width), 1) % half
    causal = key_row <= query
    for block in range(2):
        rows = slice(block * half, (block + 1) * half)
        for h in range(heads):
            q = jnp.dot(q_ref[rows, h * dim : (h + 1) * dim], basis, preferred_element_type=jnp.float32)
            rot_ref[block, h * half : (h + 1) * half, :] = q.astype(jnp.bfloat16)
    for block in range(2):
        rows = slice(block * half, (block + 1) * half)
        k, v_t = kv_ref[rows, :dim], kv_ref[rows, dim:].T

        def score(step, block=block, k=k):
            s = scores_of(k, rot_ref[block, step * width : (step + 1) * width, :]) * scale
            return jnp.where(causal, s, NEG)

        def save(step, m, l, acc, block=block):
            for ref, value in zip((m_ref, l_ref, acc_ref), (m, l, acc), strict=True):
                ref[block, :, step * width : (step + 1) * width] = value

        attend_all(heads * half // width, score, v_t, None, save)


def gathered(count, moved_refs, first_m, block, inner_ref, prev):
    planes = count // PLANE
    kv, masks = [], []
    for i, ref in enumerate(moved_refs):
        ok = usable(count, block, first_m + i)
        if first_m + i == PLANE - 1 and block == 0:
            kv += [inner_ref[at(0)], ref[planes * KB :]]
        else:
            first = (1 - block) * planes * KB
            kv.append(ref[first : first + planes * KB])
        masks += ok
    if prev is not None:
        kv.append(prev)
        masks += [lax.axis_index("pb") >= 1 if block == 0 else None] * (prev.shape[0] // KB)
    return jnp.concatenate(kv, axis=0), masks


def mid_kernel(count, scale, width, *refs):
    moved_refs, rot_ref, old, new = refs[0:2], refs[2], refs[3:6], refs[6:9]
    odd = lax.axis_index("pb") % 2 == 1
    after = 2 * (count // PLANE) * KB

    def run(block, with_prev):
        def save(step, m, l, acc):
            for ref, value in zip(new, (m, l, acc), strict=True):
                ref[block, :, step * width : (step + 1) * width] = value

        kv, masks = gathered(count, moved_refs, 0, block, None, moved_refs[1][after:] if with_prev else None)
        fold(kv, masks, scale, width, block, rot_ref, old, save)

    @pl.when(odd)
    def _():
        run(0, True)
        run(1, False)

    @pl.when(jnp.logical_not(odd))
    def _():
        run(0, False)
        run(1, True)


def far_kernel(count, scale, width, *refs):
    kv_ref, inner_ref, cross_ref, moved_refs, rot_ref, old, out_ref = *refs[:3], refs[3:5], refs[5], refs[6:9], refs[9]
    me, _, r = place(count)
    odd = me % 2 == 1
    dim = rot_ref.shape[2]
    half = out_ref.shape[0] // 2

    def finish(block, step, l, acc):
        done = acc / l
        for h in range(width // half):
            head = step * (width // half) + h
            out_ref[block * half : (block + 1) * half, head * dim : (head + 1) * dim] = (
                done[:, h * half : (h + 1) * half].T.astype(out_ref.dtype)
            )

    def run(block, with_prev):
        prev = None
        if with_prev:
            prev = jnp.where((r == 0) | (r == PLANE - 1), cross_ref[...], inner_ref[...])
            if block == 1:
                prev = jnp.where(me == count - 1, kv_ref[:half], prev)
        kv, masks = gathered(count, moved_refs, 2, block, inner_ref, prev)
        fold(kv, masks, scale, width, block, rot_ref, old, lambda step, m, l, acc: finish(block, step, l, acc))

    @pl.when(odd)
    def _():
        run(1, True)

    @pl.when(jnp.logical_not(odd))
    def _():
        run(1, False)

    @pl.when((me >= 2) & odd)
    def _():
        run(0, False)

    @pl.when((me >= 2) & jnp.logical_not(odd))
    def _():
        run(0, True)

    @pl.when(me < 2)
    def _():
        for step in range(rot_ref.shape[1] // width):
            cols = slice(step * width, (step + 1) * width)
            finish(0, step, old[1][0, :, cols], old[2][0, :, cols])


def per_device(queries, keys, values, basis, picks):
    rows_dev, dim = keys.shape
    half = rows_dev // 2
    count = lax.axis_size("pb")
    planes = count // PLANE
    wide = queries.shape[1] // dim * half
    width = 2 * half
    scale = dim**-0.5 * math.log2(math.e)
    vmem = pl.BlockSpec(memory_space=pltpu.VMEM)
    smem = pl.BlockSpec(memory_space=pltpu.SMEM)
    params = pltpu.CompilerParams(vmem_limit_bytes=VMEM_BYTES)
    bf16, f32 = jnp.bfloat16, jnp.float32
    state = [
        jax.ShapeDtypeStruct((2, 1, wide), f32),
        jax.ShapeDtypeStruct((2, 1, wide), f32),
        jax.ShapeDtypeStruct((2, dim, wide), f32),
    ]

    def rows(n):
        return jax.ShapeDtypeStruct((n * KB, 2 * dim), bf16)

    def permute(value, pairs):
        return lax.ppermute(value, "pb", pairs)

    def cost(keys_each):
        return pl.CostEstimate(
            flops=8 * wide * keys_each * dim, bytes_accessed=4_000_000, transcendentals=2 * wide * keys_each
        )

    by_source = picks.T
    per_half = half // KB
    table = jax.ShapeDtypeStruct(((planes - 1) * PLANE * 2, dim), jnp.int32)
    kv, table, own, inner, cross, *packets = pl.pallas_call(
        functools.partial(pack_kernel, count),
        out_shape=[rows(2 * per_half), table, rows(2 * PLANE), rows(per_half), rows(per_half)]
        + [rows(PLANE)] * (planes - 1),
        in_specs=[smem, vmem, vmem],
        out_specs=[vmem] * (4 + planes),
        compiler_params=pltpu.CompilerParams(vmem_limit_bytes=60 * 1024 * 1024),
        name="pack",
    )(by_source, keys, values)

    packets = [
        permute(packet, [(s, (s + j * PLANE) % count) for s in range(count)]) for j, packet in enumerate(packets, 1)
    ]

    near = pl.pallas_call(
        functools.partial(near_kernel, scale, width),
        out_shape=[jax.ShapeDtypeStruct((2, wide, dim), bf16)] + state,
        in_specs=[vmem] * 3,
        out_specs=[vmem] * 4,
        compiler_params=params,
        cost_estimate=cost(half),
        name="near",
    )(queries, basis, kv)
    packets, near = lax.optimization_barrier((packets, near))
    inner = permute(inner, [(s, s ^ (PLANE - 1)) for s in range(count)])
    packets, inner = lax.optimization_barrier((packets, inner))

    sizes = [2 * planes, 2 * planes + per_half, 2 * planes, 2 * planes - 1]
    moved = list(
        pl.pallas_call(
            functools.partial(select_kernel, count),
            out_shape=[rows(size) for size in sizes],
            in_specs=[vmem] * (planes + 2),
            out_specs=[vmem] * PLANE,
            compiler_params=params,
            name="select",
        )(table, own, kv, *packets)
    )
    moved[1:] = [permute(moved[m], [(s, s ^ m) for s in range(count)]) for m in range(1, PLANE)]
    borders = range(PLANE - 1, count - 1, PLANE)
    cross = permute(cross, [(s, s + 1) for s in borders] + [(s + 1, s) for s in borders])

    mid = pl.pallas_call(
        functools.partial(mid_kernel, count, scale, width),
        out_shape=state,
        in_specs=[vmem] * 6,
        out_specs=[vmem] * 3,
        compiler_params=params,
        cost_estimate=cost(3 * half),
        name="mid",
    )(*moved[:2], *near)

    return pl.pallas_call(
        functools.partial(far_kernel, count, scale, width),
        out_shape=jax.ShapeDtypeStruct(queries.shape, bf16),
        in_specs=[vmem] * 9,
        out_specs=vmem,
        compiler_params=params,
        cost_estimate=cost(2 * half),
        name="far",
    )(kv, inner, cross, *moved[2:], near[0], *mid)


def solution(mesh):
    in_specs = (P("pb", "grp"), P("pb", "grp"), P("pb", "grp"), P("grp", None), P("grp", None))
    out_specs = P("pb", "grp")
    return jax.shard_map(
        per_device, mesh=mesh, in_specs=in_specs, out_specs=out_specs, check_vma=False
    )
```

```python
import functools
import math

import jax
import jax.numpy as jnp
from jax import lax
from jax.experimental import pallas as pl
from jax.experimental.pallas import tpu as pltpu
from jax.sharding import PartitionSpec as P

KB = 32
PLANE = 4
NEG = -1e30
VMEM_BYTES = 40 * 1024 * 1024
CHUNK = 16


def place(count):
    me = lax.axis_index("pb")
    return me, me // PLANE, me % PLANE


def sub(index):
    return pl.ds(pl.multiple_of(index * KB, KB), KB)


def at(n):
    return slice(n * KB, (n + 1) * KB)


def scores_of(k, q):
    return lax.dot_general(k, q, (((1,), (1,)), ((), ())), preferred_element_type=jnp.float32)


def splat(picks_ref, wanted, width):
    lane = lax.broadcasted_iota(jnp.int32, (1, picks_ref.shape[1]), 1)
    rows = [jnp.where(lane == block, picks_ref[pl.ds(source, 1), :], 0) for source, block in wanted]
    total = jnp.sum(jnp.concatenate(rows, axis=0), axis=1, keepdims=True)
    return jnp.broadcast_to(jnp.maximum(total, 0), (len(wanted), width))


def chosen(index, choices):
    index = jnp.broadcast_to(index, choices[0].shape)
    value = choices[0]
    for t, choice in enumerate(choices[1:], 1):
        value = jnp.where(index == t, choice, value)
    return value


def pack_kernel(count, picks_ref, both_ref, *refs):
    planes = count // PLANE
    kv_ref, table_ref, own_ref, inner_ref, cross_ref, packet_refs = *refs[:5], refs[5:]
    me, z, r = place(count)
    dim = both_ref.shape[1]
    total = both_ref.shape[0] // 2 // KB
    per_half = total // 2
    for part in range(2):
        kv_ref[:, part * dim : (part + 1) * dim] = both_ref[part * total * KB : (part + 1) * total * KB]
    wanted, down = [], []
    for j in range(1, planes):
        up = z + j < planes
        to = jnp.where(up, 0, (z + j - planes) * PLANE)
        wanted += [(me, 2 * count - 1 - (to + t)) for t in range(PLANE)]
        down += [up] * PLANE
    for m in range(PLANE):
        dest = z * PLANE + (r ^ m)
        wanted += [(me, 2 * count - 1 - dest), (me, dest)]
    wanted.append((me, jnp.minimum(me + PLANE - 1, count - 1)))
    index = splat(picks_ref, wanted, dim)
    for part in range(2):
        cols = slice(part * dim, (part + 1) * dim)
        subs = [both_ref[at(part * total + t)] for t in range(total)]
        for g, up in enumerate(down):
            j, t = g // PLANE, g % PLANE
            packet_refs[j][at(t), cols] = jnp.where(up, subs[t], chosen(index[g : g + 1], subs))
        for g in range(2 * PLANE):
            i = len(down) + g
            own_ref[at(g), cols] = chosen(index[i : i + 1], subs)
        for t in range(per_half):
            inner = jnp.where(r == 1, subs[t], subs[per_half + t])
            if t == 0:
                inner = jnp.where(r == 0, chosen(index[len(wanted) - 1 :], subs), inner)
            inner_ref[at(t), cols] = inner
            cross_ref[at(t), cols] = jnp.where(r == PLANE - 1, subs[t], subs[per_half + t])
    wanted, fixed = [], []
    for j in range(1, planes):
        up = z >= j
        source = jnp.where(up, z - j, z - j + planes) * PLANE + r
        for m in range(PLANE):
            dest = z * PLANE + (r ^ m)
            wanted += [(source, 2 * count - 1 - dest), (source, dest)]
            fixed += [(up, r ^ m), (up, 0)]
    index = splat(picks_ref, wanted, dim)
    for g, (up, other) in enumerate(fixed):
        table_ref[g : g + 1] = jnp.where(up, index[g : g + 1], other)


def select_kernel(count, table_ref, own_ref, kv_ref, *refs):
    planes = count // PLANE
    packet_refs, moved_refs = refs[: planes - 1], refs[planes - 1 :]
    dim = table_ref.shape[1]
    per_half = kv_ref.shape[0] // 2 // KB
    for t in range(per_half):
        moved_refs[1][at(2 * planes + t)] = kv_ref[sub(lax.axis_index("pb") % 2 * per_half + t)]
    for m in range(PLANE):
        moved_refs[m][at(0)] = own_ref[at(2 * m)]
        if m < PLANE - 1:
            moved_refs[m][at(planes)] = own_ref[at(2 * m + 1)]
    for j, packet in enumerate(packet_refs, 1):
        for part in (slice(0, dim), slice(dim, 2 * dim)):
            choices = [packet[at(t), part] for t in range(PLANE)]
            for m in range(PLANE):
                row = ((j - 1) * PLANE + m) * 2
                moved_refs[m][at(j), part] = chosen(table_ref[row : row + 1], choices)
                early = chosen(table_ref[row + 1 : row + 2], choices)
                if m < 2:
                    moved_refs[m][at(planes + j), part] = early
                else:
                    moved_refs[m][at(planes + j - (m == 3)), part] = early


def usable(count, block, m):
    me, z, r = place(count)
    planes = count // PLANE
    if block == 1:
        return [me < count - 1 if m == 0 else None] + [None] * (planes - 1)
    return [(r ^ m) < r - 1] + [(z >= j) & ((z - j) * PLANE + (r ^ m) < me - 1) for j in range(1, planes)]


def attend_all(n_cols, score, v_ts, state, save):
    ahead = score(0)
    for step in range(n_cols):
        s = ahead
        if step + 1 < n_cols:
            ahead = score(step + 1)
        m = jnp.max(s, axis=0, keepdims=True)
        if state is not None:
            m_old, l_old, acc_old = state(step)
            m = jnp.maximum(m, m_old)
        w = jnp.exp2(s - m)
        l = jnp.sum(w, axis=0, keepdims=True)
        acc = jnp.dot(v_ts, w.astype(jnp.bfloat16), preferred_element_type=jnp.float32)
        if state is not None:
            old = jnp.exp2(m_old - m)
            l = l + l_old * old
            acc = acc + acc_old * old
        save(step, m, l, acc)


def fold(kv, masks, scale, width, block, rot_ref, old_refs, save):
    dim = rot_ref.shape[2]
    total = len(masks)
    steps = rot_ref.shape[1] // width
    carried = [tuple(ref[block, :, step * width : (step + 1) * width] for ref in old_refs) for step in range(steps)]
    for first in range(0, total, CHUNK):
        last = min(first + CHUNK, total)
        k = kv[first * KB : last * KB, :dim]
        v_t = kv[first * KB : last * KB, dim:].T

        def score(step, k=k, first=first, last=last):
            s = scores_of(k, rot_ref[block, step * width : (step + 1) * width, :]) * scale
            if all(ok is None for ok in masks[first:last]):
                return s
            return jnp.concatenate(
                [s[at(g - first)] if masks[g] is None else jnp.where(masks[g], s[at(g - first)], NEG) for g in range(first, last)]
            )

        def keep(step, *values):
            carried[step] = values

        attend_all(steps, score, v_t, carried.__getitem__, save if last == total else keep)


def near_kernel(scale, width, q_ref, basis_ref, kv_ref, rot_ref, m_ref, l_ref, acc_ref):
    dim = basis_ref.shape[0]
    half = q_ref.shape[0] // 2
    heads = q_ref.shape[1] // dim
    basis = basis_ref[...]
    key_row = lax.broadcasted_iota(jnp.int32, (half, width), 0)
    query = lax.broadcasted_iota(jnp.int32, (half, width), 1) % half
    causal = key_row <= query
    for block in range(2):
        rows = slice(block * half, (block + 1) * half)
        for h in range(heads):
            q = jnp.dot(q_ref[rows, h * dim : (h + 1) * dim], basis, preferred_element_type=jnp.float32)
            rot_ref[block, h * half : (h + 1) * half, :] = q.astype(jnp.bfloat16)
    for block in range(2):
        rows = slice(block * half, (block + 1) * half)
        k, v_t = kv_ref[rows, :dim], kv_ref[rows, dim:].T

        def score(step, block=block, k=k):
            s = scores_of(k, rot_ref[block, step * width : (step + 1) * width, :]) * scale
            return jnp.where(causal, s, NEG)

        def save(step, m, l, acc, block=block):
            for ref, value in zip((m_ref, l_ref, acc_ref), (m, l, acc), strict=True):
                ref[block, :, step * width : (step + 1) * width] = value

        attend_all(heads * half // width, score, v_t, None, save)


def fold_kernel(count, scale, width, first_m, *refs):
    inner_ref, moved_refs, rot_ref, old, new = refs[0], refs[1:-7], refs[-7], refs[-6:-3], refs[-3:]
    me, _, r = place(count)
    even = me % 2 == 0
    late = (count // PLANE) * KB

    def run(block):
        parts, masks = [], []
        for i, ref in enumerate(moved_refs):
            m = first_m + i
            masks += usable(count, block, m)
            if block == 1:
                parts.append(ref[:late])
            elif m == PLANE - 1:
                parts += [inner_ref[at(0)], ref[late : 2 * late - KB]]
            else:
                parts.append(ref[late : 2 * late])
        if first_m == 0:
            beside = even if block == 1 else jnp.logical_not(even)
            parts.append(jnp.where(beside, moved_refs[1][2 * late :], inner_ref[...]))
            masks += [beside | (r == 1 + (1 - block))] * (inner_ref.shape[0] // KB)

        def save(step, m, l, acc):
            for ref, value in zip(new, (m, l, acc), strict=True):
                ref[block, :, step * width : (step + 1) * width] = value

        fold(jnp.concatenate(parts, axis=0), masks, scale, width, block, rot_ref, old, save)

    run(1)
    pl.when(me >= (1 if first_m == 0 else 2))(lambda: run(0))


def last_kernel(count, scale, width, kv_ref, cross_ref, rot_ref, m_ref, l_ref, acc_ref, out_ref):
    me, z, r = place(count)
    half = out_ref.shape[0] // 2
    dim = rot_ref.shape[2]
    old = (m_ref, l_ref, acc_ref)

    def finish(block, step, l, acc):
        done = acc / l
        for h in range(width // half):
            head = step * (width // half) + h
            out_ref[block * half : (block + 1) * half, head * dim : (head + 1) * dim] = (
                done[:, h * half : (h + 1) * half].T.astype(out_ref.dtype)
            )

    def add(block):
        prev = cross_ref[...]
        if block == 1:
            prev = jnp.where(me == count - 1, kv_ref[:half], prev)
        masks = [None] * (half // KB)
        fold(prev, masks, scale, width, block, rot_ref, old, lambda step, m, l, acc: finish(block, step, l, acc))

    def close(block):
        for step in range(rot_ref.shape[1] // width):
            cols = slice(step * width, (step + 1) * width)
            finish(block, step, l_ref[block, :, cols], acc_ref[block, :, cols])

    for block, outer in enumerate(((r == 0) & (z > 0), r == PLANE - 1)):
        pl.when(outer)(functools.partial(add, block))
        pl.when(jnp.logical_not(outer))(functools.partial(close, block))


def per_device(queries, keys, values, basis, picks):
    rows_dev, dim = keys.shape
    half = rows_dev // 2
    count = lax.axis_size("pb")
    planes = count // PLANE
    wide = queries.shape[1] // dim * half
    width = 2 * half
    scale = dim**-0.5 * math.log2(math.e)
    vmem = pl.BlockSpec(memory_space=pltpu.VMEM)
    params = pltpu.CompilerParams(vmem_limit_bytes=VMEM_BYTES)
    bf16, f32 = jnp.bfloat16, jnp.float32
    shapes = [
        jax.ShapeDtypeStruct((2, 1, wide), f32),
        jax.ShapeDtypeStruct((2, 1, wide), f32),
        jax.ShapeDtypeStruct((2, dim, wide), f32),
    ]

    def rows(n):
        return jax.ShapeDtypeStruct((n * KB, 2 * dim), bf16)

    def permute(value, pairs):
        return lax.ppermute(value, "pb", pairs)

    def cost(keys_each):
        return pl.CostEstimate(
            flops=8 * wide * keys_each * dim, bytes_accessed=4_000_000, transcendentals=2 * wide * keys_each
        )

    per_half = half // KB
    table = jax.ShapeDtypeStruct(((planes - 1) * PLANE * 2, dim), jnp.int32)
    kv, table, own, inner, cross, *packets = pl.pallas_call(
        functools.partial(pack_kernel, count),
        out_shape=[rows(2 * per_half), table, rows(2 * PLANE), rows(per_half), rows(per_half)]
        + [rows(PLANE)] * (planes - 1),
        in_specs=[vmem] * 2,
        out_specs=[vmem] * (4 + planes),
        compiler_params=params,
        name="pack",
    )(picks.T, jnp.concatenate([keys, values]))

    packets = [
        permute(packet, [(s, (s + j * PLANE) % count) for s in range(count)]) for j, packet in enumerate(packets, 1)
    ]

    near = pl.pallas_call(
        functools.partial(near_kernel, scale, width),
        out_shape=[jax.ShapeDtypeStruct((2, wide, dim), bf16)] + shapes,
        in_specs=[vmem] * 3,
        out_specs=[vmem] * 4,
        compiler_params=params,
        cost_estimate=cost(half),
        name="near",
    )(queries, basis, kv)
    packets, near = lax.optimization_barrier((packets, near))
    inner = permute(inner, [(s, s ^ (PLANE - 1)) for s in range(count)])

    sizes = [2 * planes, 2 * planes + per_half, 2 * planes, 2 * planes - 1]
    moved = list(
        pl.pallas_call(
            functools.partial(select_kernel, count),
            out_shape=[rows(size) for size in sizes],
            in_specs=[vmem] * (planes + 2),
            out_specs=[vmem] * len(sizes),
            compiler_params=params,
            name="select",
        )(table, own, kv, *packets)
    )
    moved[1], inner = lax.optimization_barrier((moved[1], inner))
    for m in range(1, PLANE):
        moved[m] = permute(moved[m], [(s, s ^ m) for s in range(count)])

    rotated, *state = near

    def folded(state, first_m, messages):
        return pl.pallas_call(
            functools.partial(fold_kernel, count, scale, width, first_m),
            out_shape=shapes,
            in_specs=[vmem] * (5 + len(messages)),
            out_specs=[vmem] * 3,
            input_output_aliases={2 + len(messages) + i: i for i in range(3)},
            compiler_params=params,
            cost_estimate=cost(half * len(messages)),
            name=f"fold{first_m}",
        )(inner, *messages, rotated, *state)

    state = folded(state, 0, moved[:2])
    borders = range(PLANE - 1, count - 1, PLANE)
    cross = permute(cross, [(s, s + 1) for s in borders] + [(s + 1, s) for s in borders])
    state = folded(state, 2, moved[2:3])
    state = folded(state, 3, moved[3:4])
    return pl.pallas_call(
        functools.partial(last_kernel, count, scale, width),
        out_shape=jax.ShapeDtypeStruct(queries.shape, bf16),
        in_specs=[vmem] * 6,
        out_specs=vmem,
        compiler_params=params,
        cost_estimate=cost(half),
        name="last",
    )(kv, cross, rotated, *state)


def solution(mesh):
    in_specs = (P("pb", "grp"), P("pb", "grp"), P("pb", "grp"), P("grp", None), P("grp", None))
    out_specs = P("pb", "grp")
    return jax.shard_map(
        per_device, mesh=mesh, in_specs=in_specs, out_specs=out_specs, check_vma=False
    )
```

```python
import functools
import math

import jax
import jax.numpy as jnp
from jax import lax
from jax.experimental import pallas as pl
from jax.experimental.pallas import tpu as pltpu
from jax.sharding import PartitionSpec as P

KB = 32
PLANE = 4
NEG = -1e30
VMEM_BYTES = 40 * 1024 * 1024
CHUNK = 16


def place(count):
    me = lax.axis_index("pb")
    return me, me // PLANE, me % PLANE


def sub(index):
    return pl.ds(pl.multiple_of(index * KB, KB), KB)


def at(n):
    return slice(n * KB, (n + 1) * KB)


def scores_of(k, q):
    return lax.dot_general(k, q, (((1,), (1,)), ((), ())), preferred_element_type=jnp.float32)


def splat(picks_ref, wanted, width):
    lane = lax.broadcasted_iota(jnp.int32, (1, picks_ref.shape[1]), 1)
    rows = [jnp.where(lane == block, picks_ref[pl.ds(source, 1), :], 0) for source, block in wanted]
    total = jnp.sum(jnp.concatenate(rows, axis=0), axis=1, keepdims=True)
    return jnp.broadcast_to(jnp.maximum(total, 0), (len(wanted), width))


def chosen(index, choices):
    index = jnp.broadcast_to(index, choices[0].shape)
    value = choices[0]
    for t, choice in enumerate(choices[1:], 1):
        value = jnp.where(index == t, choice, value)
    return value


def pack_kernel(count, picks_ref, both_ref, *refs):
    planes = count // PLANE
    kv_ref, table_ref, own_ref, side_ref, packet_refs = *refs[:4], refs[4:]
    me, z, r = place(count)
    dim = both_ref.shape[1]
    total = both_ref.shape[0] // 2 // KB
    per_half = total // 2
    for part in range(2):
        kv_ref[:, part * dim : (part + 1) * dim] = both_ref[part * total * KB : (part + 1) * total * KB]
    wanted, down = [], []
    for j in range(1, planes):
        up = z + j < planes
        to = jnp.where(up, 0, (z + j - planes) * PLANE)
        wanted += [(me, 2 * count - 1 - (to + t)) for t in range(PLANE)]
        down += [up] * PLANE
    for m in range(PLANE):
        dest = z * PLANE + (r ^ m)
        wanted += [(me, 2 * count - 1 - dest), (me, dest)]
    index = splat(picks_ref, wanted, dim)
    for part in range(2):
        cols = slice(part * dim, (part + 1) * dim)
        subs = [both_ref[at(part * total + t)] for t in range(total)]
        for g, up in enumerate(down):
            j, t = g // PLANE, g % PLANE
            packet_refs[j][at(t), cols] = jnp.where(up, subs[t], chosen(index[g : g + 1], subs))
        for g in range(2 * PLANE):
            i = len(down) + g
            own_ref[at(g), cols] = chosen(index[i : i + 1], subs)
        for t in range(per_half):
            side_ref[at(t), cols] = jnp.where(me % 2 == 1, subs[t], subs[per_half + t])
    wanted, fixed = [], []
    for j in range(1, planes):
        up = z >= j
        source = jnp.where(up, z - j, z - j + planes) * PLANE + r
        for m in range(PLANE):
            dest = z * PLANE + (r ^ m)
            wanted += [(source, 2 * count - 1 - dest), (source, dest)]
            fixed += [(up, r ^ m), (up, 0)]
    index = splat(picks_ref, wanted, dim)
    for g, (up, other) in enumerate(fixed):
        table_ref[g : g + 1] = jnp.where(up, index[g : g + 1], other)


def select_kernel(count, table_ref, own_ref, kv_ref, *refs):
    planes = count // PLANE
    packet_refs, moved_refs, early_ref = refs[: planes - 1], refs[planes - 1 : planes + 3], refs[planes + 3]
    dim = table_ref.shape[1]
    per_half = kv_ref.shape[0] // 2 // KB
    for t in range(per_half):
        moved_refs[1][at(2 * planes + t)] = kv_ref[sub(lax.axis_index("pb") % 2 * per_half + t)]
    for m in range(PLANE):
        moved_refs[m][at(0)] = own_ref[at(2 * m)]
        moved_refs[m][at(planes)] = own_ref[at(2 * m + 1)]
    for j, packet in enumerate(packet_refs, 1):
        for part in (slice(0, dim), slice(dim, 2 * dim)):
            choices = [packet[at(t), part] for t in range(PLANE)]
            for m in range(PLANE):
                row = ((j - 1) * PLANE + m) * 2
                moved_refs[m][at(j), part] = chosen(table_ref[row : row + 1], choices)
                early = chosen(table_ref[row + 1 : row + 2], choices)
                if m < PLANE - 1:
                    moved_refs[m][at(planes + j), part] = early
                else:
                    early_ref[at(j - 1), part] = early


def usable(count, block, m):
    me, z, r = place(count)
    planes = count // PLANE
    if block == 1:
        return [me < count - 1 if m == 0 else None] + [None] * (planes - 1)
    return [(r ^ m) < r - 1] + [(z >= j) & ((z - j) * PLANE + (r ^ m) < me - 1) for j in range(1, planes)]


def attend_all(n_cols, score, v_ts, state, save):
    ahead = score(0)
    for step in range(n_cols):
        s = ahead
        if step + 1 < n_cols:
            ahead = score(step + 1)
        m = jnp.max(s, axis=0, keepdims=True)
        if state is not None:
            m_old, l_old, acc_old = state(step)
            m = jnp.maximum(m, m_old)
        w = jnp.exp2(s - m)
        l = jnp.sum(w, axis=0, keepdims=True)
        acc = jnp.dot(v_ts, w.astype(jnp.bfloat16), preferred_element_type=jnp.float32)
        if state is not None:
            old = jnp.exp2(m_old - m)
            l = l + l_old * old
            acc = acc + acc_old * old
        save(step, m, l, acc)


def fold(kv, masks, scale, width, block, rot_ref, old_refs, save):
    dim = rot_ref.shape[2]
    total = len(masks)
    steps = rot_ref.shape[1] // width
    carried = [tuple(ref[block, :, step * width : (step + 1) * width] for ref in old_refs) for step in range(steps)]
    for first in range(0, total, CHUNK):
        last = min(first + CHUNK, total)
        k = kv[first * KB : last * KB, :dim]
        v_t = kv[first * KB : last * KB, dim:].T

        def score(step, k=k, first=first, last=last):
            s = scores_of(k, rot_ref[block, step * width : (step + 1) * width, :]) * scale
            if all(ok is None for ok in masks[first:last]):
                return s
            return jnp.concatenate(
                [s[at(g - first)] if masks[g] is None else jnp.where(masks[g], s[at(g - first)], NEG) for g in range(first, last)]
            )

        def keep(step, *values):
            carried[step] = values

        attend_all(steps, score, v_t, carried.__getitem__, save if last == total else keep)


def near_kernel(scale, width, q_ref, basis_ref, kv_ref, rot_ref, m_ref, l_ref, acc_ref):
    dim = basis_ref.shape[0]
    half = q_ref.shape[0] // 2
    heads = q_ref.shape[1] // dim
    basis = basis_ref[...]
    key_row = lax.broadcasted_iota(jnp.int32, (half, width), 0)
    query = lax.broadcasted_iota(jnp.int32, (half, width), 1) % half
    causal = key_row <= query
    for block in range(2):
        rows = slice(block * half, (block + 1) * half)
        for h in range(heads):
            q = jnp.dot(q_ref[rows, h * dim : (h + 1) * dim], basis, preferred_element_type=jnp.float32)
            rot_ref[block, h * half : (h + 1) * half, :] = q.astype(jnp.bfloat16)
    for block in range(2):
        rows = slice(block * half, (block + 1) * half)
        k, v_t = kv_ref[rows, :dim], kv_ref[rows, dim:].T

        def score(step, block=block, k=k):
            s = scores_of(k, rot_ref[block, step * width : (step + 1) * width, :]) * scale
            return jnp.where(causal, s, NEG)

        def save(step, m, l, acc, block=block):
            for ref, value in zip((m_ref, l_ref, acc_ref), (m, l, acc), strict=True):
                ref[block, :, step * width : (step + 1) * width] = value

        attend_all(heads * half // width, score, v_t, None, save)


def fold_kernel(count, scale, width, stage, *refs):
    come, rot_ref, old, new = refs[:-7], refs[-7], refs[-6:-3], refs[-3:]
    me, z, _ = place(count)
    late = (count // PLANE) * KB

    def run(block):
        if stage == 0:
            mine_ref, next_ref, side_ref, kv_ref = come
            half = side_ref.shape[0]
            masks = usable(count, block, 0) + usable(count, block, 1) + [None] * (half // KB)
            parts = [ref[(1 - block) * late : (2 - block) * late] for ref in (mine_ref, next_ref)]
            side = side_ref[...]
            if block == 1:
                side = jnp.where(me == count - 1, kv_ref[:half], side)
            parts.append(jnp.where(me % 2 == block, side, next_ref[2 * late :]))
        else:
            first = (1 - block) * late
            parts, masks = [come[0][first : first + late]], usable(count, block, stage)

        def save(step, m, l, acc):
            for ref, value in zip(new, (m, l, acc), strict=True):
                ref[block, :, step * width : (step + 1) * width] = value

        fold(jnp.concatenate(parts, axis=0), masks, scale, width, block, rot_ref, old, save)

    if stage == 0:
        run(1)
        pl.when(me >= 1)(lambda: run(0))
    elif stage == 2:
        run(1)
        pl.when(me >= 2)(lambda: run(0))
    else:
        pl.when(z >= 1)(lambda: run(1))


def last_kernel(count, scale, width, third_ref, early_ref, rot_ref, *refs):
    old, out_ref = refs[:3], refs[3]
    me, z, _ = place(count)
    late = (count // PLANE) * KB
    half = out_ref.shape[0] // 2
    dim = rot_ref.shape[2]

    def finish(block, step, l, acc):
        done = acc / l
        for h in range(width // half):
            head = step * (width // half) + h
            out_ref[block * half : (block + 1) * half, head * dim : (head + 1) * dim] = (
                done[:, h * half : (h + 1) * half].T.astype(out_ref.dtype)
            )

    def add(block, parts, masks):
        kv = jnp.concatenate(parts, axis=0)
        fold(kv, masks, scale, width, block, rot_ref, old, lambda step, m, l, acc: finish(block, step, l, acc))

    def close(block):
        for step in range(rot_ref.shape[1] // width):
            cols = slice(step * width, (step + 1) * width)
            finish(block, step, old[1][block, :, cols], old[2][block, :, cols])

    @pl.when(z == 0)
    def _():
        add(1, [third_ref[:late]], usable(count, 1, 3))

    @pl.when(z > 0)
    def _():
        close(1)

    @pl.when(me >= 2)
    def _():
        add(0, [third_ref[late:], early_ref[...]], usable(count, 0, 3))

    @pl.when(me < 2)
    def _():
        close(0)


def per_device(queries, keys, values, basis, picks):
    rows_dev, dim = keys.shape
    half = rows_dev // 2
    count = lax.axis_size("pb")
    planes = count // PLANE
    wide = queries.shape[1] // dim * half
    width = 2 * half
    scale = dim**-0.5 * math.log2(math.e)
    vmem = pl.BlockSpec(memory_space=pltpu.VMEM)
    params = pltpu.CompilerParams(vmem_limit_bytes=VMEM_BYTES)
    bf16, f32 = jnp.bfloat16, jnp.float32
    shapes = [
        jax.ShapeDtypeStruct((2, 1, wide), f32),
        jax.ShapeDtypeStruct((2, 1, wide), f32),
        jax.ShapeDtypeStruct((2, dim, wide), f32),
    ]

    def rows(n):
        return jax.ShapeDtypeStruct((n * KB, 2 * dim), bf16)

    def permute(value, pairs):
        return lax.ppermute(value, "pb", pairs)

    def cost(keys_each):
        return pl.CostEstimate(
            flops=8 * wide * keys_each * dim, bytes_accessed=4_000_000, transcendentals=2 * wide * keys_each
        )

    per_half = half // KB
    table = jax.ShapeDtypeStruct(((planes - 1) * PLANE * 2, dim), jnp.int32)
    kv, table, own, side, *packets = pl.pallas_call(
        functools.partial(pack_kernel, count),
        out_shape=[rows(2 * per_half), table, rows(2 * PLANE), rows(per_half)]
        + [rows(PLANE)] * (planes - 1),
        in_specs=[vmem] * 2,
        out_specs=[vmem] * (3 + planes),
        compiler_params=params,
        name="pack",
    )(picks.T, jnp.concatenate([keys, values]))

    packets = [
        permute(packet, [(s, (s + j * PLANE) % count) for s in range(count)]) for j, packet in enumerate(packets, 1)
    ]

    near = pl.pallas_call(
        functools.partial(near_kernel, scale, width),
        out_shape=[jax.ShapeDtypeStruct((2, wide, dim), bf16)] + shapes,
        in_specs=[vmem] * 3,
        out_specs=[vmem] * 4,
        compiler_params=params,
        cost_estimate=cost(half),
        name="near",
    )(queries, basis, kv)
    packets, near = lax.optimization_barrier((packets, near))
    groups = lax.axis_size("grp")
    pairs = []
    for g in range(groups):
        pairs += [(g * count + s, g * count + s + (1 if s % 2 else -1)) for s in range(1, count - 1)]
        pairs += [(g * count + s, (g + 1) % groups * count + s) for s in (0, count - 1)]
    side = lax.ppermute(side, ("grp", "pb"), pairs)

    def swap(value, m):
        return permute(value, [(s, s ^ m) for s in range(count)])

    sizes = [2 * planes, 2 * planes + per_half, 2 * planes, planes + 1, planes - 1]
    moved = list(
        pl.pallas_call(
            functools.partial(select_kernel, count),
            out_shape=[rows(size) for size in sizes],
            in_specs=[vmem] * (planes + 2),
            out_specs=[vmem] * len(sizes),
            compiler_params=params,
            name="select",
        )(table, own, kv, *packets)
    )
    moved[1], side = lax.optimization_barrier((moved[1], side))
    for m in (1, 2, 3):
        moved[m] = swap(moved[m], m)
    early = permute(moved[PLANE], [(s, s ^ (PLANE - 1 if s >= PLANE else 1)) for s in range(count)])

    rotated, *state = near

    def folded(state, stage, messages):
        return pl.pallas_call(
            functools.partial(fold_kernel, count, scale, width, stage),
            out_shape=shapes,
            in_specs=[vmem] * (4 + len(messages)),
            out_specs=[vmem] * 3,
            input_output_aliases={1 + len(messages) + i: i for i in range(3)},
            compiler_params=params,
            cost_estimate=cost(half),
            name=f"fold{stage}",
        )(*messages, rotated, *state)

    state = folded(state, 0, [moved[0], moved[1], side, kv])
    state = folded(state, 2, [moved[2]])
    state = folded(state, 3, [moved[3]])
    return pl.pallas_call(
        functools.partial(last_kernel, count, scale, width),
        out_shape=jax.ShapeDtypeStruct(queries.shape, bf16),
        in_specs=[vmem] * 6,
        out_specs=vmem,
        compiler_params=params,
        cost_estimate=cost(half),
        name="last",
    )(moved[3], early, rotated, *state)


def solution(mesh):
    in_specs = (P("pb", "grp"), P("pb", "grp"), P("pb", "grp"), P("grp", None), P("grp", None))
    out_specs = P("pb", "grp")
    return jax.shard_map(
        per_device, mesh=mesh, in_specs=in_specs, out_specs=out_specs, check_vma=False
    )
```

```python
import functools
import math

import jax
import jax.numpy as jnp
from jax import lax
from jax.experimental import pallas as pl
from jax.experimental.pallas import tpu as pltpu
from jax.sharding import PartitionSpec as P

KB = 32
PLANE = 4
NEG = -1e30
VMEM_BYTES = 40 * 1024 * 1024
CHUNK = 16


def place(count):
    me = lax.axis_index("pb")
    return me, me // PLANE, me % PLANE


def sub(index):
    return pl.ds(pl.multiple_of(index * KB, KB), KB)


def at(n):
    return slice(n * KB, (n + 1) * KB)


def scores_of(k, q):
    return lax.dot_general(k, q, (((1,), (1,)), ((), ())), preferred_element_type=jnp.float32)


def splat(picks_ref, wanted, width):
    lane = lax.broadcasted_iota(jnp.int32, (1, picks_ref.shape[1]), 1)
    rows = [jnp.where(lane == block, picks_ref[pl.ds(source, 1), :], 0) for source, block in wanted]
    total = jnp.sum(jnp.concatenate(rows, axis=0), axis=1, keepdims=True)
    return jnp.broadcast_to(jnp.maximum(total, 0), (len(wanted), width))


def chosen(index, choices):
    index = jnp.broadcast_to(index, choices[0].shape)
    value = choices[0]
    for t, choice in enumerate(choices[1:], 1):
        value = jnp.where(index == t, choice, value)
    return value


def pack_kernel(count, picks_ref, both_ref, *refs):
    planes = count // PLANE
    kv_ref, table_ref, own_ref, over_ref, side_ref, packet_refs = *refs[:5], refs[5:]
    me, z, r = place(count)
    dim = both_ref.shape[1]
    total = both_ref.shape[0] // 2 // KB
    per_half = total // 2
    for part in range(2):
        kv_ref[:, part * dim : (part + 1) * dim] = both_ref[part * total * KB : (part + 1) * total * KB]
    wanted, down = [], []
    for j in range(1, planes):
        up = z + j < planes
        to = jnp.where(up, 0, (z + j - planes) * PLANE)
        wanted += [(me, 2 * count - 1 - (to + t)) for t in range(PLANE)]
        down += [up] * PLANE
    for m in (0, 1):
        wanted.append((me, 2 * count - 1 - (z * PLANE + (r ^ m))))
    for m in (2, 3):
        dest = z * PLANE + (r ^ m)
        wanted += [(me, 2 * count - 1 - dest), (me, dest)]
    index = splat(picks_ref, wanted, dim)
    for part in range(2):
        cols = slice(part * dim, (part + 1) * dim)
        subs = [both_ref[at(part * total + t)] for t in range(total)]
        for g, up in enumerate(down):
            j, t = g // PLANE, g % PLANE
            packet_refs[j][at(t), cols] = jnp.where(up, subs[t], chosen(index[g : g + 1], subs))
        for g in range(6):
            ref, t = (own_ref, g) if g < 2 else (over_ref, g - 2)
            ref[at(t), cols] = chosen(index[len(down) + g : len(down) + g + 1], subs)
        for t in range(per_half):
            side_ref[at(t), cols] = jnp.where(me % 2 == 1, subs[t], subs[per_half + t])
    wanted, fixed = [], []
    for j in range(1, planes):
        up = z >= j
        source = jnp.where(up, z - j, z - j + planes) * PLANE + r
        for m in range(PLANE):
            dest = z * PLANE + (r ^ m)
            wanted += [(source, 2 * count - 1 - dest), (source, dest)]
            fixed += [(up, r ^ m), (up, 0)]
    index = splat(picks_ref, wanted, dim)
    for g, (up, other) in enumerate(fixed):
        table_ref[g : g + 1] = jnp.where(up, index[g : g + 1], other)


def select_kernel(count, table_ref, own_ref, over_ref, kv_ref, *refs):
    planes = count // PLANE
    packet_refs, moved_refs, early_refs = refs[: planes - 1], refs[planes - 1 : planes + 3], refs[planes + 3 :]
    dim = table_ref.shape[1]
    per_half = kv_ref.shape[0] // 2 // KB
    for m in (0, 1):
        moved_refs[m][at(0)] = own_ref[at(m)]
    moved_refs[1][(2 * planes - 1) * KB : (2 * planes + 1) * KB] = over_ref[2 * KB :]
    for t in range(per_half):
        moved_refs[1][at(2 * planes + 1 + t)] = kv_ref[sub(lax.axis_index("pb") % 2 * per_half + t)]
    for j, packet in enumerate(packet_refs, 1):
        for part in (slice(0, dim), slice(dim, 2 * dim)):
            choices = [packet[at(t), part] for t in range(PLANE)]
            for m, ref in enumerate(moved_refs):
                row = ((j - 1) * PLANE + m) * 2
                first = j - (m > 1)
                ref[at(first), part] = chosen(table_ref[row : row + 1], choices)
                early = chosen(table_ref[row + 1 : row + 2], choices)
                if m < 2:
                    ref[at(first + planes - 1), part] = early
                else:
                    early_refs[m - 2][at(first), part] = early


def usable(count, block, m):
    me, z, r = place(count)
    planes = count // PLANE
    if block == 1:
        return [me < count - 1 if m == 0 else None] + [None] * (planes - 1)
    return [(r ^ m) < r - 1] + [(z >= j) & ((z - j) * PLANE + (r ^ m) < me - 1) for j in range(1, planes)]


def attend_all(n_cols, score, v_ts, state, save):
    ahead = score(0)
    for step in range(n_cols):
        s = ahead
        if step + 1 < n_cols:
            ahead = score(step + 1)
        m = jnp.max(s, axis=0, keepdims=True)
        if state is not None:
            m_old, l_old, acc_old = state(step)
            m = jnp.maximum(m, m_old)
        w = jnp.exp2(s - m)
        l = jnp.sum(w, axis=0, keepdims=True)
        acc = jnp.dot(v_ts, w.astype(jnp.bfloat16), preferred_element_type=jnp.float32)
        if state is not None:
            old = jnp.exp2(m_old - m)
            l = l + l_old * old
            acc = acc + acc_old * old
        save(step, m, l, acc)


def fold(kv, masks, scale, width, block, rot_ref, old_refs, save):
    dim = rot_ref.shape[2]
    total = len(masks)
    steps = rot_ref.shape[1] // width
    carried = [tuple(ref[block, :, step * width : (step + 1) * width] for ref in old_refs) for step in range(steps)]
    for first in range(0, total, CHUNK):
        last = min(first + CHUNK, total)
        k = kv[first * KB : last * KB, :dim]
        v_t = kv[first * KB : last * KB, dim:].T

        def score(step, k=k, first=first, last=last):
            s = scores_of(k, rot_ref[block, step * width : (step + 1) * width, :]) * scale
            if all(ok is None for ok in masks[first:last]):
                return s
            return jnp.concatenate(
                [s[at(g - first)] if masks[g] is None else jnp.where(masks[g], s[at(g - first)], NEG) for g in range(first, last)]
            )

        def keep(step, *values):
            carried[step] = values

        attend_all(steps, score, v_t, carried.__getitem__, save if last == total else keep)


def near_kernel(scale, width, q_ref, basis_ref, kv_ref, rot_ref, m_ref, l_ref, acc_ref):
    dim = basis_ref.shape[0]
    half = q_ref.shape[0] // 2
    heads = q_ref.shape[1] // dim
    basis = basis_ref[...]
    key_row = lax.broadcasted_iota(jnp.int32, (half, width), 0)
    query = lax.broadcasted_iota(jnp.int32, (half, width), 1) % half
    causal = key_row <= query
    for block in range(2):
        rows = slice(block * half, (block + 1) * half)
        for h in range(heads):
            q = jnp.dot(q_ref[rows, h * dim : (h + 1) * dim], basis, preferred_element_type=jnp.float32)
            rot_ref[block, h * half : (h + 1) * half, :] = q.astype(jnp.bfloat16)
    for block in range(2):
        rows = slice(block * half, (block + 1) * half)
        k, v_t = kv_ref[rows, :dim], kv_ref[rows, dim:].T

        def score(step, block=block, k=k):
            s = scores_of(k, rot_ref[block, step * width : (step + 1) * width, :]) * scale
            return jnp.where(causal, s, NEG)

        def save(step, m, l, acc, block=block):
            for ref, value in zip((m_ref, l_ref, acc_ref), (m, l, acc), strict=True):
                ref[block, :, step * width : (step + 1) * width] = value

        attend_all(heads * half // width, score, v_t, None, save)


def fold_kernel(count, scale, width, stage, *refs):
    come, rot_ref, old, new = refs[:-7], refs[-7], refs[-6:-3], refs[-3:]
    me = lax.axis_index("pb")
    rest = (count // PLANE - 1) * KB

    def run(block):
        masks = [usable(count, block, m) for m in range(PLANE)]
        if stage == 0:
            mine_ref, next_ref, over_ref, side_ref, kv_ref = come
            half = side_ref.shape[0]
            far = slice(0, rest + KB) if block == 1 else slice(rest + KB, 2 * rest + KB)
            side = side_ref[...]
            if block == 1:
                side = jnp.where(me == count - 1, kv_ref[:half], side)
            third = 2 * rest + (2 - block) * KB
            parts = [mine_ref[far], next_ref[far], over_ref[at(1 - block)], next_ref[third : third + KB]]
            parts.append(jnp.where(me % 2 == block, side, next_ref[2 * rest + 3 * KB :]))
            masks = masks[0][1 - block :] + masks[1][1 - block :] + masks[2][:1] + masks[3][:1] + [None] * (half // KB)
        else:
            parts, masks = [come[0][...]], masks[stage][1:]

        def save(step, m, l, acc):
            for ref, value in zip(new, (m, l, acc), strict=True):
                ref[block, :, step * width : (step + 1) * width] = value

        fold(jnp.concatenate(parts, axis=0), masks, scale, width, block, rot_ref, old, save)

    run(1)
    if stage == 0:
        pl.when(me >= 1)(lambda: run(0))


def last_kernel(count, scale, width, third_ref, early2_ref, early3_ref, rot_ref, *refs):
    old, out_ref = refs[:3], refs[3]
    _, z, _ = place(count)
    half = out_ref.shape[0] // 2
    dim = rot_ref.shape[2]

    def finish(block, step, l, acc):
        done = acc / l
        for h in range(width // half):
            head = step * (width // half) + h
            out_ref[block * half : (block + 1) * half, head * dim : (head + 1) * dim] = (
                done[:, h * half : (h + 1) * half].T.astype(out_ref.dtype)
            )

    def add(block):
        masks = usable(count, block, PLANE - 1)[1:]
        kv = third_ref[...]
        if block == 0:
            kv = jnp.concatenate([early2_ref[...], early3_ref[...]], axis=0)
            masks = usable(count, block, 2)[1:] + masks
        fold(kv, masks, scale, width, block, rot_ref, old, lambda step, m, l, acc: finish(block, step, l, acc))

    add(1)
    pl.when(z >= 1)(lambda: add(0))

    @pl.when(z < 1)
    def _():
        for step in range(rot_ref.shape[1] // width):
            cols = slice(step * width, (step + 1) * width)
            finish(0, step, old[1][0, :, cols], old[2][0, :, cols])


def per_device(queries, keys, values, basis, picks):
    rows_dev, dim = keys.shape
    half = rows_dev // 2
    count = lax.axis_size("pb")
    planes = count // PLANE
    wide = queries.shape[1] // dim * half
    width = 2 * half
    scale = dim**-0.5 * math.log2(math.e)
    vmem = pl.BlockSpec(memory_space=pltpu.VMEM)
    params = pltpu.CompilerParams(vmem_limit_bytes=VMEM_BYTES)
    bf16, f32 = jnp.bfloat16, jnp.float32
    shapes = [
        jax.ShapeDtypeStruct((2, 1, wide), f32),
        jax.ShapeDtypeStruct((2, 1, wide), f32),
        jax.ShapeDtypeStruct((2, dim, wide), f32),
    ]

    def rows(n):
        return jax.ShapeDtypeStruct((n * KB, 2 * dim), bf16)

    def permute(value, pairs):
        return lax.ppermute(value, "pb", pairs)

    def cost(keys_each):
        return pl.CostEstimate(
            flops=8 * wide * keys_each * dim, bytes_accessed=4_000_000, transcendentals=2 * wide * keys_each
        )

    per_half = half // KB
    table = jax.ShapeDtypeStruct(((planes - 1) * PLANE * 2, dim), jnp.int32)
    kv, table, own, over, side, *packets = pl.pallas_call(
        functools.partial(pack_kernel, count),
        out_shape=[rows(2 * per_half), table, rows(2), rows(4), rows(per_half)]
        + [rows(PLANE)] * (planes - 1),
        in_specs=[vmem] * 2,
        out_specs=[vmem] * (4 + planes),
        compiler_params=params,
        cost_estimate=pl.CostEstimate(flops=4000000000, bytes_accessed=1_000_000, transcendentals=0),
        name="pack",
    )(picks.T, jnp.concatenate([keys, values]))

    packets = [
        permute(packet, [(s, (s + j * PLANE) % count) for s in range(count)]) for j, packet in enumerate(packets, 1)
    ]

    near = pl.pallas_call(
        functools.partial(near_kernel, scale, width),
        out_shape=[jax.ShapeDtypeStruct((2, wide, dim), bf16)] + shapes,
        in_specs=[vmem] * 3,
        out_specs=[vmem] * 4,
        compiler_params=params,
        cost_estimate=cost(half),
        name="near",
    )(queries, basis, kv)
    packets, near = lax.optimization_barrier((packets, near))
    over = permute(over, [(s, s ^ 2) for s in range(count)])
    groups = lax.axis_size("grp")
    pairs = []
    for g in range(groups):
        pairs += [(g * count + s, g * count + s + (1 if s % 2 else -1)) for s in range(1, count - 1)]
        pairs += [(g * count + s, (g + 1) % groups * count + s) for s in (0, count - 1)]
    side = lax.ppermute(side, ("grp", "pb"), pairs)

    def swap(value, m):
        return permute(value, [(s, s ^ m) for s in range(count)])

    sizes = [2 * planes - 1, 2 * planes + 1 + per_half, planes - 1, planes - 1, planes - 1, planes - 1]
    moved = list(
        pl.pallas_call(
            functools.partial(select_kernel, count),
            out_shape=[rows(size) for size in sizes],
            in_specs=[vmem] * (planes + 3),
            out_specs=[vmem] * len(sizes),
            compiler_params=params,
            name="select",
        )(table, own, over, kv, *packets)
    )
    moved[1], side = lax.optimization_barrier((moved[1], side))
    for m in (1, 2, 3):
        moved[m] = swap(moved[m], m)
    for i in range(PLANE, len(moved)):
        m = PLANE - len(moved) + i
        moved[i] = permute(moved[i], [(s, s ^ (m if s >= PLANE else 1)) for s in range(count)])

    rotated, *state = near

    def folded(state, stage, messages):
        return pl.pallas_call(
            functools.partial(fold_kernel, count, scale, width, stage),
            out_shape=shapes,
            in_specs=[vmem] * (4 + len(messages)),
            out_specs=[vmem] * 3,
            input_output_aliases={1 + len(messages) + i: i for i in range(3)},
            compiler_params=params,
            cost_estimate=cost(half),
            name=f"fold{stage}",
        )(*messages, rotated, *state)

    state = folded(state, 0, [moved[0], moved[1], over, side, kv])
    state = folded(state, 2, [moved[2]])
    return pl.pallas_call(
        functools.partial(last_kernel, count, scale, width),
        out_shape=jax.ShapeDtypeStruct(queries.shape, bf16),
        in_specs=[vmem] * 7,
        out_specs=vmem,
        compiler_params=params,
        cost_estimate=cost(half),
        name="last",
    )(*moved[3:], rotated, *state)


def solution(mesh):
    in_specs = (P("pb", "grp"), P("pb", "grp"), P("pb", "grp"), P("grp", None), P("grp", None))
    out_specs = P("pb", "grp")
    return jax.shard_map(
        per_device, mesh=mesh, in_specs=in_specs, out_specs=out_specs, check_vma=False
    )
```

```python
import functools
import math

import jax
import jax.numpy as jnp
from jax import lax
from jax.experimental import pallas as pl
from jax.experimental.pallas import tpu as pltpu
from jax.sharding import PartitionSpec as P

KB = 32
PLANE = 4
NEG = -1e30
VMEM_BYTES = 40 * 1024 * 1024
CHUNK = 16


def place(count):
    me = lax.axis_index("pb")
    return me, me // PLANE, me % PLANE


def sub(index):
    return pl.ds(pl.multiple_of(index * KB, KB), KB)


def at(n):
    return slice(n * KB, (n + 1) * KB)


def scores_of(k, q):
    return lax.dot_general(k, q, (((1,), (1,)), ((), ())), preferred_element_type=jnp.float32)


def splat(picks_ref, wanted, width):
    lane = lax.broadcasted_iota(jnp.int32, (1, picks_ref.shape[1]), 1)
    rows = [jnp.where(lane == block, picks_ref[pl.ds(source, 1), :], 0) for source, block in wanted]
    total = jnp.sum(jnp.concatenate(rows, axis=0), axis=1, keepdims=True)
    return jnp.broadcast_to(jnp.maximum(total, 0), (len(wanted), width))


def chosen(index, choices):
    index = jnp.broadcast_to(index, choices[0].shape)
    value = choices[0]
    for t, choice in enumerate(choices[1:], 1):
        value = jnp.where(index == t, choice, value)
    return value


def pack_kernel(count, picks_ref, both_ref, *refs):
    planes = count // PLANE
    kv_ref, table_ref, own_ref, over_ref, side_ref, packet_refs = *refs[:5], refs[5:]
    me, z, r = place(count)
    dim = both_ref.shape[1]
    total = both_ref.shape[0] // 2 // KB
    per_half = total // 2
    for part in range(2):
        kv_ref[:, part * dim : (part + 1) * dim] = both_ref[part * total * KB : (part + 1) * total * KB]
    wanted, down = [], []
    for j in range(1, planes):
        up = z + j < planes
        to = jnp.where(up, 0, (z + j - planes) * PLANE)
        wanted += [(me, 2 * count - 1 - (to + t)) for t in range(PLANE)]
        down += [up] * PLANE
    for m in (0, 1):
        wanted.append((me, 2 * count - 1 - (z * PLANE + (r ^ m))))
    for m in (2, 3):
        dest = z * PLANE + (r ^ m)
        wanted += [(me, 2 * count - 1 - dest), (me, dest)]
    index = splat(picks_ref, wanted, dim)
    for part in range(2):
        cols = slice(part * dim, (part + 1) * dim)
        subs = [both_ref[at(part * total + t)] for t in range(total)]
        for g, up in enumerate(down):
            j, t = g // PLANE, g % PLANE
            packet_refs[j][at(t), cols] = jnp.where(up, subs[t], chosen(index[g : g + 1], subs))
        for g in range(6):
            ref, t = (own_ref, g) if g < 2 else (over_ref, g - 2)
            ref[at(t), cols] = chosen(index[len(down) + g : len(down) + g + 1], subs)
        for t in range(per_half):
            side_ref[at(t), cols] = jnp.where(me % 2 == 1, subs[t], subs[per_half + t])
    wanted, fixed = [], []
    for j in range(1, planes):
        up = z >= j
        source = jnp.where(up, z - j, z - j + planes) * PLANE + r
        for m in range(PLANE):
            dest = z * PLANE + (r ^ m)
            wanted += [(source, 2 * count - 1 - dest), (source, dest)]
            fixed += [(up, r ^ m), (up, 0)]
    index = splat(picks_ref, wanted, dim)
    for g, (up, other) in enumerate(fixed):
        table_ref[g : g + 1] = jnp.where(up, index[g : g + 1], other)


def select_kernel(count, table_ref, own_ref, over_ref, kv_ref, *refs):
    planes = count // PLANE
    packet_refs, moved_refs, early_refs = refs[: planes - 1], refs[planes - 1 : planes + 3], refs[planes + 3 :]
    dim = table_ref.shape[1]
    per_half = kv_ref.shape[0] // 2 // KB
    for m in (0, 1):
        moved_refs[m][at(0)] = own_ref[at(m)]
    moved_refs[1][(2 * planes - 1) * KB : (2 * planes + 1) * KB] = over_ref[2 * KB :]
    for t in range(per_half):
        moved_refs[1][at(2 * planes + 1 + t)] = kv_ref[sub(lax.axis_index("pb") % 2 * per_half + t)]
    for j, packet in enumerate(packet_refs, 1):
        for part in (slice(0, dim), slice(dim, 2 * dim)):
            choices = [packet[at(t), part] for t in range(PLANE)]
            for m, ref in enumerate(moved_refs):
                row = ((j - 1) * PLANE + m) * 2
                first = j - (m > 1)
                ref[at(first), part] = chosen(table_ref[row : row + 1], choices)
                early = chosen(table_ref[row + 1 : row + 2], choices)
                if m < 2:
                    ref[at(first + planes - 1), part] = early
                else:
                    early_refs[m - 2][at(first), part] = early


def usable(count, block, m):
    me, z, r = place(count)
    planes = count // PLANE
    if block == 1:
        return [me < count - 1 if m == 0 else None] + [None] * (planes - 1)
    return [(r ^ m) < r - 1] + [(z >= j) & ((z - j) * PLANE + (r ^ m) < me - 1) for j in range(1, planes)]


def attend_all(n_cols, score, v_ts, state, save):
    ahead = score(0)
    for step in range(n_cols):
        s = ahead
        if step + 1 < n_cols:
            ahead = score(step + 1)
        m = jnp.max(s, axis=0, keepdims=True)
        if state is not None:
            m_old, l_old, acc_old = state(step)
            m = jnp.maximum(m, m_old)
        w = jnp.exp2(s - m)
        l = jnp.sum(w, axis=0, keepdims=True)
        acc = jnp.dot(v_ts, w.astype(jnp.bfloat16), preferred_element_type=jnp.float32)
        if state is not None:
            old = jnp.exp2(m_old - m)
            l = l + l_old * old
            acc = acc + acc_old * old
        save(step, m, l, acc)


def fold(kv, masks, scale, width, block, rot_ref, old_refs, save):
    dim = rot_ref.shape[2]
    total = len(masks)
    steps = rot_ref.shape[1] // width
    carried = [tuple(ref[block, :, step * width : (step + 1) * width] for ref in old_refs) for step in range(steps)]
    for first in range(0, total, CHUNK):
        last = min(first + CHUNK, total)
        k = kv[first * KB : last * KB, :dim]
        v_t = kv[first * KB : last * KB, dim:].T

        def score(step, k=k, first=first, last=last):
            s = scores_of(k, rot_ref[block, step * width : (step + 1) * width, :]) * scale
            if all(ok is None for ok in masks[first:last]):
                return s
            return jnp.concatenate(
                [s[at(g - first)] if masks[g] is None else jnp.where(masks[g], s[at(g - first)], NEG) for g in range(first, last)]
            )

        def keep(step, *values):
            carried[step] = values

        attend_all(steps, score, v_t, carried.__getitem__, save if last == total else keep)


def near_kernel(scale, width, q_ref, basis_ref, kv_ref, rot_ref, m_ref, l_ref, acc_ref):
    dim = basis_ref.shape[0]
    half = q_ref.shape[0] // 2
    heads = q_ref.shape[1] // dim
    basis = basis_ref[...]
    key_row = lax.broadcasted_iota(jnp.int32, (half, width), 0)
    query = lax.broadcasted_iota(jnp.int32, (half, width), 1) % half
    causal = key_row <= query
    for block in range(2):
        rows = slice(block * half, (block + 1) * half)
        for h in range(heads):
            q = jnp.dot(q_ref[rows, h * dim : (h + 1) * dim], basis, preferred_element_type=jnp.float32)
            rot_ref[block, h * half : (h + 1) * half, :] = q.astype(jnp.bfloat16)
    for block in range(2):
        rows = slice(block * half, (block + 1) * half)
        k, v_t = kv_ref[rows, :dim], kv_ref[rows, dim:].T

        def score(step, block=block, k=k):
            s = scores_of(k, rot_ref[block, step * width : (step + 1) * width, :]) * scale
            return jnp.where(causal, s, NEG)

        def save(step, m, l, acc, block=block):
            for ref, value in zip((m_ref, l_ref, acc_ref), (m, l, acc), strict=True):
                ref[block, :, step * width : (step + 1) * width] = value

        attend_all(heads * half // width, score, v_t, None, save)


def fold_kernel(count, scale, width, stage, *refs):
    come, rot_ref, old, new = refs[:-7], refs[-7], refs[-6:-3], refs[-3:]
    me, z, _ = place(count)
    rest = (count // PLANE - 1) * KB

    def run(block):
        masks = [usable(count, block, m) for m in range(PLANE)]
        if stage == 0:
            mine_ref, next_ref, over_ref, side_ref, kv_ref = come
            half = side_ref.shape[0]
            far = slice(0, rest + KB) if block == 1 else slice(rest + KB, 2 * rest + KB)
            side = side_ref[...]
            if block == 1:
                side = jnp.where(me == count - 1, kv_ref[:half], side)
            third = 2 * rest + (2 - block) * KB
            parts = [mine_ref[far], next_ref[far], over_ref[at(1 - block)], next_ref[third : third + KB]]
            parts.append(jnp.where(me % 2 == block, side, next_ref[2 * rest + 3 * KB :]))
            masks = masks[0][1 - block :] + masks[1][1 - block :] + masks[2][:1] + masks[3][:1] + [None] * (half // KB)
        else:
            parts, masks = [come[0][...]], masks[stage][1:]

        def save(step, m, l, acc):
            for ref, value in zip(new, (m, l, acc), strict=True):
                ref[block, :, step * width : (step + 1) * width] = value

        fold(jnp.concatenate(parts, axis=0), masks, scale, width, block, rot_ref, old, save)

    if stage < 3:
        run(1)
    if stage == 0:
        pl.when(me >= 1)(lambda: run(0))
    if stage == 3:
        pl.when(z >= 1)(lambda: run(1))


def last_kernel(count, scale, width, third_ref, second_early_ref, third_early_ref, rot_ref, *refs):
    old, out_ref, done_ref, sems = refs[:3], refs[3], refs[4], refs[5]
    _, z, _ = place(count)
    half = out_ref.shape[0] // 2
    dim = rot_ref.shape[2]

    def piece(block, step):
        rows, cols = pl.ds(block * half, half), pl.ds(step * (width // half) * dim, width // half * dim)
        return pltpu.make_async_copy(done_ref.at[rows, cols], out_ref.at[rows, cols], sems.at[block, step])

    def finish(block, step, l, acc):
        done = acc / l
        for h in range(width // half):
            head = step * (width // half) + h
            done_ref[block * half : (block + 1) * half, head * dim : (head + 1) * dim] = (
                done[:, h * half : (h + 1) * half].T.astype(done_ref.dtype)
            )
        piece(block, step).start()

    def add(block):
        kv, masks = third_ref[...], usable(count, block, PLANE - 1)[1:]
        if block == 0:
            kv = jnp.concatenate([second_early_ref[...], third_early_ref[...]], axis=0)
            masks = usable(count, block, 2)[1:] + masks
        fold(kv, masks, scale, width, block, rot_ref, old, lambda step, m, l, acc: finish(block, step, l, acc))

    def close(block):
        for step in range(rot_ref.shape[1] // width):
            cols = slice(step * width, (step + 1) * width)
            finish(block, step, old[1][block, :, cols], old[2][block, :, cols])

    @pl.when(z >= 1)
    def _():
        close(1)
        add(0)

    @pl.when(z < 1)
    def _():
        close(0)
        add(1)

    for block in range(2):
        for step in range(rot_ref.shape[1] // width):
            piece(block, step).wait()


def per_device(queries, keys, values, basis, picks):
    rows_dev, dim = keys.shape
    half = rows_dev // 2
    count = lax.axis_size("pb")
    planes = count // PLANE
    wide = queries.shape[1] // dim * half
    width = 4 * half
    scale = dim**-0.5 * math.log2(math.e)
    vmem = pl.BlockSpec(memory_space=pltpu.VMEM)
    params = pltpu.CompilerParams(vmem_limit_bytes=VMEM_BYTES)
    bf16, f32 = jnp.bfloat16, jnp.float32
    shapes = [
        jax.ShapeDtypeStruct((2, 1, wide), f32),
        jax.ShapeDtypeStruct((2, 1, wide), f32),
        jax.ShapeDtypeStruct((2, dim, wide), f32),
    ]

    def rows(n):
        return jax.ShapeDtypeStruct((n * KB, 2 * dim), bf16)

    def permute(value, pairs):
        return lax.ppermute(value, "pb", pairs)

    def cost(keys_each):
        return pl.CostEstimate(
            flops=8 * wide * keys_each * dim, bytes_accessed=4_000_000, transcendentals=2 * wide * keys_each
        )

    per_half = half // KB
    table = jax.ShapeDtypeStruct(((planes - 1) * PLANE * 2, dim), jnp.int32)
    kv, table, own, over, side, *packets = pl.pallas_call(
        functools.partial(pack_kernel, count),
        out_shape=[rows(2 * per_half), table, rows(2), rows(4), rows(per_half)]
        + [rows(PLANE)] * (planes - 1),
        in_specs=[vmem] * 2,
        out_specs=[vmem] * (4 + planes),
        compiler_params=params,
        cost_estimate=pl.CostEstimate(flops=4000000000, bytes_accessed=1_000_000, transcendentals=0),
        name="pack",
    )(picks.T, jnp.concatenate([keys, values]))

    packets = [
        permute(packet, [(s, (s + j * PLANE) % count) for s in range(count)]) for j, packet in enumerate(packets, 1)
    ]

    near = pl.pallas_call(
        functools.partial(near_kernel, scale, width),
        out_shape=[jax.ShapeDtypeStruct((2, wide, dim), bf16)] + shapes,
        in_specs=[vmem] * 3,
        out_specs=[vmem] * 4,
        compiler_params=params,
        cost_estimate=cost(half),
        name="near",
    )(queries, basis, kv)
    packets, near = lax.optimization_barrier((packets, near))
    over = permute(over, [(s, s ^ 2) for s in range(count)])
    groups = lax.axis_size("grp")
    pairs = []
    for g in range(groups):
        pairs += [(g * count + s, g * count + s + (1 if s % 2 else -1)) for s in range(1, count - 1)]
        pairs += [(g * count + s, (g + 1) % groups * count + s) for s in (0, count - 1)]
    side = lax.ppermute(side, ("grp", "pb"), pairs)

    def swap(value, m):
        return permute(value, [(s, s ^ m) for s in range(count)])

    sizes = [2 * planes - 1, 2 * planes + 1 + per_half, planes - 1, planes - 1, planes - 1, planes - 1]
    moved = list(
        pl.pallas_call(
            functools.partial(select_kernel, count),
            out_shape=[rows(size) for size in sizes],
            in_specs=[vmem] * (planes + 3),
            out_specs=[vmem] * len(sizes),
            compiler_params=params,
            name="select",
        )(table, own, over, kv, *packets)
    )
    moved[1], side = lax.optimization_barrier((moved[1], side))
    for m in (1, 2, 3):
        moved[m] = swap(moved[m], m)
    for i in range(PLANE, len(moved)):
        m = PLANE - len(moved) + i
        moved[i] = permute(moved[i], [(s, s ^ (m if s >= PLANE else 1)) for s in range(count)])

    rotated, *state = near

    def folded(state, stage, messages):
        return pl.pallas_call(
            functools.partial(fold_kernel, count, scale, width, stage),
            out_shape=shapes,
            in_specs=[vmem] * (4 + len(messages)),
            out_specs=[vmem] * 3,
            input_output_aliases={1 + len(messages) + i: i for i in range(3)},
            compiler_params=params,
            cost_estimate=cost(half),
            name=f"fold{stage}",
        )(*messages, rotated, *state)

    state = folded(state, 0, [moved[0], moved[1], over, side, kv])
    state = folded(state, 2, [moved[2]])
    state = folded(state, 3, [moved[3]])
    return pl.pallas_call(
        functools.partial(last_kernel, count, scale, width),
        out_shape=jax.ShapeDtypeStruct(queries.shape, bf16),
        in_specs=[vmem] * 7,
        out_specs=pl.BlockSpec(memory_space=pl.ANY),
        scratch_shapes=[pltpu.VMEM(queries.shape, bf16), pltpu.SemaphoreType.DMA((2, wide // width))],
        compiler_params=params,
        cost_estimate=cost(half),
        name="last",
    )(*moved[3:], rotated, *state)


def solution(mesh):
    in_specs = (P("pb", "grp"), P("pb", "grp"), P("pb", "grp"), P("grp", None), P("grp", None))
    out_specs = P("pb", "grp")
    return jax.shard_map(
        per_device, mesh=mesh, in_specs=in_specs, out_specs=out_specs, check_vma=False
    )
```

```python
import functools
import math

import jax
import jax.numpy as jnp
from jax import lax
from jax.experimental import pallas as pl
from jax.experimental.pallas import tpu as pltpu
from jax.sharding import PartitionSpec as P

KB = 32
PLANE = 4
NEG = -1e30
VMEM_BYTES = 40 * 1024 * 1024
CHUNK = 16


def place(count):
    me = lax.axis_index("pb")
    return me, me // PLANE, me % PLANE


def sub(index):
    return pl.ds(pl.multiple_of(index * KB, KB), KB)


def at(n):
    return slice(n * KB, (n + 1) * KB)


def scores_of(k, q):
    return lax.dot_general(k, q, (((1,), (1,)), ((), ())), preferred_element_type=jnp.float32)


def splat(picks_ref, wanted, width):
    lane = lax.broadcasted_iota(jnp.int32, (1, picks_ref.shape[1]), 1)
    rows = [jnp.where(lane == block, picks_ref[pl.ds(source, 1), :], 0) for source, block in wanted]
    total = jnp.sum(jnp.concatenate(rows, axis=0), axis=1, keepdims=True)
    return jnp.broadcast_to(jnp.maximum(total, 0), (len(wanted), width))


def chosen(index, choices):
    index = jnp.broadcast_to(index, choices[0].shape)
    value = choices[0]
    for t, choice in enumerate(choices[1:], 1):
        value = jnp.where(index == t, choice, value)
    return value


def index_kernel(count, picks_ref, out_ref, table_ref):
    planes = count // PLANE
    me, z, r = place(count)
    dim = out_ref.shape[1]
    wanted, up_of = [], []
    for j in range(1, planes):
        up = z + j < planes
        to = jnp.where(up, 0, (z + j - planes) * PLANE)
        wanted += [(me, 2 * count - 1 - (to + t)) for t in range(PLANE)]
        up_of += [(up, t) for t in range(PLANE)]
    for m in (0, 1):
        wanted.append((me, 2 * count - 1 - (z * PLANE + (r ^ m))))
    for m in (2, 3):
        dest = z * PLANE + (r ^ m)
        wanted += [(me, 2 * count - 1 - dest), (me, dest)]
    index = splat(picks_ref, wanted, dim)
    for g in range(len(wanted)):
        row = index[g : g + 1]
        out_ref[g : g + 1] = jnp.where(up_of[g][0], up_of[g][1], row) if g < len(up_of) else row
    wanted, fixed = [], []
    for j in range(1, planes):
        up = z >= j
        source = jnp.where(up, z - j, z - j + planes) * PLANE + r
        for m in range(PLANE):
            dest = z * PLANE + (r ^ m)
            wanted += [(source, 2 * count - 1 - dest), (source, dest)]
            fixed += [(up, r ^ m), (up, 0)]
    index = splat(picks_ref, wanted, dim)
    for g, (up, other) in enumerate(fixed):
        table_ref[g : g + 1] = jnp.where(up, index[g : g + 1], other)


def halves(both_ref):
    dim = both_ref.shape[1]
    total = both_ref.shape[0] // 2 // KB
    for part in range(2):
        yield slice(part * dim, (part + 1) * dim), [both_ref[at(part * total + t)] for t in range(total)]


def pack_kernel(index_ref, both_ref, *packet_refs):
    for cols, subs in halves(both_ref):
        for g in range(len(packet_refs) * PLANE):
            packet_refs[g // PLANE][at(g % PLANE), cols] = chosen(index_ref[g : g + 1], subs)


def pack_own_kernel(first, index_ref, both_ref, kv_ref, own_ref, beside_ref, over_ref, side_ref):
    odd = lax.axis_index("pb") % 2 == 1
    for cols, subs in halves(both_ref):
        for t, value in enumerate(subs):
            kv_ref[at(t), cols] = value
        per_half = len(subs) // 2
        for g in range(6):
            ref, t = ((own_ref, 0), (beside_ref, per_half))[g] if g < 2 else (over_ref, g - 2)
            ref[at(t), cols] = chosen(index_ref[first + g : first + g + 1], subs)
        for t in range(per_half):
            side_ref[at(t), cols] = jnp.where(odd, subs[t], subs[per_half + t])
            beside_ref[at(t), cols] = jnp.where(odd, subs[per_half + t], subs[t])


def select_kernel(count, table_ref, own_ref, *refs):
    planes = count // PLANE
    packet_refs, moved_refs = refs[: planes - 1], refs[planes - 1 :]
    dim = table_ref.shape[1]
    moved_refs[0][at(0)] = own_ref[...]
    for j, packet in enumerate(packet_refs, 1):
        for part in (slice(0, dim), slice(dim, 2 * dim)):
            choices = [packet[at(t), part] for t in range(PLANE)]
            for m, ref in enumerate(moved_refs):
                row = ((j - 1) * PLANE + m) * 2
                first = j - (m > 0)
                ref[at(first), part] = chosen(table_ref[row : row + 1], choices)
                ref[at(first + planes - 1), part] = chosen(table_ref[row + 1 : row + 2], choices)


def usable(count, block, m):
    me, z, r = place(count)
    planes = count // PLANE
    if block == 1:
        return [me < count - 1 if m == 0 else None] + [None] * (planes - 1)
    return [(r ^ m) < r - 1] + [(z >= j) & ((z - j) * PLANE + (r ^ m) < me - 1) for j in range(1, planes)]


def attend_all(n_cols, score, v_ts, state, save):
    ahead = score(0)
    for step in range(n_cols):
        s = ahead
        if step + 1 < n_cols:
            ahead = score(step + 1)
        m = jnp.max(s, axis=0, keepdims=True)
        if state is not None:
            m_old, l_old, acc_old = state(step)
            m = jnp.maximum(m, m_old)
        w = jnp.exp2(s - m)
        l = jnp.sum(w, axis=0, keepdims=True)
        acc = jnp.dot(v_ts, w.astype(jnp.bfloat16), preferred_element_type=jnp.float32)
        if state is not None:
            old = jnp.exp2(m_old - m)
            l = l + l_old * old
            acc = acc + acc_old * old
        save(step, m, l, acc)


def fold(kv, masks, scale, width, block, rot_ref, old_refs, save):
    dim = rot_ref.shape[2]
    total = len(masks)
    steps = rot_ref.shape[1] // width
    carried = [tuple(ref[block, :, step * width : (step + 1) * width] for ref in old_refs) for step in range(steps)]
    for first in range(0, total, CHUNK):
        last = min(first + CHUNK, total)
        k = kv[first * KB : last * KB, :dim]
        v_t = kv[first * KB : last * KB, dim:].T

        def score(step, k=k, first=first, last=last):
            s = scores_of(k, rot_ref[block, step * width : (step + 1) * width, :]) * scale
            if all(ok is None for ok in masks[first:last]):
                return s
            return jnp.concatenate(
                [s[at(g - first)] if masks[g] is None else jnp.where(masks[g], s[at(g - first)], NEG) for g in range(first, last)]
            )

        def keep(step, *values):
            carried[step] = values

        attend_all(steps, score, v_t, carried.__getitem__, save if last == total else keep)


def near_kernel(scale, width, q_ref, basis_ref, kv_ref, rot_ref, m_ref, l_ref, acc_ref):
    dim = basis_ref.shape[0]
    half = q_ref.shape[0] // 2
    heads = q_ref.shape[1] // dim
    basis = basis_ref[...]
    key_row = lax.broadcasted_iota(jnp.int32, (half, width), 0)
    query = lax.broadcasted_iota(jnp.int32, (half, width), 1) % half
    causal = key_row <= query
    for block in range(2):
        rows = slice(block * half, (block + 1) * half)
        for h in range(heads):
            q = jnp.dot(q_ref[rows, h * dim : (h + 1) * dim], basis, preferred_element_type=jnp.float32)
            rot_ref[block, h * half : (h + 1) * half, :] = q.astype(jnp.bfloat16)
    for block in range(2):
        rows = slice(block * half, (block + 1) * half)
        k, v_t = kv_ref[rows, :dim], kv_ref[rows, dim:].T

        def score(step, block=block, k=k):
            s = scores_of(k, rot_ref[block, step * width : (step + 1) * width, :]) * scale
            return jnp.where(causal, s, NEG)

        def save(step, m, l, acc, block=block):
            for ref, value in zip((m_ref, l_ref, acc_ref), (m, l, acc), strict=True):
                ref[block, :, step * width : (step + 1) * width] = value

        attend_all(heads * half // width, score, v_t, None, save)


def fold_kernel(count, scale, width, stage, *refs):
    come, rot_ref, old, new = refs[:-7], refs[-7], refs[-6:-3], refs[-3:]
    me, z, _ = place(count)
    rest = (count // PLANE - 1) * KB

    def run(block):
        masks = [usable(count, block, m) for m in range(PLANE)]
        if stage == 0:
            mine_ref, next_ref, beside_ref, over_ref, passed_ref, side_ref, kv_ref = come
            half = kv_ref.shape[0] // 2
            far = slice(0, rest + KB) if block == 1 else slice(rest + KB, 2 * rest + KB)
            side = side_ref[:half]
            if block == 1:
                side = jnp.where(me == count - 1, kv_ref[:half], side)
            near = slice(0, rest) if block == 1 else slice(rest, 2 * rest)
            parts = [mine_ref[far], next_ref[near], over_ref[at(1 - block)], passed_ref[at(1 - block)]]
            masks = masks[0][1 - block :] + masks[1][1:] + masks[2][:1] + masks[3][:1]
            if block == 1:
                parts.append(beside_ref[half:])
                masks.append(None)
            parts.append(jnp.where(me % 2 == block, side, beside_ref[:half]))
            masks += [None] * (half // KB)
        else:
            parts, masks = [come[0][(1 - block) * rest : (2 - block) * rest]], masks[stage][1:]

        def save(step, m, l, acc):
            for ref, value in zip(new, (m, l, acc), strict=True):
                ref[block, :, step * width : (step + 1) * width] = value

        fold(jnp.concatenate(parts, axis=0), masks, scale, width, block, rot_ref, old, save)

    run(1)
    pl.when(me >= 1 if stage == 0 else z >= 1)(lambda: run(0))


def last_kernel(count, scale, width, third_ref, rot_ref, *refs):
    old, out_ref, done_ref, sems = refs[:3], refs[3], refs[4], refs[5]
    _, z, _ = place(count)
    half = out_ref.shape[0] // 2
    dim = rot_ref.shape[2]

    def piece(block, step):
        rows, cols = pl.ds(block * half, half), pl.ds(step * (width // half) * dim, width // half * dim)
        return pltpu.make_async_copy(done_ref.at[rows, cols], out_ref.at[rows, cols], sems.at[block, step])

    def finish(block, step, l, acc):
        done = acc / l
        for h in range(width // half):
            head = step * (width // half) + h
            done_ref[block * half : (block + 1) * half, head * dim : (head + 1) * dim] = (
                done[:, h * half : (h + 1) * half].T.astype(done_ref.dtype)
            )
        piece(block, step).start()

    def add(block):
        rest = third_ref.shape[0] // 2
        kv, masks = third_ref[(1 - block) * rest : (2 - block) * rest], usable(count, block, PLANE - 1)[1:]
        fold(kv, masks, scale, width, block, rot_ref, old, lambda step, m, l, acc: finish(block, step, l, acc))

    @pl.when(z < 1)
    def _():
        for step in range(rot_ref.shape[1] // width):
            cols = slice(step * width, (step + 1) * width)
            finish(0, step, old[1][0, :, cols], old[2][0, :, cols])

    add(1)
    pl.when(z >= 1)(lambda: add(0))

    for block in range(2):
        for step in range(rot_ref.shape[1] // width):
            piece(block, step).wait()


def per_device(queries, keys, values, basis, picks):
    rows_dev, dim = keys.shape
    half = rows_dev // 2
    count = lax.axis_size("pb")
    planes = count // PLANE
    wide = queries.shape[1] // dim * half
    width = 4 * half
    scale = dim**-0.5 * math.log2(math.e)
    vmem = pl.BlockSpec(memory_space=pltpu.VMEM)
    params = pltpu.CompilerParams(vmem_limit_bytes=VMEM_BYTES)
    bf16, f32 = jnp.bfloat16, jnp.float32
    shapes = [
        jax.ShapeDtypeStruct((2, 1, wide), f32),
        jax.ShapeDtypeStruct((2, 1, wide), f32),
        jax.ShapeDtypeStruct((2, dim, wide), f32),
    ]

    def rows(n):
        return jax.ShapeDtypeStruct((n * KB, 2 * dim), bf16)

    def permute(value, pairs):
        return lax.ppermute(value, "pb", pairs)

    def cost(keys_each):
        return pl.CostEstimate(
            flops=8 * wide * keys_each * dim, bytes_accessed=4_000_000, transcendentals=2 * wide * keys_each
        )

    per_half = half // KB
    z_rows = (planes - 1) * PLANE
    both, by_source = lax.optimization_barrier((jnp.concatenate([keys, values]), picks.T))
    index, table = pl.pallas_call(
        functools.partial(index_kernel, count),
        out_shape=[jax.ShapeDtypeStruct((n, dim), jnp.int32) for n in (z_rows + 6, 2 * z_rows)],
        in_specs=[vmem],
        out_specs=[vmem] * 2,
        compiler_params=params,
        cost_estimate=pl.CostEstimate(flops=4_000_000_000, bytes_accessed=1_000_000, transcendentals=0),
        name="index",
    )(by_source)
    packets = pl.pallas_call(
        pack_kernel,
        out_shape=[rows(PLANE)] * (planes - 1),
        in_specs=[vmem] * 2,
        out_specs=[vmem] * (planes - 1),
        compiler_params=params,
        cost_estimate=pl.CostEstimate(flops=4_000_000_000, bytes_accessed=1_000_000, transcendentals=0),
        name="pack",
    )(index, both)
    kv, own, beside, over, side = pl.pallas_call(
        functools.partial(pack_own_kernel, z_rows),
        out_shape=[rows(2 * per_half), rows(1), rows(per_half + 1), rows(4 + 0), rows(per_half + 0)],
        in_specs=[vmem] * 2,
        out_specs=[vmem] * 5,
        compiler_params=params,
        name="pack_own",
    )(index, both)

    packets = [
        permute(packet, [(s, (s + j * PLANE) % count) for s in range(count)]) for j, packet in enumerate(packets, 1)
    ]

    near = pl.pallas_call(
        functools.partial(near_kernel, scale, width),
        out_shape=[jax.ShapeDtypeStruct((2, wide, dim), bf16)] + shapes,
        in_specs=[vmem] * 3,
        out_specs=[vmem] * 4,
        compiler_params=params,
        cost_estimate=cost(half),
        name="near",
    )(queries, basis, kv)
    packets, near = lax.optimization_barrier((packets, near))
    over = permute(over, [(s, s ^ 2) for s in range(count)])
    groups = lax.axis_size("grp")
    pairs = []
    for g in range(groups):
        pairs += [(g * count + s, g * count + s + (1 if s % 2 else -1)) for s in range(1, count - 1)]
        pairs += [(g * count + s, (g + 1) % groups * count + s) for s in (0, count - 1)]
    side = lax.ppermute(side, ("grp", "pb"), pairs)

    def swap(value, m):
        return permute(value, [(s, s ^ m) for s in range(count)])

    sizes = [2 * planes - 1, 2 * planes - 2, 2 * planes - 2, 2 * planes - 2]
    moved = list(
        pl.pallas_call(
            functools.partial(select_kernel, count),
            out_shape=[rows(size) for size in sizes],
            in_specs=[vmem] * (planes + 1),
            out_specs=[vmem] * len(sizes),
            compiler_params=params,
            name="select",
        )(table, own, *packets)
    )
    for m in (1, 2, 3):
        moved[m] = swap(moved[m], m)
    beside, passed = swap(beside, 1), swap(over[2 * KB : 4 * KB], 1)

    rotated, *state = near

    def folded(state, stage, messages):
        return pl.pallas_call(
            functools.partial(fold_kernel, count, scale, width, stage),
            out_shape=shapes,
            in_specs=[vmem] * (4 + len(messages)),
            out_specs=[vmem] * 3,
            input_output_aliases={1 + len(messages) + i: i for i in range(3)},
            compiler_params=params,
            cost_estimate=cost(half),
            name=f"fold{stage}",
        )(*messages, rotated, *state)

    state = folded(state, 0, [moved[0], moved[1], beside, over, passed, side, kv])
    state = folded(state, 2, [moved[2]])
    return pl.pallas_call(
        functools.partial(last_kernel, count, scale, width),
        out_shape=jax.ShapeDtypeStruct(queries.shape, bf16),
        in_specs=[vmem] * 5,
        out_specs=pl.BlockSpec(memory_space=pl.ANY),
        scratch_shapes=[pltpu.VMEM(queries.shape, bf16), pltpu.SemaphoreType.DMA((2, wide // width))],
        compiler_params=params,
        cost_estimate=cost(half),
        name="last",
    )(moved[3], rotated, *state)


def solution(mesh):
    in_specs = (P("pb", "grp"), P("pb", "grp"), P("pb", "grp"), P("grp", None), P("grp", None))
    out_specs = P("pb", "grp")
    return jax.shard_map(
        per_device, mesh=mesh, in_specs=in_specs, out_specs=out_specs, check_vma=False
    )
```

```python
import functools
import math

import jax
import jax.numpy as jnp
from jax import lax
from jax.experimental import pallas as pl
from jax.experimental.pallas import tpu as pltpu
from jax.sharding import PartitionSpec as P

KB = 32
PLANE = 4
NEG = -1e30
VMEM_BYTES = 40 * 1024 * 1024
CHUNK = 16


def place(count):
    me = lax.axis_index("pb")
    return me, me // PLANE, me % PLANE


def sub(index):
    return pl.ds(pl.multiple_of(index * KB, KB), KB)


def at(n):
    return slice(n * KB, (n + 1) * KB)


def scores_of(k, q):
    return lax.dot_general(k, q, (((1,), (1,)), ((), ())), preferred_element_type=jnp.float32)


def splat(picks_ref, wanted, width):
    lane = lax.broadcasted_iota(jnp.int32, (1, picks_ref.shape[1]), 1)
    rows = [jnp.where(lane == block, picks_ref[pl.ds(source, 1), :], 0) for source, block in wanted]
    total = jnp.sum(jnp.concatenate(rows, axis=0), axis=1, keepdims=True)
    return jnp.broadcast_to(jnp.maximum(total, 0), (len(wanted), width))


def chosen(index, choices):
    index = jnp.broadcast_to(index, choices[0].shape)
    value = choices[0]
    for t, choice in enumerate(choices[1:], 1):
        value = jnp.where(index == t, choice, value)
    return value


def index_kernel(count, picks_ref, out_ref, table_ref):
    planes = count // PLANE
    me, z, r = place(count)
    dim = out_ref.shape[1]
    wanted, up_of = [], []
    for j in range(1, planes):
        up = z + j < planes
        to = jnp.where(up, 0, (z + j - planes) * PLANE)
        wanted += [(me, 2 * count - 1 - (to + t)) for t in range(PLANE)]
        up_of += [(up, t) for t in range(PLANE)]
    for m in (0, 1):
        wanted.append((me, 2 * count - 1 - (z * PLANE + (r ^ m))))
    for m in (2, 3):
        dest = z * PLANE + (r ^ m)
        wanted += [(me, 2 * count - 1 - dest), (me, dest)]
    index = splat(picks_ref, wanted, dim)
    for g in range(len(wanted)):
        row = index[g : g + 1]
        out_ref[g : g + 1] = jnp.where(up_of[g][0], up_of[g][1], row) if g < len(up_of) else row
    wanted, fixed = [], []
    for j in range(1, planes):
        up = z >= j
        source = jnp.where(up, z - j, z - j + planes) * PLANE + r
        for m in range(PLANE):
            dest = z * PLANE + (r ^ m)
            wanted += [(source, 2 * count - 1 - dest), (source, dest)]
            fixed += [(up, r ^ m), (up, 0)]
    index = splat(picks_ref, wanted, dim)
    for g, (up, other) in enumerate(fixed):
        table_ref[g : g + 1] = jnp.where(up, index[g : g + 1], other)


def halves(both_ref):
    dim = both_ref.shape[1]
    total = both_ref.shape[0] // 2 // KB
    for part in range(2):
        yield slice(part * dim, (part + 1) * dim), [both_ref[at(part * total + t)] for t in range(total)]


def pack_kernel(index_ref, both_ref, *packet_refs):
    for cols, subs in halves(both_ref):
        for g in range(len(packet_refs) * PLANE):
            packet_refs[g // PLANE][at(g % PLANE), cols] = chosen(index_ref[g : g + 1], subs)


def pack_own_kernel(first, index_ref, both_ref, kv_ref, own_ref, beside_ref, over_ref, side_ref):
    odd = lax.axis_index("pb") % 2 == 1
    for cols, subs in halves(both_ref):
        for t, value in enumerate(subs):
            kv_ref[at(t), cols] = value
        per_half = len(subs) // 2
        for g in range(6):
            ref, t = ((own_ref, 0), (beside_ref, per_half))[g] if g < 2 else (over_ref, g - 2)
            ref[at(t), cols] = chosen(index_ref[first + g : first + g + 1], subs)
        for t in range(per_half):
            side_ref[at(t), cols] = jnp.where(odd, subs[t], subs[per_half + t])
            beside_ref[at(t), cols] = jnp.where(odd, subs[per_half + t], subs[t])


def select_kernel(count, table_ref, own_ref, *refs):
    planes = count // PLANE
    packet_refs, moved_refs = refs[: planes - 1], refs[planes - 1 :]
    dim = table_ref.shape[1]
    moved_refs[0][at(0)] = own_ref[...]
    for j, packet in enumerate(packet_refs, 1):
        for part in (slice(0, dim), slice(dim, 2 * dim)):
            choices = [packet[at(t), part] for t in range(PLANE)]
            for m, ref in enumerate(moved_refs):
                row = ((j - 1) * PLANE + m) * 2
                first = j - (m > 0)
                ref[at(first), part] = chosen(table_ref[row : row + 1], choices)
                ref[at(first + planes - 1), part] = chosen(table_ref[row + 1 : row + 2], choices)


def usable(count, block, m):
    me, z, r = place(count)
    planes = count // PLANE
    if block == 1:
        return [me < count - 1 if m == 0 else None] + [None] * (planes - 1)
    return [(r ^ m) < r - 1] + [(z >= j) & ((z - j) * PLANE + (r ^ m) < me - 1) for j in range(1, planes)]


def attend_all(n_cols, score, v_ts, state, save):
    ahead = score(0)
    for step in range(n_cols):
        s = ahead
        if step + 1 < n_cols:
            ahead = score(step + 1)
        m = jnp.max(s, axis=0, keepdims=True)
        if state is not None:
            m_old, l_old, acc_old = state(step)
            m = jnp.maximum(m, m_old)
        w = jnp.exp2(s - m)
        l = jnp.sum(w, axis=0, keepdims=True)
        acc = jnp.dot(v_ts, w.astype(jnp.bfloat16), preferred_element_type=jnp.float32)
        if state is not None:
            old = jnp.exp2(m_old - m)
            l = l + l_old * old
            acc = acc + acc_old * old
        save(step, m, l, acc)


def fold(kv, masks, scale, width, block, rot_ref, old_refs, save):
    dim = rot_ref.shape[2]
    total = len(masks)
    steps = rot_ref.shape[1] // width
    carried = [tuple(ref[block, :, step * width : (step + 1) * width] for ref in old_refs) for step in range(steps)]
    for first in range(0, total, CHUNK):
        last = min(first + CHUNK, total)
        k = kv[first * KB : last * KB, :dim]
        v_t = kv[first * KB : last * KB, dim:].T

        def score(step, k=k, first=first, last=last):
            s = scores_of(k, rot_ref[block, step * width : (step + 1) * width, :]) * scale
            if all(ok is None for ok in masks[first:last]):
                return s
            return jnp.concatenate(
                [s[at(g - first)] if masks[g] is None else jnp.where(masks[g], s[at(g - first)], NEG) for g in range(first, last)]
            )

        def keep(step, *values):
            carried[step] = values

        attend_all(steps, score, v_t, carried.__getitem__, save if last == total else keep)


def rotate_kernel(q_ref, basis_ref, rot_ref):
    dim = basis_ref.shape[0]
    half = q_ref.shape[0] // 2
    basis = basis_ref[...]
    for block in range(2):
        for h in range(q_ref.shape[1] // dim):
            q = q_ref[block * half : (block + 1) * half, h * dim : (h + 1) * dim]
            q = jnp.dot(q, basis, preferred_element_type=jnp.float32)
            rot_ref[block, h * half : (h + 1) * half, :] = q.astype(rot_ref.dtype)


def near_kernel(scale, width, kv_ref, rot_ref, *state_refs):
    dim = rot_ref.shape[2]
    half = kv_ref.shape[0] // 2
    key_row = lax.broadcasted_iota(jnp.int32, (half, width), 0)
    query = lax.broadcasted_iota(jnp.int32, (half, width), 1) % half
    causal = key_row <= query
    for block in range(2):
        rows = slice(block * half, (block + 1) * half)
        k, v_t = kv_ref[rows, :dim], kv_ref[rows, dim:].T

        def score(step, block=block, k=k):
            s = scores_of(k, rot_ref[block, step * width : (step + 1) * width, :]) * scale
            return jnp.where(causal, s, NEG)

        def save(step, m, l, acc, block=block):
            for ref, value in zip(state_refs, (m, l, acc), strict=True):
                ref[block, :, step * width : (step + 1) * width] = value

        attend_all(rot_ref.shape[1] // width, score, v_t, None, save)


def fold_kernel(count, scale, width, stage, *refs):
    come, rot_ref, old, new = refs[:-7], refs[-7], refs[-6:-3], refs[-3:]
    me, z, _ = place(count)
    rest = (count // PLANE - 1) * KB

    def run(block):
        masks = [usable(count, block, m) for m in range(PLANE)]
        if stage == 0:
            mine_ref, next_ref, beside_ref, over_ref, passed_ref, side_ref, kv_ref = come
            half = kv_ref.shape[0] // 2
            far = slice(0, rest + KB) if block == 1 else slice(rest + KB, 2 * rest + KB)
            side = side_ref[:half]
            if block == 1:
                side = jnp.where(me == count - 1, kv_ref[:half], side)
            near = slice(0, rest) if block == 1 else slice(rest, 2 * rest)
            parts = [mine_ref[far], next_ref[near], over_ref[at(1 - block)], passed_ref[at(1 - block)]]
            masks = masks[0][1 - block :] + masks[1][1:] + masks[2][:1] + masks[3][:1]
            if block == 1:
                parts.append(beside_ref[half:])
                masks.append(None)
            parts.append(jnp.where(me % 2 == block, side, beside_ref[:half]))
            masks += [None] * (half // KB)
        else:
            parts, masks = [come[0][(1 - block) * rest : (2 - block) * rest]], masks[stage][1:]

        def save(step, m, l, acc):
            for ref, value in zip(new, (m, l, acc), strict=True):
                ref[block, :, step * width : (step + 1) * width] = value

        fold(jnp.concatenate(parts, axis=0), masks, scale, width, block, rot_ref, old, save)

    run(1)
    pl.when(me >= 1 if stage == 0 else z >= 1)(lambda: run(0))


def last_kernel(count, scale, width, second_ref, third_ref, rot_ref, *refs):
    old, out_ref, done_ref, sems = refs[:3], refs[3], refs[4], refs[5]
    _, z, _ = place(count)
    half = out_ref.shape[0] // 2
    dim = rot_ref.shape[2]

    def piece(block, step):
        rows, cols = pl.ds(block * half, half), pl.ds(step * (width // half) * dim, width // half * dim)
        return pltpu.make_async_copy(done_ref.at[rows, cols], out_ref.at[rows, cols], sems.at[block, step])

    def finish(block, step, l, acc):
        done = acc / l
        for h in range(width // half):
            head = step * (width // half) + h
            done_ref[block * half : (block + 1) * half, head * dim : (head + 1) * dim] = (
                done[:, h * half : (h + 1) * half].T.astype(done_ref.dtype)
            )
        piece(block, step).start()

    def add(block):
        rest = third_ref.shape[0] // 2
        part = slice((1 - block) * rest, (2 - block) * rest)
        kv = jnp.concatenate([second_ref[part], third_ref[part]], axis=0)
        masks = usable(count, block, 2)[1:] + usable(count, block, PLANE - 1)[1:]
        fold(kv, masks, scale, width, block, rot_ref, old, lambda step, m, l, acc: finish(block, step, l, acc))

    @pl.when(z < 1)
    def _():
        for step in range(rot_ref.shape[1] // width):
            cols = slice(step * width, (step + 1) * width)
            finish(0, step, old[1][0, :, cols], old[2][0, :, cols])

    add(1)
    pl.when(z >= 1)(lambda: add(0))

    for block in range(2):
        for step in range(rot_ref.shape[1] // width):
            piece(block, step).wait()


def per_device(queries, keys, values, basis, picks):
    rows_dev, dim = keys.shape
    half = rows_dev // 2
    count = lax.axis_size("pb")
    planes = count // PLANE
    wide = queries.shape[1] // dim * half
    width = 4 * half
    scale = dim**-0.5 * math.log2(math.e)
    vmem = pl.BlockSpec(memory_space=pltpu.VMEM)
    params = pltpu.CompilerParams(vmem_limit_bytes=VMEM_BYTES)
    bf16, f32 = jnp.bfloat16, jnp.float32
    shapes = [
        jax.ShapeDtypeStruct((2, 1, wide), f32),
        jax.ShapeDtypeStruct((2, 1, wide), f32),
        jax.ShapeDtypeStruct((2, dim, wide), f32),
    ]

    def rows(n):
        return jax.ShapeDtypeStruct((n * KB, 2 * dim), bf16)

    def permute(value, pairs):
        return lax.ppermute(value, "pb", pairs)

    def cost(keys_each):
        return pl.CostEstimate(
            flops=8 * wide * keys_each * dim, bytes_accessed=4_000_000, transcendentals=2 * wide * keys_each
        )

    per_half = half // KB
    z_rows = (planes - 1) * PLANE
    both, by_source = lax.optimization_barrier((jnp.concatenate([keys, values]), picks.T))
    index, table = pl.pallas_call(
        functools.partial(index_kernel, count),
        out_shape=[jax.ShapeDtypeStruct((n, dim), jnp.int32) for n in (z_rows + 6, 2 * z_rows)],
        in_specs=[vmem],
        out_specs=[vmem] * 2,
        compiler_params=params,
        cost_estimate=pl.CostEstimate(flops=4_000_000_000, bytes_accessed=1_000_000, transcendentals=0),
        name="index",
    )(by_source)
    packets = pl.pallas_call(
        pack_kernel,
        out_shape=[rows(PLANE)] * (planes - 1),
        in_specs=[vmem] * 2,
        out_specs=[vmem] * (planes - 1),
        compiler_params=params,
        cost_estimate=pl.CostEstimate(flops=4_000_000_000, bytes_accessed=1_000_000, transcendentals=0),
        name="pack",
    )(index, both)
    kv, own, beside, over, side = pl.pallas_call(
        functools.partial(pack_own_kernel, z_rows),
        out_shape=[rows(2 * per_half), rows(1), rows(per_half + 1), rows(4 + 0), rows(per_half + 0)],
        in_specs=[vmem] * 2,
        out_specs=[vmem] * 5,
        compiler_params=params,
        name="pack_own",
    )(index, both)

    packets = [
        permute(packet, [(s, (s + j * PLANE) % count) for s in range(count)]) for j, packet in enumerate(packets, 1)
    ]

    rotated = pl.pallas_call(
        rotate_kernel,
        out_shape=jax.ShapeDtypeStruct((2, wide, dim), bf16),
        in_specs=[vmem] * 2,
        out_specs=vmem,
        compiler_params=params,
        cost_estimate=pl.CostEstimate(flops=4 * wide * dim * dim, bytes_accessed=2_000_000, transcendentals=0),
        name="rotate",
    )(queries, basis)
    packets, rotated = lax.optimization_barrier((packets, rotated))
    over = permute(over, [(s, s ^ 2) for s in range(count)])
    groups = lax.axis_size("grp")
    pairs = []
    for g in range(groups):
        pairs += [(g * count + s, g * count + s + (1 if s % 2 else -1)) for s in range(1, count - 1)]
        pairs += [(g * count + s, (g + 1) % groups * count + s) for s in (0, count - 1)]
    side = lax.ppermute(side, ("grp", "pb"), pairs)

    def swap(value, m):
        return permute(value, [(s, s ^ m) for s in range(count)])

    sizes = [2 * planes - 1, 2 * planes - 2, 2 * planes - 2, 2 * planes - 2]
    moved = list(
        pl.pallas_call(
            functools.partial(select_kernel, count),
            out_shape=[rows(size) for size in sizes],
            in_specs=[vmem] * (planes + 1),
            out_specs=[vmem] * len(sizes),
            compiler_params=params,
            name="select",
        )(table, own, *packets)
    )
    for m in (1, 2, 3):
        moved[m] = swap(moved[m], m)
    beside, passed = swap(beside, 1), swap(over[2 * KB : 4 * KB], 1)

    state = pl.pallas_call(
        functools.partial(near_kernel, scale, width),
        out_shape=shapes,
        in_specs=[vmem] * 2,
        out_specs=[vmem] * 3,
        compiler_params=params,
        cost_estimate=cost(half),
        name="near",
    )(kv, rotated)

    def folded(state, stage, messages):
        return pl.pallas_call(
            functools.partial(fold_kernel, count, scale, width, stage),
            out_shape=shapes,
            in_specs=[vmem] * (4 + len(messages)),
            out_specs=[vmem] * 3,
            input_output_aliases={1 + len(messages) + i: i for i in range(3)},
            compiler_params=params,
            cost_estimate=cost(half),
            name=f"fold{stage}",
        )(*messages, rotated, *state)

    state = folded(state, 0, [moved[0], moved[1], beside, over, passed, side, kv])
    return pl.pallas_call(
        functools.partial(last_kernel, count, scale, width),
        out_shape=jax.ShapeDtypeStruct(queries.shape, bf16),
        in_specs=[vmem] * 6,
        out_specs=pl.BlockSpec(memory_space=pl.ANY),
        scratch_shapes=[pltpu.VMEM(queries.shape, bf16), pltpu.SemaphoreType.DMA((2, wide // width))],
        compiler_params=params,
        cost_estimate=cost(half),
        name="last",
    )(moved[2], moved[3], rotated, *state)


def solution(mesh):
    in_specs = (P("pb", "grp"), P("pb", "grp"), P("pb", "grp"), P("grp", None), P("grp", None))
    out_specs = P("pb", "grp")
    return jax.shard_map(
        per_device, mesh=mesh, in_specs=in_specs, out_specs=out_specs, check_vma=False
    )
```

```python
import functools
import math

import jax
import jax.numpy as jnp
from jax import lax
from jax.experimental import pallas as pl
from jax.experimental.pallas import tpu as pltpu
from jax.sharding import PartitionSpec as P

KB = 32
PLANE = 4
NEG = -1e30
VMEM_BYTES = 40 * 1024 * 1024
CHUNK = 16


def place(count):
    me = lax.axis_index("pb")
    return me, me // PLANE, me % PLANE


def sub(index):
    return pl.ds(pl.multiple_of(index * KB, KB), KB)


def at(n):
    return slice(n * KB, (n + 1) * KB)


def scores_of(k, q):
    return lax.dot_general(k, q, (((1,), (1,)), ((), ())), preferred_element_type=jnp.float32)


def splat(picks_ref, wanted, width):
    lane = lax.broadcasted_iota(jnp.int32, (1, picks_ref.shape[1]), 1)
    rows = [jnp.where(lane == block, picks_ref[pl.ds(source, 1), :], 0) for source, block in wanted]
    total = jnp.sum(jnp.concatenate(rows, axis=0), axis=1, keepdims=True)
    return jnp.broadcast_to(jnp.maximum(total, 0), (len(wanted), width))


def chosen(index, choices):
    index = jnp.broadcast_to(index, choices[0].shape)
    value = choices[0]
    for t, choice in enumerate(choices[1:], 1):
        value = jnp.where(index == t, choice, value)
    return value


def index_kernel(count, picks_ref, out_ref, table_ref):
    planes = count // PLANE
    me, z, r = place(count)
    dim = out_ref.shape[1]
    wanted, up_of = [], []
    for j in range(1, planes):
        up = z + j < planes
        to = jnp.where(up, 0, (z + j - planes) * PLANE)
        wanted += [(me, 2 * count - 1 - (to + t)) for t in range(PLANE)]
        up_of += [(up, t) for t in range(PLANE)]
    for m in (0, 1):
        wanted.append((me, 2 * count - 1 - (z * PLANE + (r ^ m))))
    for m in (2, 3):
        dest = z * PLANE + (r ^ m)
        wanted += [(me, 2 * count - 1 - dest), (me, dest)]
    index = splat(picks_ref, wanted, dim)
    for g in range(len(wanted)):
        row = index[g : g + 1]
        out_ref[g : g + 1] = jnp.where(up_of[g][0], up_of[g][1], row) if g < len(up_of) else row
    wanted, fixed = [], []
    for j in range(1, planes):
        up = z >= j
        source = jnp.where(up, z - j, z - j + planes) * PLANE + r
        for m in range(PLANE):
            dest = z * PLANE + (r ^ m)
            wanted += [(source, 2 * count - 1 - dest), (source, dest)]
            fixed += [(up, r ^ m), (up, 0)]
    index = splat(picks_ref, wanted, dim)
    for g, (up, other) in enumerate(fixed):
        table_ref[g : g + 1] = jnp.where(up, index[g : g + 1], other)


def halves(both_ref):
    dim = both_ref.shape[1]
    total = both_ref.shape[0] // 2 // KB
    for part in range(2):
        yield slice(part * dim, (part + 1) * dim), [both_ref[at(part * total + t)] for t in range(total)]


def pack_kernel(index_ref, both_ref, *packet_refs):
    for cols, subs in halves(both_ref):
        for g in range(len(packet_refs) * PLANE):
            packet_refs[g // PLANE][at(g % PLANE), cols] = chosen(index_ref[g : g + 1], subs)


def pack_own_kernel(first, index_ref, both_ref, kv_ref, own_ref, beside_ref, over_ref, side_ref):
    odd = lax.axis_index("pb") % 2 == 1
    for cols, subs in halves(both_ref):
        for t, value in enumerate(subs):
            kv_ref[at(t), cols] = value
        per_half = len(subs) // 2
        for g in range(6):
            ref, t = ((own_ref, 0), (beside_ref, per_half))[g] if g < 2 else (over_ref, g - 2)
            ref[at(t), cols] = chosen(index_ref[first + g : first + g + 1], subs)
        for t in range(per_half):
            side_ref[at(t), cols] = jnp.where(odd, subs[t], subs[per_half + t])
            beside_ref[at(t), cols] = jnp.where(odd, subs[per_half + t], subs[t])


def select_kernel(count, table_ref, own_ref, *refs):
    planes = count // PLANE
    packet_refs, moved_refs = refs[: planes - 1], refs[planes - 1 :]
    dim = table_ref.shape[1]
    moved_refs[0][at(0)] = own_ref[...]
    for j, packet in enumerate(packet_refs, 1):
        for part in (slice(0, dim), slice(dim, 2 * dim)):
            choices = [packet[at(t), part] for t in range(PLANE)]
            for m, ref in enumerate(moved_refs):
                row = ((j - 1) * PLANE + m) * 2
                first = j - (m > 0)
                ref[at(first), part] = chosen(table_ref[row : row + 1], choices)
                ref[at(first + planes - 1), part] = chosen(table_ref[row + 1 : row + 2], choices)


def usable(count, block, m):
    me, z, r = place(count)
    planes = count // PLANE
    if block == 1:
        return [me < count - 1 if m == 0 else None] + [None] * (planes - 1)
    return [(r ^ m) < r - 1] + [(z >= j) & ((z - j) * PLANE + (r ^ m) < me - 1) for j in range(1, planes)]


def attend_all(n_cols, score, v_ts, state, save):
    ahead = score(0)
    for step in range(n_cols):
        s = ahead
        if step + 1 < n_cols:
            ahead = score(step + 1)
        m = jnp.max(s, axis=0, keepdims=True)
        if state is not None:
            m_old, l_old, acc_old = state(step)
            m = jnp.maximum(m, m_old)
        w = jnp.exp2(s - m)
        l = jnp.sum(w, axis=0, keepdims=True)
        acc = jnp.dot(v_ts, w.astype(jnp.bfloat16), preferred_element_type=jnp.float32)
        if state is not None:
            old = jnp.exp2(m_old - m)
            l = l + l_old * old
            acc = acc + acc_old * old
        save(step, m, l, acc)


def fold(kv, masks, scale, width, block, rot_ref, old_refs, save):
    dim = rot_ref.shape[2]
    total = len(masks)
    steps = rot_ref.shape[1] // width
    carried = [tuple(ref[block, :, step * width : (step + 1) * width] for ref in old_refs) for step in range(steps)]
    for first in range(0, total, CHUNK):
        last = min(first + CHUNK, total)
        k = kv[first * KB : last * KB, :dim]
        v_t = kv[first * KB : last * KB, dim:].T

        def score(step, k=k, first=first, last=last):
            s = scores_of(k, rot_ref[block, step * width : (step + 1) * width, :]) * scale
            if all(ok is None for ok in masks[first:last]):
                return s
            return jnp.concatenate(
                [s[at(g - first)] if masks[g] is None else jnp.where(masks[g], s[at(g - first)], NEG) for g in range(first, last)]
            )

        def keep(step, *values):
            carried[step] = values

        attend_all(steps, score, v_t, carried.__getitem__, save if last == total else keep)


def rotate_kernel(q_ref, basis_ref, rot_ref):
    dim = basis_ref.shape[0]
    half = q_ref.shape[0] // 2
    basis = basis_ref[...]
    for block in range(2):
        for h in range(q_ref.shape[1] // dim):
            q = q_ref[block * half : (block + 1) * half, h * dim : (h + 1) * dim]
            q = jnp.dot(q, basis, preferred_element_type=jnp.float32)
            rot_ref[block, h * half : (h + 1) * half, :] = q.astype(rot_ref.dtype)


def near_kernel(scale, width, kv_ref, rot_ref, *state_refs):
    dim = rot_ref.shape[2]
    half = kv_ref.shape[0] // 2
    key_row = lax.broadcasted_iota(jnp.int32, (half, width), 0)
    query = lax.broadcasted_iota(jnp.int32, (half, width), 1) % half
    causal = key_row <= query
    for block in range(2):
        rows = slice(block * half, (block + 1) * half)
        k, v_t = kv_ref[rows, :dim], kv_ref[rows, dim:].T

        def score(step, block=block, k=k):
            s = scores_of(k, rot_ref[block, step * width : (step + 1) * width, :]) * scale
            return jnp.where(causal, s, NEG)

        def save(step, m, l, acc, block=block):
            for ref, value in zip(state_refs, (m, l, acc), strict=True):
                ref[block, :, step * width : (step + 1) * width] = value

        attend_all(rot_ref.shape[1] // width, score, v_t, None, save)


def fold_kernel(count, scale, width, stage, *refs):
    come, rot_ref, old, new = refs[:-7], refs[-7], refs[-6:-3], refs[-3:]
    me, z, _ = place(count)
    rest = (count // PLANE - 1) * KB

    def run(block):
        masks = [usable(count, block, m) for m in range(PLANE)]
        if stage == 0:
            mine_ref, next_ref, beside_ref, over_ref, passed_ref, side_ref, kv_ref = come
            half = kv_ref.shape[0] // 2
            far = slice(0, rest + KB) if block == 1 else slice(rest + KB, 2 * rest + KB)
            side = side_ref[:half]
            if block == 1:
                side = jnp.where(me == count - 1, kv_ref[:half], side)
            near = slice(0, rest) if block == 1 else slice(rest, 2 * rest)
            parts = [mine_ref[far], next_ref[near], over_ref[at(1 - block)], passed_ref[at(1 - block)]]
            masks = masks[0][1 - block :] + masks[1][1:] + masks[2][:1] + masks[3][:1]
            if block == 1:
                parts.append(beside_ref[half:])
                masks.append(None)
            parts.append(jnp.where(me % 2 == block, side, beside_ref[:half]))
            masks += [None] * (half // KB)
        else:
            parts, masks = [come[0][(1 - block) * rest : (2 - block) * rest]], masks[stage][1:]

        def save(step, m, l, acc):
            for ref, value in zip(new, (m, l, acc), strict=True):
                ref[block, :, step * width : (step + 1) * width] = value

        fold(jnp.concatenate(parts, axis=0), masks, scale, width, block, rot_ref, old, save)

    run(1)
    pl.when(me >= 1 if stage == 0 else z >= 1)(lambda: run(0))


def put_heads(ref, first, half, step, l, acc):
    dim, width = acc.shape
    done = acc / l
    for h in range(width // half):
        head = step * (width // half) + h
        ref[first : first + half, head * dim : (head + 1) * dim] = done[:, h * half : (h + 1) * half].T.astype(ref.dtype)


def close_kernel(width, l_ref, acc_ref, first_ref):
    half = first_ref.shape[0]
    _, z, _ = place(lax.axis_size("pb"))

    @pl.when(z < 1)
    def _():
        for step in range(acc_ref.shape[2] // width):
            cols = slice(step * width, (step + 1) * width)
            put_heads(first_ref, 0, half, step, l_ref[0, :, cols], acc_ref[0, :, cols])


def last_kernel(count, scale, width, second_ref, third_ref, first_ref, rot_ref, *refs):
    old, out_ref, done_ref, sems = refs[:3], refs[3], refs[4], refs[5]
    _, z, _ = place(count)
    half = out_ref.shape[0] // 2
    dim = rot_ref.shape[2]

    def piece(block, step, ready=None):
        rows, cols = pl.ds(block * half, half), pl.ds(step * (width // half) * dim, width // half * dim)
        source = done_ref.at[rows, cols] if ready is None else ready.at[:, cols]
        return pltpu.make_async_copy(source, out_ref.at[rows, cols], sems.at[block, step])

    def finish(block, step, l, acc):
        put_heads(done_ref, block * half, half, step, l, acc)
        piece(block, step).start()

    def add(block):
        rest = third_ref.shape[0] // 2
        part = slice((1 - block) * rest, (2 - block) * rest)
        kv = jnp.concatenate([second_ref[part], third_ref[part]], axis=0)
        masks = usable(count, block, 2)[1:] + usable(count, block, PLANE - 1)[1:]
        fold(kv, masks, scale, width, block, rot_ref, old, lambda step, m, l, acc: finish(block, step, l, acc))

    @pl.when(z < 1)
    def _():
        for step in range(rot_ref.shape[1] // width):
            piece(0, step, first_ref).start()

    add(1)
    pl.when(z >= 1)(lambda: add(0))

    for block in range(2):
        for step in range(rot_ref.shape[1] // width):
            piece(block, step).wait()


def per_device(queries, keys, values, basis, picks):
    rows_dev, dim = keys.shape
    half = rows_dev // 2
    count = lax.axis_size("pb")
    planes = count // PLANE
    wide = queries.shape[1] // dim * half
    width = 4 * half
    scale = dim**-0.5 * math.log2(math.e)
    vmem = pl.BlockSpec(memory_space=pltpu.VMEM)
    params = pltpu.CompilerParams(vmem_limit_bytes=VMEM_BYTES)
    bf16, f32 = jnp.bfloat16, jnp.float32
    shapes = [
        jax.ShapeDtypeStruct((2, 1, wide), f32),
        jax.ShapeDtypeStruct((2, 1, wide), f32),
        jax.ShapeDtypeStruct((2, dim, wide), f32),
    ]

    def rows(n):
        return jax.ShapeDtypeStruct((n * KB, 2 * dim), bf16)

    def permute(value, pairs):
        return lax.ppermute(value, "pb", pairs)

    def cost(keys_each):
        return pl.CostEstimate(
            flops=8 * wide * keys_each * dim, bytes_accessed=4_000_000, transcendentals=2 * wide * keys_each
        )

    per_half = half // KB
    z_rows = (planes - 1) * PLANE
    both, by_source = lax.optimization_barrier((jnp.concatenate([keys, values]), picks.T))
    index, table = pl.pallas_call(
        functools.partial(index_kernel, count),
        out_shape=[jax.ShapeDtypeStruct((n, dim), jnp.int32) for n in (z_rows + 6, 2 * z_rows)],
        in_specs=[vmem],
        out_specs=[vmem] * 2,
        compiler_params=params,
        cost_estimate=pl.CostEstimate(flops=4_000_000_000, bytes_accessed=1_000_000, transcendentals=0),
        name="index",
    )(by_source)
    packets = pl.pallas_call(
        pack_kernel,
        out_shape=[rows(PLANE)] * (planes - 1),
        in_specs=[vmem] * 2,
        out_specs=[vmem] * (planes - 1),
        compiler_params=params,
        cost_estimate=pl.CostEstimate(flops=4_000_000_000, bytes_accessed=1_000_000, transcendentals=0),
        name="pack",
    )(index, both)
    kv, own, beside, over, side = pl.pallas_call(
        functools.partial(pack_own_kernel, z_rows),
        out_shape=[rows(2 * per_half), rows(1), rows(per_half + 1), rows(4 + 0), rows(per_half + 0)],
        in_specs=[vmem] * 2,
        out_specs=[vmem] * 5,
        compiler_params=params,
        name="pack_own",
    )(index, both)

    packets = [
        permute(packet, [(s, (s + j * PLANE) % count) for s in range(count)]) for j, packet in enumerate(packets, 1)
    ]

    rotated = pl.pallas_call(
        rotate_kernel,
        out_shape=jax.ShapeDtypeStruct((2, wide, dim), bf16),
        in_specs=[vmem] * 2,
        out_specs=vmem,
        compiler_params=params,
        cost_estimate=pl.CostEstimate(flops=4 * wide * dim * dim, bytes_accessed=2_000_000, transcendentals=0),
        name="rotate",
    )(queries, basis)
    over = permute(over, [(s, s ^ 2) for s in range(count)])
    groups = lax.axis_size("grp")
    pairs = []
    for g in range(groups):
        pairs += [(g * count + s, g * count + s + (1 if s % 2 else -1)) for s in range(1, count - 1)]
        pairs += [(g * count + s, (g + 1) % groups * count + s) for s in (0, count - 1)]
    side = lax.ppermute(side, ("grp", "pb"), pairs)

    def swap(value, m):
        return permute(value, [(s, s ^ m) for s in range(count)])

    sizes = [2 * planes - 1, 2 * planes - 2, 2 * planes - 2, 2 * planes - 2]
    moved = list(
        pl.pallas_call(
            functools.partial(select_kernel, count),
            out_shape=[rows(size) for size in sizes],
            in_specs=[vmem] * (planes + 1),
            out_specs=[vmem] * len(sizes),
            compiler_params=params,
            name="select",
        )(table, own, *packets)
    )
    for m in (1, 2, 3):
        moved[m] = swap(moved[m], m)
    beside, passed = swap(beside, 1), swap(over[2 * KB : 4 * KB], 1)

    state = pl.pallas_call(
        functools.partial(near_kernel, scale, width),
        out_shape=shapes,
        in_specs=[vmem] * 2,
        out_specs=[vmem] * 3,
        compiler_params=params,
        cost_estimate=cost(half),
        name="near",
    )(kv, rotated)

    def folded(state, stage, messages):
        return pl.pallas_call(
            functools.partial(fold_kernel, count, scale, width, stage),
            out_shape=shapes,
            in_specs=[vmem] * (4 + len(messages)),
            out_specs=[vmem] * 3,
            input_output_aliases={1 + len(messages) + i: i for i in range(3)},
            compiler_params=params,
            cost_estimate=cost(half),
            name=f"fold{stage}",
        )(*messages, rotated, *state)

    state = folded(state, 0, [moved[0], moved[1], beside, over, passed, side, kv])
    first = pl.pallas_call(
        functools.partial(close_kernel, width),
        out_shape=jax.ShapeDtypeStruct((half, queries.shape[1]), bf16),
        in_specs=[vmem] * 2,
        out_specs=vmem,
        compiler_params=params,
        name="close",
    )(*state[1:])
    return pl.pallas_call(
        functools.partial(last_kernel, count, scale, width),
        out_shape=jax.ShapeDtypeStruct(queries.shape, bf16),
        in_specs=[vmem] * 7,
        out_specs=pl.BlockSpec(memory_space=pl.ANY),
        scratch_shapes=[pltpu.VMEM(queries.shape, bf16), pltpu.SemaphoreType.DMA((2, wide // width))],
        compiler_params=params,
        cost_estimate=cost(half),
        name="last",
    )(moved[2], moved[3], first, rotated, *state)


def solution(mesh):
    in_specs = (P("pb", "grp"), P("pb", "grp"), P("pb", "grp"), P("grp", None), P("grp", None))
    out_specs = P("pb", "grp")
    return jax.shard_map(
        per_device, mesh=mesh, in_specs=in_specs, out_specs=out_specs, check_vma=False
    )
```

```python
import functools
import math

import jax
import jax.numpy as jnp
from jax import lax
from jax.experimental import pallas as pl
from jax.experimental.pallas import tpu as pltpu
from jax.sharding import PartitionSpec as P

KB = 32
PLANE = 4
NEG = -1e30
VMEM_BYTES = 40 * 1024 * 1024
CHUNK = 16


def place(count):
    me = lax.axis_index("pb")
    return me, me // PLANE, me % PLANE


def sub(index):
    return pl.ds(pl.multiple_of(index * KB, KB), KB)


def at(n):
    return slice(n * KB, (n + 1) * KB)


def scores_of(k, q):
    return lax.dot_general(k, q, (((1,), (1,)), ((), ())), preferred_element_type=jnp.float32)


def splat(picks_ref, wanted, width):
    lane = lax.broadcasted_iota(jnp.int32, (1, picks_ref.shape[1]), 1)
    rows = [jnp.where(lane == block, picks_ref[pl.ds(source, 1), :], 0) for source, block in wanted]
    total = jnp.sum(jnp.concatenate(rows, axis=0), axis=1, keepdims=True)
    return jnp.broadcast_to(jnp.maximum(total, 0), (len(wanted), width))


def chosen(index, choices):
    index = jnp.broadcast_to(index, choices[0].shape)
    value = choices[0]
    for t, choice in enumerate(choices[1:], 1):
        value = jnp.where(index == t, choice, value)
    return value


def index_kernel(count, picks_ref, out_ref, table_ref):
    planes = count // PLANE
    me, z, r = place(count)
    dim = out_ref.shape[1]
    wanted, up_of = [], []
    for j in range(1, planes):
        up = z + j < planes
        to = jnp.where(up, 0, (z + j - planes) * PLANE)
        wanted += [(me, 2 * count - 1 - (to + t)) for t in range(PLANE)]
        up_of += [(up, t) for t in range(PLANE)]
    for m in (0, 1):
        wanted.append((me, 2 * count - 1 - (z * PLANE + (r ^ m))))
    for m in (2, 3):
        dest = z * PLANE + (r ^ m)
        wanted += [(me, 2 * count - 1 - dest), (me, dest)]
    index = splat(picks_ref, wanted, dim)
    for g in range(len(wanted)):
        row = index[g : g + 1]
        out_ref[g : g + 1] = jnp.where(up_of[g][0], up_of[g][1], row) if g < len(up_of) else row
    wanted, fixed = [], []
    for j in range(1, planes):
        up = z >= j
        source = jnp.where(up, z - j, z - j + planes) * PLANE + r
        for m in range(PLANE):
            dest = z * PLANE + (r ^ m)
            wanted += [(source, 2 * count - 1 - dest), (source, dest)]
            fixed += [(up, r ^ m), (up, 0)]
    index = splat(picks_ref, wanted, dim)
    for g, (up, other) in enumerate(fixed):
        table_ref[g : g + 1] = jnp.where(up, index[g : g + 1], other)


def halves(both_ref):
    dim = both_ref.shape[1]
    total = both_ref.shape[0] // 2 // KB
    for part in range(2):
        yield slice(part * dim, (part + 1) * dim), [both_ref[at(part * total + t)] for t in range(total)]


def pack_kernel(index_ref, both_ref, *packet_refs):
    for cols, subs in halves(both_ref):
        for g in range(len(packet_refs) * PLANE):
            packet_refs[g // PLANE][at(g % PLANE), cols] = chosen(index_ref[g : g + 1], subs)


def pack_own_kernel(first, index_ref, both_ref, kv_ref, own_ref, beside_ref, over_ref, side_ref):
    odd = lax.axis_index("pb") % 2 == 1
    for cols, subs in halves(both_ref):
        for t, value in enumerate(subs):
            kv_ref[at(t), cols] = value
        per_half = len(subs) // 2
        for g in range(6):
            ref, t = ((own_ref, 0), (beside_ref, per_half))[g] if g < 2 else (over_ref, g - 2)
            ref[at(t), cols] = chosen(index_ref[first + g : first + g + 1], subs)
        for t in range(per_half):
            side_ref[at(t), cols] = jnp.where(odd, subs[t], subs[per_half + t])
            beside_ref[at(t), cols] = jnp.where(odd, subs[per_half + t], subs[t])


def select_kernel(count, table_ref, own_ref, *refs):
    planes = count // PLANE
    packet_refs, moved_refs, early_ref = refs[: planes - 1], refs[planes - 1 : planes + 3], refs[planes + 3]
    dim = table_ref.shape[1]
    moved_refs[0][at(0)] = own_ref[...]
    for j, packet in enumerate(packet_refs, 1):
        for part in (slice(0, dim), slice(dim, 2 * dim)):
            choices = [packet[at(t), part] for t in range(PLANE)]
            for m, ref in enumerate(moved_refs):
                row = ((j - 1) * PLANE + m) * 2
                first = j - (m > 0)
                ref[at(first), part] = chosen(table_ref[row : row + 1], choices)
                early = chosen(table_ref[row + 1 : row + 2], choices)
                if m < PLANE - 1:
                    ref[at(first + planes - 1), part] = early
                else:
                    early_ref[at(first), part] = early


def usable(count, block, m):
    me, z, r = place(count)
    planes = count // PLANE
    if block == 1:
        return [me < count - 1 if m == 0 else None] + [None] * (planes - 1)
    return [(r ^ m) < r - 1] + [(z >= j) & ((z - j) * PLANE + (r ^ m) < me - 1) for j in range(1, planes)]


def attend_all(n_cols, score, v_ts, state, save):
    ahead = score(0)
    for step in range(n_cols):
        s = ahead
        if step + 1 < n_cols:
            ahead = score(step + 1)
        m = jnp.max(s, axis=0, keepdims=True)
        if state is not None:
            m_old, l_old, acc_old = state(step)
            m = jnp.maximum(m, m_old)
        w = jnp.exp2(s - m)
        l = jnp.sum(w, axis=0, keepdims=True)
        acc = jnp.dot(v_ts, w.astype(jnp.bfloat16), preferred_element_type=jnp.float32)
        if state is not None:
            old = jnp.exp2(m_old - m)
            l = l + l_old * old
            acc = acc + acc_old * old
        save(step, m, l, acc)


def fold(kv, masks, scale, width, block, rot_ref, old_refs, save):
    dim = rot_ref.shape[2]
    total = len(masks)
    steps = rot_ref.shape[1] // width
    carried = [tuple(ref[block, :, step * width : (step + 1) * width] for ref in old_refs) for step in range(steps)]
    for first in range(0, total, CHUNK):
        last = min(first + CHUNK, total)
        k = kv[first * KB : last * KB, :dim]
        v_t = kv[first * KB : last * KB, dim:].T

        def score(step, k=k, first=first, last=last):
            s = scores_of(k, rot_ref[block, step * width : (step + 1) * width, :]) * scale
            if all(ok is None for ok in masks[first:last]):
                return s
            return jnp.concatenate(
                [s[at(g - first)] if masks[g] is None else jnp.where(masks[g], s[at(g - first)], NEG) for g in range(first, last)]
            )

        def keep(step, *values):
            carried[step] = values

        attend_all(steps, score, v_t, carried.__getitem__, save if last == total else keep)


def rotate_kernel(q_ref, basis_ref, rot_ref):
    dim = basis_ref.shape[0]
    half = q_ref.shape[0] // 2
    basis = basis_ref[...]
    for block in range(2):
        for h in range(q_ref.shape[1] // dim):
            q = q_ref[block * half : (block + 1) * half, h * dim : (h + 1) * dim]
            q = jnp.dot(q, basis, preferred_element_type=jnp.float32)
            rot_ref[block, h * half : (h + 1) * half, :] = q.astype(rot_ref.dtype)


def near_kernel(scale, width, kv_ref, rot_ref, *state_refs):
    dim = rot_ref.shape[2]
    half = kv_ref.shape[0] // 2
    key_row = lax.broadcasted_iota(jnp.int32, (half, width), 0)
    query = lax.broadcasted_iota(jnp.int32, (half, width), 1) % half
    causal = key_row <= query
    for block in range(2):
        rows = slice(block * half, (block + 1) * half)
        k, v_t = kv_ref[rows, :dim], kv_ref[rows, dim:].T

        def score(step, block=block, k=k):
            s = scores_of(k, rot_ref[block, step * width : (step + 1) * width, :]) * scale
            return jnp.where(causal, s, NEG)

        def save(step, m, l, acc, block=block):
            for ref, value in zip(state_refs, (m, l, acc), strict=True):
                ref[block, :, step * width : (step + 1) * width] = value

        attend_all(rot_ref.shape[1] // width, score, v_t, None, save)


def fold_kernel(count, scale, width, stage, *refs):
    come, rot_ref, old, new = refs[:-7], refs[-7], refs[-6:-3], refs[-3:]
    me, z, _ = place(count)
    rest = (count // PLANE - 1) * KB

    def run(block, light=False):
        masks = [usable(count, block, m) for m in range(PLANE)]
        if stage == 0:
            mine_ref, next_ref, beside_ref, over_ref, passed_ref, side_ref, kv_ref = come
            half = kv_ref.shape[0] // 2
            far = slice(0, rest + KB) if block == 1 else slice(rest + KB, 2 * rest + KB)
            side = side_ref[:half]
            if block == 1:
                side = jnp.where(me == count - 1, kv_ref[:half], side)
            near = slice(0, rest) if block == 1 else slice(rest, 2 * rest)
            parts = [mine_ref[far], next_ref[near], over_ref[at(1 - block)], passed_ref[at(1 - block)]]
            masks = masks[0][1 - block :] + masks[1][1:] + masks[2][:1] + masks[3][:1]
            if block == 1:
                parts.append(beside_ref[half:])
                masks.append(None)
            if light:
                parts, masks = parts[2:], masks[2 * rest // KB :]
            parts.append(jnp.where(me % 2 == block, side, beside_ref[:half]))
            masks += [None] * (half // KB)
        else:
            parts, masks = [come[0][(1 - block) * rest : (2 - block) * rest]], masks[stage][1:]

        def save(step, m, l, acc):
            for ref, value in zip(new, (m, l, acc), strict=True):
                ref[block, :, step * width : (step + 1) * width] = value

        fold(jnp.concatenate(parts, axis=0), masks, scale, width, block, rot_ref, old, save)

    run(1)
    pl.when(z >= 1)(lambda: run(0))
    if stage == 0:
        pl.when((z < 1) & (me >= 1))(lambda: run(0, True))


def put_heads(ref, first, half, step, l, acc):
    dim, width = acc.shape
    done = acc / l
    for h in range(width // half):
        head = step * (width // half) + h
        ref[first : first + half, head * dim : (head + 1) * dim] = done[:, h * half : (h + 1) * half].T.astype(ref.dtype)


def close_kernel(width, l_ref, acc_ref, first_ref):
    half = first_ref.shape[0]
    _, z, _ = place(lax.axis_size("pb"))

    @pl.when(z < 1)
    def _():
        for step in range(acc_ref.shape[2] // width):
            cols = slice(step * width, (step + 1) * width)
            put_heads(first_ref, 0, half, step, l_ref[0, :, cols], acc_ref[0, :, cols])


def last_kernel(count, scale, width, second_ref, third_ref, early_ref, first_ref, rot_ref, *refs):
    old, out_ref, done_ref, sems = refs[:3], refs[3], refs[4], refs[5]
    _, z, _ = place(count)
    half = out_ref.shape[0] // 2
    dim = rot_ref.shape[2]

    def piece(block, step, ready=None):
        rows, cols = pl.ds(block * half, half), pl.ds(step * (width // half) * dim, width // half * dim)
        source = done_ref.at[rows, cols] if ready is None else ready.at[:, cols]
        return pltpu.make_async_copy(source, out_ref.at[rows, cols], sems.at[block, step])

    def finish(block, step, l, acc):
        put_heads(done_ref, block * half, half, step, l, acc)
        piece(block, step).start()

    def add(block):
        rest = third_ref.shape[0]
        part = slice((1 - block) * rest, (2 - block) * rest)
        third = third_ref if block == 1 else early_ref
        kv = jnp.concatenate([second_ref[part], third[...]], axis=0)
        masks = usable(count, block, 2)[1:] + usable(count, block, PLANE - 1)[1:]
        fold(kv, masks, scale, width, block, rot_ref, old, lambda step, m, l, acc: finish(block, step, l, acc))

    @pl.when(z < 1)
    def _():
        for step in range(rot_ref.shape[1] // width):
            piece(0, step, first_ref).start()

    add(1)
    pl.when(z >= 1)(lambda: add(0))

    for block in range(2):
        for step in range(rot_ref.shape[1] // width):
            piece(block, step).wait()


def per_device(queries, keys, values, basis, picks):
    rows_dev, dim = keys.shape
    half = rows_dev // 2
    count = lax.axis_size("pb")
    planes = count // PLANE
    wide = queries.shape[1] // dim * half
    width = 4 * half
    scale = dim**-0.5 * math.log2(math.e)
    vmem = pl.BlockSpec(memory_space=pltpu.VMEM)
    params = pltpu.CompilerParams(vmem_limit_bytes=VMEM_BYTES)
    bf16, f32 = jnp.bfloat16, jnp.float32
    shapes = [
        jax.ShapeDtypeStruct((2, 1, wide), f32),
        jax.ShapeDtypeStruct((2, 1, wide), f32),
        jax.ShapeDtypeStruct((2, dim, wide), f32),
    ]

    def rows(n):
        return jax.ShapeDtypeStruct((n * KB, 2 * dim), bf16)

    def permute(value, pairs):
        return lax.ppermute(value, "pb", pairs)

    def cost(keys_each):
        return pl.CostEstimate(
            flops=8 * wide * keys_each * dim, bytes_accessed=4_000_000, transcendentals=2 * wide * keys_each
        )

    per_half = half // KB
    z_rows = (planes - 1) * PLANE
    both, by_source = lax.optimization_barrier((jnp.concatenate([keys, values]), picks.T))
    index, table = pl.pallas_call(
        functools.partial(index_kernel, count),
        out_shape=[jax.ShapeDtypeStruct((n, dim), jnp.int32) for n in (z_rows + 6, 2 * z_rows)],
        in_specs=[vmem],
        out_specs=[vmem] * 2,
        compiler_params=params,
        cost_estimate=pl.CostEstimate(flops=4_000_000_000, bytes_accessed=1_000_000, transcendentals=0),
        name="index",
    )(by_source)
    packets = pl.pallas_call(
        pack_kernel,
        out_shape=[rows(PLANE)] * (planes - 1),
        in_specs=[vmem] * 2,
        out_specs=[vmem] * (planes - 1),
        compiler_params=params,
        cost_estimate=pl.CostEstimate(flops=4_000_000_000, bytes_accessed=1_000_000, transcendentals=0),
        name="pack",
    )(index, both)
    kv, own, beside, over, side = pl.pallas_call(
        functools.partial(pack_own_kernel, z_rows),
        out_shape=[rows(2 * per_half), rows(1), rows(per_half + 1), rows(4 + 0), rows(per_half + 0)],
        in_specs=[vmem] * 2,
        out_specs=[vmem] * 5,
        compiler_params=params,
        name="pack_own",
    )(index, both)

    packets = [
        permute(packet, [(s, (s + j * PLANE) % count) for s in range(count)]) for j, packet in enumerate(packets, 1)
    ]

    rotated = pl.pallas_call(
        rotate_kernel,
        out_shape=jax.ShapeDtypeStruct((2, wide, dim), bf16),
        in_specs=[vmem] * 2,
        out_specs=vmem,
        compiler_params=params,
        cost_estimate=pl.CostEstimate(flops=4 * wide * dim * dim, bytes_accessed=2_000_000, transcendentals=0),
        name="rotate",
    )(queries, basis)
    packets, rotated = lax.optimization_barrier((packets, rotated))
    over = permute(over, [(s, s ^ 2) for s in range(count)])
    groups = lax.axis_size("grp")
    pairs = []
    for g in range(groups):
        pairs += [(g * count + s, g * count + s + (1 if s % 2 else -1)) for s in range(1, count - 1)]
        pairs += [(g * count + s, (g + 1) % groups * count + s) for s in (0, count - 1)]
    side = lax.ppermute(side, ("grp", "pb"), pairs)

    def swap(value, m):
        return permute(value, [(s, s ^ m) for s in range(count)])

    sizes = [2 * planes - 1, 2 * planes - 2, 2 * planes - 2, planes - 1, planes - 1]
    moved = list(
        pl.pallas_call(
            functools.partial(select_kernel, count),
            out_shape=[rows(size) for size in sizes],
            in_specs=[vmem] * (planes + 1),
            out_specs=[vmem] * len(sizes),
            compiler_params=params,
            name="select",
        )(table, own, *packets)
    )
    for m in (1, 2, 3):
        moved[m] = swap(moved[m], m)
    early = permute(moved[PLANE], [(s, s ^ (PLANE - 1 if s >= PLANE else 1)) for s in range(count)])
    beside, passed = swap(beside, 1), swap(over[2 * KB : 4 * KB], 1)

    state = pl.pallas_call(
        functools.partial(near_kernel, scale, width),
        out_shape=shapes,
        in_specs=[vmem] * 2,
        out_specs=[vmem] * 3,
        compiler_params=params,
        cost_estimate=cost(half),
        name="near",
    )(kv, rotated)

    def folded(state, stage, messages):
        return pl.pallas_call(
            functools.partial(fold_kernel, count, scale, width, stage),
            out_shape=shapes,
            in_specs=[vmem] * (4 + len(messages)),
            out_specs=[vmem] * 3,
            input_output_aliases={1 + len(messages) + i: i for i in range(3)},
            compiler_params=params,
            cost_estimate=cost(half),
            name=f"fold{stage}",
        )(*messages, rotated, *state)

    state = folded(state, 0, [moved[0], moved[1], beside, over, passed, side, kv])
    first = pl.pallas_call(
        functools.partial(close_kernel, width),
        out_shape=jax.ShapeDtypeStruct((half, queries.shape[1]), bf16),
        in_specs=[vmem] * 2,
        out_specs=vmem,
        compiler_params=params,
        name="close",
    )(*state[1:])
    return pl.pallas_call(
        functools.partial(last_kernel, count, scale, width),
        out_shape=jax.ShapeDtypeStruct(queries.shape, bf16),
        in_specs=[vmem] * 8,
        out_specs=pl.BlockSpec(memory_space=pl.ANY),
        scratch_shapes=[pltpu.VMEM(queries.shape, bf16), pltpu.SemaphoreType.DMA((2, wide // width))],
        compiler_params=params,
        cost_estimate=cost(half),
        name="last",
    )(moved[2], moved[3], early, first, rotated, *state)


def solution(mesh):
    in_specs = (P("pb", "grp"), P("pb", "grp"), P("pb", "grp"), P("grp", None), P("grp", None))
    out_specs = P("pb", "grp")
    return jax.shard_map(
        per_device, mesh=mesh, in_specs=in_specs, out_specs=out_specs, check_vma=False
    )
```

```python
import functools
import math

import jax
import jax.numpy as jnp
from jax import lax
from jax.experimental import pallas as pl
from jax.experimental.pallas import tpu as pltpu
from jax.sharding import PartitionSpec as P

KB = 32
PLANE = 4
NEG = -1e30
VMEM_BYTES = 40 * 1024 * 1024
CHUNK = 16


def place(count):
    me = lax.axis_index("pb")
    return me, me // PLANE, me % PLANE


def sub(index):
    return pl.ds(pl.multiple_of(index * KB, KB), KB)


def at(n):
    return slice(n * KB, (n + 1) * KB)


def scores_of(k, q):
    return lax.dot_general(k, q, (((1,), (1,)), ((), ())), preferred_element_type=jnp.float32)


def splat(picks_ref, wanted, width):
    lane = lax.broadcasted_iota(jnp.int32, (1, picks_ref.shape[1]), 1)
    rows = [jnp.where(lane == block, picks_ref[pl.ds(source, 1), :], 0) for source, block in wanted]
    total = jnp.sum(jnp.concatenate(rows, axis=0), axis=1, keepdims=True)
    return jnp.broadcast_to(jnp.maximum(total, 0), (len(wanted), width))


def chosen(index, choices):
    index = jnp.broadcast_to(index, choices[0].shape)
    value = choices[0]
    for t, choice in enumerate(choices[1:], 1):
        value = jnp.where(index == t, choice, value)
    return value


def index_kernel(count, picks_ref, out_ref, table_ref):
    planes = count // PLANE
    me, z, r = place(count)
    dim = out_ref.shape[1]
    wanted, up_of = [], []
    for j in range(1, planes):
        up = z + j < planes
        to = jnp.where(up, 0, (z + j - planes) * PLANE)
        wanted += [(me, 2 * count - 1 - (to + t)) for t in range(PLANE)]
        up_of += [(up, t) for t in range(PLANE)]
    for m in (0, 1):
        wanted.append((me, 2 * count - 1 - (z * PLANE + (r ^ m))))
    for m in (2, 3):
        dest = z * PLANE + (r ^ m)
        wanted += [(me, 2 * count - 1 - dest), (me, dest)]
    index = splat(picks_ref, wanted, dim)
    for g in range(len(wanted)):
        row = index[g : g + 1]
        out_ref[g : g + 1] = jnp.where(up_of[g][0], up_of[g][1], row) if g < len(up_of) else row
    wanted, fixed = [], []
    for j in range(1, planes):
        up = z >= j
        source = jnp.where(up, z - j, z - j + planes) * PLANE + r
        for m in range(PLANE):
            dest = z * PLANE + (r ^ m)
            wanted += [(source, 2 * count - 1 - dest), (source, dest)]
            fixed += [(up, r ^ m), (up, 0)]
    index = splat(picks_ref, wanted, dim)
    for g, (up, other) in enumerate(fixed):
        table_ref[g : g + 1] = jnp.where(up, index[g : g + 1], other)


def halves(both_ref):
    dim = both_ref.shape[1]
    total = both_ref.shape[0] // 2 // KB
    for part in range(2):
        yield slice(part * dim, (part + 1) * dim), [both_ref[at(part * total + t)] for t in range(total)]


def pack_kernel(index_ref, both_ref, *packet_refs):
    for cols, subs in halves(both_ref):
        for g in range(len(packet_refs) * PLANE):
            packet_refs[g // PLANE][at(g % PLANE), cols] = chosen(index_ref[g : g + 1], subs)


def pack_own_kernel(first, index_ref, both_ref, kv_ref, own_ref, beside_ref, over_ref, side_ref):
    odd = lax.axis_index("pb") % 2 == 1
    for cols, subs in halves(both_ref):
        for t, value in enumerate(subs):
            kv_ref[at(t), cols] = value
        per_half = len(subs) // 2
        for g in range(6):
            ref, t = ((own_ref, 0), (beside_ref, per_half))[g] if g < 2 else (over_ref, g - 2)
            ref[at(t), cols] = chosen(index_ref[first + g : first + g + 1], subs)
        for t in range(per_half):
            side_ref[at(t), cols] = jnp.where(odd, subs[t], subs[per_half + t])
            beside_ref[at(t), cols] = jnp.where(odd, subs[per_half + t], subs[t])


def select_kernel(count, table_ref, own_ref, *refs):
    planes = count // PLANE
    packet_refs, moved_refs, early_ref = refs[: planes - 1], refs[planes - 1 : planes + 3], refs[planes + 3]
    dim = table_ref.shape[1]
    moved_refs[0][at(0)] = own_ref[...]
    for j, packet in enumerate(packet_refs, 1):
        for part in (slice(0, dim), slice(dim, 2 * dim)):
            choices = [packet[at(t), part] for t in range(PLANE)]
            for m, ref in enumerate(moved_refs):
                row = ((j - 1) * PLANE + m) * 2
                first = j - (m > 0)
                ref[at(first), part] = chosen(table_ref[row : row + 1], choices)
                early = chosen(table_ref[row + 1 : row + 2], choices)
                if m < PLANE - 1:
                    ref[at(first + planes - 1), part] = early
                else:
                    early_ref[at(first), part] = early


def usable(count, block, m):
    me, z, r = place(count)
    planes = count // PLANE
    if block == 1:
        return [me < count - 1 if m == 0 else None] + [None] * (planes - 1)
    return [(r ^ m) < r - 1] + [(z >= j) & ((z - j) * PLANE + (r ^ m) < me - 1) for j in range(1, planes)]


def attend_all(n_cols, score, v_ts, state, save):
    ahead = score(0)
    for step in range(n_cols):
        s = ahead
        if step + 1 < n_cols:
            ahead = score(step + 1)
        m = jnp.max(s, axis=0, keepdims=True)
        if state is not None:
            m_old, l_old, acc_old = state(step)
            m = jnp.maximum(m, m_old)
        w = jnp.exp2(s - m)
        l = jnp.sum(w, axis=0, keepdims=True)
        acc = jnp.dot(v_ts, w.astype(jnp.bfloat16), preferred_element_type=jnp.float32)
        if state is not None:
            old = jnp.exp2(m_old - m)
            l = l + l_old * old
            acc = acc + acc_old * old
        save(step, m, l, acc)


def fold(kv, masks, scale, width, block, rot_ref, old_refs, save):
    dim = rot_ref.shape[2]
    total = len(masks)
    steps = rot_ref.shape[1] // width
    carried = [tuple(ref[block, :, step * width : (step + 1) * width] for ref in old_refs) for step in range(steps)]
    for first in range(0, total, CHUNK):
        last = min(first + CHUNK, total)
        k = kv[first * KB : last * KB, :dim]
        v_t = kv[first * KB : last * KB, dim:].T

        def score(step, k=k, first=first, last=last):
            s = scores_of(k, rot_ref[block, step * width : (step + 1) * width, :]) * scale
            if all(ok is None for ok in masks[first:last]):
                return s
            return jnp.concatenate(
                [s[at(g - first)] if masks[g] is None else jnp.where(masks[g], s[at(g - first)], NEG) for g in range(first, last)]
            )

        def keep(step, *values):
            carried[step] = values

        attend_all(steps, score, v_t, carried.__getitem__, save if last == total else keep)


def rotate_kernel(q_ref, basis_ref, rot_ref):
    dim = basis_ref.shape[0]
    half = q_ref.shape[0] // 2
    basis = basis_ref[...]
    for block in range(2):
        for h in range(q_ref.shape[1] // dim):
            q = q_ref[block * half : (block + 1) * half, h * dim : (h + 1) * dim]
            q = jnp.dot(q, basis, preferred_element_type=jnp.float32)
            rot_ref[block, h * half : (h + 1) * half, :] = q.astype(rot_ref.dtype)


def near_kernel(scale, width, kv_ref, rot_ref, *state_refs):
    dim = rot_ref.shape[2]
    half = kv_ref.shape[0] // 2
    key_row = lax.broadcasted_iota(jnp.int32, (half, width), 0)
    query = lax.broadcasted_iota(jnp.int32, (half, width), 1) % half
    causal = key_row <= query
    for block in range(2):
        rows = slice(block * half, (block + 1) * half)
        k, v_t = kv_ref[rows, :dim], kv_ref[rows, dim:].T

        def score(step, block=block, k=k):
            s = scores_of(k, rot_ref[block, step * width : (step + 1) * width, :]) * scale
            return jnp.where(causal, s, NEG)

        def save(step, m, l, acc, block=block):
            for ref, value in zip(state_refs, (m, l, acc), strict=True):
                ref[block, :, step * width : (step + 1) * width] = value

        attend_all(rot_ref.shape[1] // width, score, v_t, None, save)


def fold_kernel(count, scale, width, stage, *refs):
    come, rot_ref, old, new = refs[:-7], refs[-7], refs[-6:-3], refs[-3:]
    me, z, _ = place(count)
    rest = (count // PLANE - 1) * KB

    def run(block, light=False, one=False):
        masks = [usable(count, block, m) for m in range(PLANE)]
        if stage == 0:
            mine_ref, next_ref, beside_ref, over_ref, passed_ref, side_ref, kv_ref = come
            half = kv_ref.shape[0] // 2
            far = slice(0, rest + KB) if block == 1 else slice(rest + KB, 2 * rest + KB)
            side = side_ref[:half]
            if block == 1:
                side = jnp.where(me == count - 1, kv_ref[:half], side)
            near = slice(0, rest) if block == 1 else slice(rest, 2 * rest)
            parts = [mine_ref[far], next_ref[near], over_ref[at(1 - block)], passed_ref[at(1 - block)]]
            masks = masks[0][1 - block :] + masks[1][1:] + masks[2][:1] + masks[3][:1]
            if block == 1:
                parts.append(beside_ref[half:])
                masks.append(None)
            if light:
                parts, masks = parts[2:], masks[2 * rest // KB :]
            if one:
                parts[:2] = [part[:KB] for part in parts[:2]]
                masks = [masks[0], masks[rest // KB]] + masks[2 * rest // KB :]
            parts.append(jnp.where(me % 2 == block, side, beside_ref[:half]))
            masks += [None] * (half // KB)
        else:
            parts, masks = [come[0][(1 - block) * rest : (2 - block) * rest]], masks[stage][1:]

        def save(step, m, l, acc):
            for ref, value in zip(new, (m, l, acc), strict=True):
                ref[block, :, step * width : (step + 1) * width] = value

        fold(jnp.concatenate(parts, axis=0), masks, scale, width, block, rot_ref, old, save)

    run(1)
    pl.when(z >= 2)(lambda: run(0))
    if stage == 0:
        pl.when(z == 1)(lambda: run(0, one=True))
        pl.when((z < 1) & (me >= 1))(lambda: run(0, True))


def put_heads(ref, first, half, step, l, acc):
    dim, width = acc.shape
    done = acc / l
    for h in range(width // half):
        head = step * (width // half) + h
        ref[first : first + half, head * dim : (head + 1) * dim] = done[:, h * half : (h + 1) * half].T.astype(ref.dtype)


def close_kernel(width, l_ref, acc_ref, first_ref):
    half = first_ref.shape[0]
    _, z, _ = place(lax.axis_size("pb"))

    @pl.when(z < 1)
    def _():
        for step in range(acc_ref.shape[2] // width):
            cols = slice(step * width, (step + 1) * width)
            put_heads(first_ref, 0, half, step, l_ref[0, :, cols], acc_ref[0, :, cols])


def last_kernel(count, scale, width, second_ref, third_ref, early_ref, first_ref, rot_ref, *refs):
    old, out_ref, done_ref, sems = refs[:3], refs[3], refs[4], refs[5]
    _, z, _ = place(count)
    half = out_ref.shape[0] // 2
    dim = rot_ref.shape[2]

    def piece(block, step, ready=None):
        rows, cols = pl.ds(block * half, half), pl.ds(step * (width // half) * dim, width // half * dim)
        source = done_ref.at[rows, cols] if ready is None else ready.at[:, cols]
        return pltpu.make_async_copy(source, out_ref.at[rows, cols], sems.at[block, step])

    def finish(block, step, l, acc):
        put_heads(done_ref, block * half, half, step, l, acc)
        piece(block, step).start()

    def add(block, one=False):
        rest = third_ref.shape[0]
        part = slice((1 - block) * rest, (2 - block) * rest)
        third = third_ref if block == 1 else early_ref
        kv = jnp.concatenate([second_ref[part], third[...]], axis=0)
        masks = usable(count, block, 2)[1:] + usable(count, block, PLANE - 1)[1:]
        if one:
            kv = jnp.concatenate([kv[:KB], kv[rest : rest + KB]], axis=0)
            masks = [masks[0], masks[rest // KB]]
        fold(kv, masks, scale, width, block, rot_ref, old, lambda step, m, l, acc: finish(block, step, l, acc))

    @pl.when(z < 1)
    def _():
        for step in range(rot_ref.shape[1] // width):
            piece(0, step, first_ref).start()

    add(1)
    pl.when(z == 1)(lambda: add(0, one=True))
    pl.when(z >= 2)(lambda: add(0))

    for block in range(2):
        for step in range(rot_ref.shape[1] // width):
            piece(block, step).wait()


def per_device(queries, keys, values, basis, picks):
    rows_dev, dim = keys.shape
    half = rows_dev // 2
    count = lax.axis_size("pb")
    planes = count // PLANE
    wide = queries.shape[1] // dim * half
    width = 4 * half
    scale = dim**-0.5 * math.log2(math.e)
    vmem = pl.BlockSpec(memory_space=pltpu.VMEM)
    params = pltpu.CompilerParams(vmem_limit_bytes=VMEM_BYTES)
    bf16, f32 = jnp.bfloat16, jnp.float32
    shapes = [
        jax.ShapeDtypeStruct((2, 1, wide), f32),
        jax.ShapeDtypeStruct((2, 1, wide), f32),
        jax.ShapeDtypeStruct((2, dim, wide), f32),
    ]

    def rows(n):
        return jax.ShapeDtypeStruct((n * KB, 2 * dim), bf16)

    def permute(value, pairs):
        return lax.ppermute(value, "pb", pairs)

    def cost(keys_each):
        return pl.CostEstimate(
            flops=8 * wide * keys_each * dim, bytes_accessed=4_000_000, transcendentals=2 * wide * keys_each
        )

    per_half = half // KB
    z_rows = (planes - 1) * PLANE
    both, by_source = lax.optimization_barrier((jnp.concatenate([keys, values]), picks.T))
    index, table = pl.pallas_call(
        functools.partial(index_kernel, count),
        out_shape=[jax.ShapeDtypeStruct((n, dim), jnp.int32) for n in (z_rows + 6, 2 * z_rows)],
        in_specs=[vmem],
        out_specs=[vmem] * 2,
        compiler_params=params,
        cost_estimate=pl.CostEstimate(flops=4_000_000_000, bytes_accessed=1_000_000, transcendentals=0),
        name="index",
    )(by_source)
    packets = pl.pallas_call(
        pack_kernel,
        out_shape=[rows(PLANE)] * (planes - 1),
        in_specs=[vmem] * 2,
        out_specs=[vmem] * (planes - 1),
        compiler_params=params,
        cost_estimate=pl.CostEstimate(flops=4_000_000_000, bytes_accessed=1_000_000, transcendentals=0),
        name="pack",
    )(index, both)
    kv, own, beside, over, side = pl.pallas_call(
        functools.partial(pack_own_kernel, z_rows),
        out_shape=[rows(2 * per_half), rows(1), rows(per_half + 1), rows(4 + 0), rows(per_half + 0)],
        in_specs=[vmem] * 2,
        out_specs=[vmem] * 5,
        compiler_params=params,
        name="pack_own",
    )(index, both)

    packets = [
        permute(packet, [(s, (s + j * PLANE) % count) for s in range(count)]) for j, packet in enumerate(packets, 1)
    ]

    rotated = pl.pallas_call(
        rotate_kernel,
        out_shape=jax.ShapeDtypeStruct((2, wide, dim), bf16),
        in_specs=[vmem] * 2,
        out_specs=vmem,
        compiler_params=params,
        cost_estimate=pl.CostEstimate(flops=4 * wide * dim * dim, bytes_accessed=2_000_000, transcendentals=0),
        name="rotate",
    )(queries, basis)
    packets, rotated = lax.optimization_barrier((packets, rotated))
    over = permute(over, [(s, s ^ 2) for s in range(count)])
    groups = lax.axis_size("grp")
    pairs = []
    for g in range(groups):
        pairs += [(g * count + s, g * count + s + (1 if s % 2 else -1)) for s in range(1, count - 1)]
        pairs += [(g * count + s, (g + 1) % groups * count + s) for s in (0, count - 1)]
    side = lax.ppermute(side, ("grp", "pb"), pairs)

    def swap(value, m):
        return permute(value, [(s, s ^ m) for s in range(count)])

    sizes = [2 * planes - 1, 2 * planes - 2, 2 * planes - 2, planes - 1, planes - 1]
    moved = list(
        pl.pallas_call(
            functools.partial(select_kernel, count),
            out_shape=[rows(size) for size in sizes],
            in_specs=[vmem] * (planes + 1),
            out_specs=[vmem] * len(sizes),
            compiler_params=params,
            name="select",
        )(table, own, *packets)
    )
    for m in (1, 2, 3):
        moved[m] = swap(moved[m], m)
    early = permute(moved[PLANE], [(s, s ^ (PLANE - 1 if s >= PLANE else 1)) for s in range(count)])
    beside, passed = swap(beside, 1), swap(over[2 * KB : 4 * KB], 1)

    state = pl.pallas_call(
        functools.partial(near_kernel, scale, width),
        out_shape=shapes,
        in_specs=[vmem] * 2,
        out_specs=[vmem] * 3,
        compiler_params=params,
        cost_estimate=cost(half),
        name="near",
    )(kv, rotated)

    def folded(state, stage, messages):
        return pl.pallas_call(
            functools.partial(fold_kernel, count, scale, width, stage),
            out_shape=shapes,
            in_specs=[vmem] * (4 + len(messages)),
            out_specs=[vmem] * 3,
            input_output_aliases={1 + len(messages) + i: i for i in range(3)},
            compiler_params=params,
            cost_estimate=cost(half),
            name=f"fold{stage}",
        )(*messages, rotated, *state)

    state = folded(state, 0, [moved[0], moved[1], beside, over, passed, side, kv])
    first = pl.pallas_call(
        functools.partial(close_kernel, width),
        out_shape=jax.ShapeDtypeStruct((half, queries.shape[1]), bf16),
        in_specs=[vmem] * 2,
        out_specs=vmem,
        compiler_params=params,
        name="close",
    )(*state[1:])
    return pl.pallas_call(
        functools.partial(last_kernel, count, scale, width),
        out_shape=jax.ShapeDtypeStruct(queries.shape, bf16),
        in_specs=[vmem] * 8,
        out_specs=pl.BlockSpec(memory_space=pl.ANY),
        scratch_shapes=[pltpu.VMEM(queries.shape, bf16), pltpu.SemaphoreType.DMA((2, wide // width))],
        compiler_params=params,
        cost_estimate=cost(half),
        name="last",
    )(moved[2], moved[3], early, first, rotated, *state)


def solution(mesh):
    in_specs = (P("pb", "grp"), P("pb", "grp"), P("pb", "grp"), P("grp", None), P("grp", None))
    out_specs = P("pb", "grp")
    return jax.shard_map(
        per_device, mesh=mesh, in_specs=in_specs, out_specs=out_specs, check_vma=False
    )
```

```python
import functools
import math

import jax
import jax.numpy as jnp
from jax import lax
from jax.experimental import pallas as pl
from jax.experimental.pallas import tpu as pltpu
from jax.sharding import PartitionSpec as P

KB = 32
PLANE = 4
NEG = -1e30
VMEM_BYTES = 40 * 1024 * 1024
CHUNK = 16


def place(count):
    me = lax.axis_index("pb")
    return me, me // PLANE, me % PLANE


def sub(index):
    return pl.ds(pl.multiple_of(index * KB, KB), KB)


def at(n):
    return slice(n * KB, (n + 1) * KB)


def scores_of(k, q):
    return lax.dot_general(k, q, (((1,), (1,)), ((), ())), preferred_element_type=jnp.float32)


def splat(picks_ref, wanted, width):
    lane = lax.broadcasted_iota(jnp.int32, (1, picks_ref.shape[1]), 1)
    rows = [jnp.where(lane == block, picks_ref[pl.ds(source, 1), :], 0) for source, block in wanted]
    total = jnp.sum(jnp.concatenate(rows, axis=0), axis=1, keepdims=True)
    return jnp.broadcast_to(jnp.maximum(total, 0), (len(wanted), width))


def chosen(index, choices):
    index = jnp.broadcast_to(index, choices[0].shape)
    value = choices[0]
    for t, choice in enumerate(choices[1:], 1):
        value = jnp.where(index == t, choice, value)
    return value


def index_kernel(count, picks_ref, out_ref, table_ref):
    planes = count // PLANE
    me, z, r = place(count)
    dim = out_ref.shape[1]
    wanted, up_of = [], []
    for j in range(1, planes):
        up = z + j < planes
        to = jnp.where(up, 0, (z + j - planes) * PLANE)
        wanted += [(me, 2 * count - 1 - (to + t)) for t in range(PLANE)]
        up_of += [(up, t) for t in range(PLANE)]
    for m in (0, 1):
        wanted.append((me, 2 * count - 1 - (z * PLANE + (r ^ m))))
    for m in (2, 3):
        dest = z * PLANE + (r ^ m)
        wanted += [(me, 2 * count - 1 - dest), (me, dest)]
    index = splat(picks_ref, wanted, dim)
    for g in range(len(wanted)):
        row = index[g : g + 1]
        out_ref[g : g + 1] = jnp.where(up_of[g][0], up_of[g][1], row) if g < len(up_of) else row
    wanted, fixed = [], []
    for j in range(1, planes):
        up = z >= j
        source = jnp.where(up, z - j, z - j + planes) * PLANE + r
        for m in range(PLANE):
            dest = z * PLANE + (r ^ m)
            wanted += [(source, 2 * count - 1 - dest), (source, dest)]
            fixed += [(up, r ^ m), (up, 0)]
    index = splat(picks_ref, wanted, dim)
    for g, (up, other) in enumerate(fixed):
        table_ref[g : g + 1] = jnp.where(up, index[g : g + 1], other)


def halves(both_ref):
    dim = both_ref.shape[1]
    total = both_ref.shape[0] // 2 // KB
    for part in range(2):
        yield slice(part * dim, (part + 1) * dim), [both_ref[at(part * total + t)] for t in range(total)]


def pack_kernel(index_ref, both_ref, *packet_refs):
    for cols, subs in halves(both_ref):
        for g in range(len(packet_refs) * PLANE):
            packet_refs[g // PLANE][at(g % PLANE), cols] = chosen(index_ref[g : g + 1], subs)


def pack_own_kernel(first, index_ref, both_ref, kv_ref, own_ref, beside_ref, over_ref, side_ref):
    odd = lax.axis_index("pb") % 2 == 1
    for cols, subs in halves(both_ref):
        for t, value in enumerate(subs):
            kv_ref[at(t), cols] = value
        per_half = len(subs) // 2
        for g in range(6):
            ref, t = ((own_ref, 0), (beside_ref, per_half))[g] if g < 2 else (over_ref, g - 2)
            ref[at(t), cols] = chosen(index_ref[first + g : first + g + 1], subs)
        for t in range(per_half):
            side_ref[at(t), cols] = jnp.where(odd, subs[t], subs[per_half + t])
            beside_ref[at(t), cols] = jnp.where(odd, subs[per_half + t], subs[t])


def select_kernel(count, table_ref, own_ref, *refs):
    planes = count // PLANE
    packet_refs, moved_refs, early_ref = refs[: planes - 1], refs[planes - 1 : planes + 3], refs[planes + 3]
    dim = table_ref.shape[1]
    moved_refs[0][at(0)] = own_ref[...]
    for j, packet in enumerate(packet_refs, 1):
        for part in (slice(0, dim), slice(dim, 2 * dim)):
            choices = [packet[at(t), part] for t in range(PLANE)]
            for m, ref in enumerate(moved_refs):
                row = ((j - 1) * PLANE + m) * 2
                first = j - (m > 0)
                ref[at(first), part] = chosen(table_ref[row : row + 1], choices)
                early = chosen(table_ref[row + 1 : row + 2], choices)
                if m < PLANE - 1:
                    ref[at(first + planes - 1), part] = early
                else:
                    early_ref[at(first), part] = early


def usable(count, block, m):
    me, z, r = place(count)
    planes = count // PLANE
    if block == 1:
        return [me < count - 1 if m == 0 else None] + [None] * (planes - 1)
    return [(r ^ m) < r - 1] + [(z >= j) & ((z - j) * PLANE + (r ^ m) < me - 1) for j in range(1, planes)]


def attend_all(n_cols, score, v_ts, state, save):
    ahead = score(0)
    for step in range(n_cols):
        s = ahead
        if step + 1 < n_cols:
            ahead = score(step + 1)
        m = jnp.max(s, axis=0, keepdims=True)
        if state is not None:
            m_old, l_old, acc_old = state(step)
            m = jnp.maximum(m, m_old)
        w = jnp.exp2(s - m)
        l = jnp.sum(w, axis=0, keepdims=True)
        acc = jnp.dot(v_ts, w.astype(jnp.bfloat16), preferred_element_type=jnp.float32)
        if state is not None:
            old = jnp.exp2(m_old - m)
            l = l + l_old * old
            acc = acc + acc_old * old
        save(step, m, l, acc)


def fold(kv, masks, scale, width, block, rot_ref, old_refs, save):
    dim = rot_ref.shape[2]
    total = len(masks)
    steps = rot_ref.shape[1] // width
    carried = [tuple(ref[block, :, step * width : (step + 1) * width] for ref in old_refs) for step in range(steps)]
    for first in range(0, total, CHUNK):
        last = min(first + CHUNK, total)
        k = kv[first * KB : last * KB, :dim]
        v_t = kv[first * KB : last * KB, dim:].T

        def score(step, k=k, first=first, last=last):
            s = scores_of(k, rot_ref[block, step * width : (step + 1) * width, :]) * scale
            if all(ok is None for ok in masks[first:last]):
                return s
            return jnp.concatenate(
                [s[at(g - first)] if masks[g] is None else jnp.where(masks[g], s[at(g - first)], NEG) for g in range(first, last)]
            )

        def keep(step, *values):
            carried[step] = values

        attend_all(steps, score, v_t, carried.__getitem__, save if last == total else keep)


def rotate_kernel(q_ref, basis_ref, rot_ref):
    dim = basis_ref.shape[0]
    half = q_ref.shape[0] // 2
    basis = basis_ref[...]
    for block in range(2):
        for h in range(q_ref.shape[1] // dim):
            q = q_ref[block * half : (block + 1) * half, h * dim : (h + 1) * dim]
            q = jnp.dot(q, basis, preferred_element_type=jnp.float32)
            rot_ref[block, h * half : (h + 1) * half, :] = q.astype(rot_ref.dtype)


def near_kernel(scale, width, kv_ref, rot_ref, *state_refs):
    dim = rot_ref.shape[2]
    half = kv_ref.shape[0] // 2
    key_row = lax.broadcasted_iota(jnp.int32, (half, width), 0)
    query = lax.broadcasted_iota(jnp.int32, (half, width), 1) % half
    causal = key_row <= query
    for block in range(2):
        rows = slice(block * half, (block + 1) * half)
        k, v_t = kv_ref[rows, :dim], kv_ref[rows, dim:].T

        def score(step, block=block, k=k):
            s = scores_of(k, rot_ref[block, step * width : (step + 1) * width, :]) * scale
            return jnp.where(causal, s, NEG)

        def save(step, m, l, acc, block=block):
            for ref, value in zip(state_refs, (m, l, acc), strict=True):
                ref[block, :, step * width : (step + 1) * width] = value

        attend_all(rot_ref.shape[1] // width, score, v_t, None, save)


def fold_kernel(count, scale, width, stage, *refs):
    come, rot_ref, old, new = refs[:-7], refs[-7], refs[-6:-3], refs[-3:]
    me, z, _ = place(count)
    rest = (count // PLANE - 1) * KB

    def run(block, light=False, one=False):
        masks = [usable(count, block, m) for m in range(PLANE)]
        if stage == 0:
            mine_ref, next_ref, beside_ref, over_ref, passed_ref, side_ref, kv_ref = come
            half = kv_ref.shape[0] // 2
            far = slice(0, rest + KB) if block == 1 else slice(rest + KB, 2 * rest + KB)
            side = side_ref[:half]
            if block == 1:
                side = jnp.where(me == count - 1, kv_ref[:half], side)
            near = slice(0, rest) if block == 1 else slice(rest, 2 * rest)
            parts = [mine_ref[far], next_ref[near], over_ref[at(1 - block)], passed_ref[at(1 - block)]]
            masks = masks[0][1 - block :] + masks[1][1:] + masks[2][:1] + masks[3][:1]
            if block == 1:
                parts.append(beside_ref[half:])
                masks.append(None)
            if light:
                parts, masks = parts[2:], masks[2 * rest // KB :]
            if one:
                parts[:2] = [part[:KB] for part in parts[:2]]
                masks = [masks[0], masks[rest // KB]] + masks[2 * rest // KB :]
            parts.append(jnp.where(me % 2 == block, side, beside_ref[:half]))
            masks += [None] * (half // KB)
        else:
            parts, masks = [come[0][(1 - block) * rest : (2 - block) * rest]], masks[stage][1:]

        def save(step, m, l, acc):
            for ref, value in zip(new, (m, l, acc), strict=True):
                ref[block, :, step * width : (step + 1) * width] = value

        fold(jnp.concatenate(parts, axis=0), masks, scale, width, block, rot_ref, old, save)

    run(1)
    pl.when(z >= 2)(lambda: run(0))
    if stage == 0:
        pl.when(z == 1)(lambda: run(0, one=True))
        pl.when((z < 1) & (me >= 1))(lambda: run(0, True))


def put_heads(ref, first, half, step, l, acc):
    dim, width = acc.shape
    done = acc / l
    for h in range(width // half):
        head = step * (width // half) + h
        ref[first : first + half, head * dim : (head + 1) * dim] = done[:, h * half : (h + 1) * half].T.astype(ref.dtype)


def close_kernel(width, l_ref, acc_ref, first_ref):
    half = first_ref.shape[0]
    _, z, _ = place(lax.axis_size("pb"))

    @pl.when(z < 1)
    def _():
        for step in range(acc_ref.shape[2] // width):
            cols = slice(step * width, (step + 1) * width)
            put_heads(first_ref, 0, half, step, l_ref[0, :, cols], acc_ref[0, :, cols])


def last_kernel(count, scale, width, second_ref, third_ref, early_ref, first_ref, rot_ref, *refs):
    old, out_ref, done_ref, sems = refs[:3], refs[3], refs[4], refs[5]
    _, z, _ = place(count)
    half = out_ref.shape[0] // 2
    dim = rot_ref.shape[2]

    def piece(block, step, ready=None):
        rows, cols = pl.ds(block * half, half), pl.ds(step * (width // half) * dim, width // half * dim)
        source = done_ref.at[rows, cols] if ready is None else ready.at[:, cols]
        return pltpu.make_async_copy(source, out_ref.at[rows, cols], sems.at[block, step])

    def finish(block, step, l, acc):
        put_heads(done_ref, block * half, half, step, l, acc)
        piece(block, step).start()

    def add(block, one=False):
        rest = third_ref.shape[0]
        part = slice((1 - block) * rest, (2 - block) * rest)
        third = third_ref if block == 1 else early_ref
        kv = jnp.concatenate([second_ref[part], third[...]], axis=0)
        masks = usable(count, block, 2)[1:] + usable(count, block, PLANE - 1)[1:]
        if one:
            kv = jnp.concatenate([kv[:KB], kv[rest : rest + KB]], axis=0)
            masks = [masks[0], masks[rest // KB]]
        fold(kv, masks, scale, width, block, rot_ref, old, lambda step, m, l, acc: finish(block, step, l, acc))

    @pl.when(z < 1)
    def _():
        for step in range(rot_ref.shape[1] // width):
            piece(0, step, first_ref).start()

    add(1)
    pl.when(z == 1)(lambda: add(0, one=True))
    pl.when(z >= 2)(lambda: add(0))

    for block in range(2):
        for step in range(rot_ref.shape[1] // width):
            piece(block, step).wait()


def per_device(queries, keys, values, basis, picks):
    rows_dev, dim = keys.shape
    half = rows_dev // 2
    count = lax.axis_size("pb")
    planes = count // PLANE
    wide = queries.shape[1] // dim * half
    width = 2 * half
    scale = dim**-0.5 * math.log2(math.e)
    vmem = pl.BlockSpec(memory_space=pltpu.VMEM)
    params = pltpu.CompilerParams(vmem_limit_bytes=VMEM_BYTES)
    bf16, f32 = jnp.bfloat16, jnp.float32
    shapes = [
        jax.ShapeDtypeStruct((2, 1, wide), f32),
        jax.ShapeDtypeStruct((2, 1, wide), f32),
        jax.ShapeDtypeStruct((2, dim, wide), f32),
    ]

    def rows(n):
        return jax.ShapeDtypeStruct((n * KB, 2 * dim), bf16)

    def permute(value, pairs):
        return lax.ppermute(value, "pb", pairs)

    def cost(keys_each):
        return pl.CostEstimate(
            flops=8 * wide * keys_each * dim, bytes_accessed=4_000_000, transcendentals=2 * wide * keys_each
        )

    per_half = half // KB
    z_rows = (planes - 1) * PLANE
    both, by_source = lax.optimization_barrier((jnp.concatenate([keys, values]), picks.T))
    index, table = pl.pallas_call(
        functools.partial(index_kernel, count),
        out_shape=[jax.ShapeDtypeStruct((n, dim), jnp.int32) for n in (z_rows + 6, 2 * z_rows)],
        in_specs=[vmem],
        out_specs=[vmem] * 2,
        compiler_params=params,
        cost_estimate=pl.CostEstimate(flops=4_000_000_000, bytes_accessed=1_000_000, transcendentals=0),
        name="index",
    )(by_source)
    packets = pl.pallas_call(
        pack_kernel,
        out_shape=[rows(PLANE)] * (planes - 1),
        in_specs=[vmem] * 2,
        out_specs=[vmem] * (planes - 1),
        compiler_params=params,
        cost_estimate=pl.CostEstimate(flops=4_000_000_000, bytes_accessed=1_000_000, transcendentals=0),
        name="pack",
    )(index, both)
    kv, own, beside, over, side = pl.pallas_call(
        functools.partial(pack_own_kernel, z_rows),
        out_shape=[rows(2 * per_half), rows(1), rows(per_half + 1), rows(4 + 0), rows(per_half + 0)],
        in_specs=[vmem] * 2,
        out_specs=[vmem] * 5,
        compiler_params=params,
        name="pack_own",
    )(index, both)

    packets = [
        permute(packet, [(s, (s + j * PLANE) % count) for s in range(count)]) for j, packet in enumerate(packets, 1)
    ]

    rotated = pl.pallas_call(
        rotate_kernel,
        out_shape=jax.ShapeDtypeStruct((2, wide, dim), bf16),
        in_specs=[vmem] * 2,
        out_specs=vmem,
        compiler_params=params,
        cost_estimate=pl.CostEstimate(flops=4 * wide * dim * dim, bytes_accessed=2_000_000, transcendentals=0),
        name="rotate",
    )(queries, basis)
    packets, rotated = lax.optimization_barrier((packets, rotated))
    over = permute(over, [(s, s ^ 2) for s in range(count)])
    groups = lax.axis_size("grp")
    pairs = []
    for g in range(groups):
        pairs += [(g * count + s, g * count + s + (1 if s % 2 else -1)) for s in range(1, count - 1)]
        pairs += [(g * count + s, (g + 1) % groups * count + s) for s in (0, count - 1)]
    side = lax.ppermute(side, ("grp", "pb"), pairs)

    def swap(value, m):
        return permute(value, [(s, s ^ m) for s in range(count)])

    sizes = [2 * planes - 1, 2 * planes - 2, 2 * planes - 2, planes - 1, planes - 1]
    moved = list(
        pl.pallas_call(
            functools.partial(select_kernel, count),
            out_shape=[rows(size) for size in sizes],
            in_specs=[vmem] * (planes + 1),
            out_specs=[vmem] * len(sizes),
            compiler_params=params,
            name="select",
        )(table, own, *packets)
    )
    for m in (1, 2, 3):
        moved[m] = swap(moved[m], m)
    early = permute(moved[PLANE], [(s, s ^ (PLANE - 1 if s >= PLANE else 1)) for s in range(count)])
    beside, passed = swap(beside, 1), swap(over[2 * KB : 4 * KB], 1)

    state = pl.pallas_call(
        functools.partial(near_kernel, scale, width),
        out_shape=shapes,
        in_specs=[vmem] * 2,
        out_specs=[vmem] * 3,
        compiler_params=params,
        cost_estimate=cost(half),
        name="near",
    )(kv, rotated)

    def folded(state, stage, messages):
        return pl.pallas_call(
            functools.partial(fold_kernel, count, scale, width, stage),
            out_shape=shapes,
            in_specs=[vmem] * (4 + len(messages)),
            out_specs=[vmem] * 3,
            input_output_aliases={1 + len(messages) + i: i for i in range(3)},
            compiler_params=params,
            cost_estimate=cost(half),
            name=f"fold{stage}",
        )(*messages, rotated, *state)

    state = folded(state, 0, [moved[0], moved[1], beside, over, passed, side, kv])
    first = pl.pallas_call(
        functools.partial(close_kernel, width),
        out_shape=jax.ShapeDtypeStruct((half, queries.shape[1]), bf16),
        in_specs=[vmem] * 2,
        out_specs=vmem,
        compiler_params=params,
        name="close",
    )(*state[1:])
    return pl.pallas_call(
        functools.partial(last_kernel, count, scale, width),
        out_shape=jax.ShapeDtypeStruct(queries.shape, bf16),
        in_specs=[vmem] * 8,
        out_specs=pl.BlockSpec(memory_space=pl.ANY),
        scratch_shapes=[pltpu.VMEM(queries.shape, bf16), pltpu.SemaphoreType.DMA((2, wide // width))],
        compiler_params=params,
        cost_estimate=cost(half),
        name="last",
    )(moved[2], moved[3], early, first, rotated, *state)


def solution(mesh):
    in_specs = (P("pb", "grp"), P("pb", "grp"), P("pb", "grp"), P("grp", None), P("grp", None))
    out_specs = P("pb", "grp")
    return jax.shard_map(
        per_device, mesh=mesh, in_specs=in_specs, out_specs=out_specs, check_vma=False
    )
```
